128 devices in a mesh: ha: 4 (over x), wa: 16 (over z, y), ba: 2 (over core).
Axes of the slice: x: 4, y: 4, z: 4, core: 2. Of those that a mesh axis runs over, the one named last changes fastest.
Arguments:
- frames: bfloat16 [2, 4, 128, 79872], P('ba', None, 'ha', 'wa'), may hold values from -6 to 6
- cache: bfloat16 [2, 2, 128, 79872], P('ba', None, 'ha', 'wa'), may hold values from -6 to 6
- norm_gain: float32 [96], replicated, may hold values from 0.5 to 2
- conv_weight: bfloat16 [27, 9216], replicated, may hold values from -0.125 to 0.125
- conv_bias: float32 [96], replicated, may hold values from -3 to 3
- down_weight: bfloat16 [9, 9216], replicated, may hold values from -0.21875 to 0.21875
- down_bias: float32 [96], replicated, may hold values from -3 to 3
- latent_weight: bfloat16 [96, 16], replicated, may hold values from -0.625 to 0.625
- latent_bias: float32 [16], replicated, may hold values from -3 to 3
- valid_frames: int32 [2], P('ba'), may hold values from 1 to 4, as said below
- owners: int32 [2, 4, 16, 64, 1], P('ba', 'ha', 'wa'), may hold values from 0 to 3; in each aligned block of 64 rows (0 to 63, 64 to 127, ..., all dimensions but the last counted through in order) at most 32 rows name the same one
Outputs:
- routed: bfloat16 [2, 4, 16, 128, 416], P('ba', 'ha', 'wa')
The draws below stay inside these ranges and needn't reach their ends.
Inputs may be any that keep to these rules, and one draw needn't show every extreme that they name: `valid_frames`: some clip has all 4 frames valid. `owners`: among the 64 rows of one tile, no owner is named more than 32 times.
All inputs are finite; a program needn't handle non-finite values.
Results may differ from the reference program's by a relative error of at most 0.0058.
Values may be sent and summed in bfloat16 or wider, within the bound.
A program may use at most 128 MiB of HBM per device.

```python
import math
import jax
import jax.numpy as jnp
import numpy as np
from jax import lax

C = 96
Z = 16
FRAMES = 4
TH = 32
TW = 52
B = 2
H = 128
W = 832
ROWS_DEV = 64
CAP = 32
LROW = 416
N_HA = 4
N_WA = 16


def draw_valid_frames(key, part):
    key = jax.random.fold_in(key, 7)
    first_key, second_key = jax.random.split(key)
    counts = jax.random.randint(first_key, (B,), 1, FRAMES + 1)
    chosen = jax.random.randint(second_key, (), 0, B)
    return jnp.where(jnp.arange(B) == chosen, FRAMES, counts).astype(jnp.int32)


def level_of(stream_key, extent, cuts, smallest, largest):
    loudness, own = 1.0, jax.random.fold_in(stream_key, 6)
    for position, shards_of in cuts:
        draws = jnp.exp(jax.random.uniform(jax.random.fold_in(own, position), (shards_of,), jnp.float32, smallest / len(cuts), largest / len(cuts)))
        loudness = loudness * jnp.repeat(draws, extent[position] // shards_of).reshape([-1 if axis == position else 1 for axis in range(len(extent))])
    return loudness


def routed_block(own_key, own, number, rows, count, top, limit, slope):
    sequence = jax.random.permutation(own_key, count)
    packed, ordinary = shares(count, rows * top, limit, slope, True), shares(count, rows * top, limit, slope, False)
    places = jnp.arange(count)

    def named(lengths, offset_by):
        used = int((lengths > 0).sum())
        fixed = max(1, used // 4)
        moved = fixed + (places - fixed + offset_by * (used - fixed)) % max(1, count - fixed)
        return jnp.zeros((count,), jnp.int32).at[sequence[jnp.where(places < fixed, places, moved)]].set(jnp.asarray(lengths, jnp.int32))

    lengths = jnp.where(number % 4 == 0, named(packed, number // 4), named(ordinary, number - number // 4 - 1))
    mixed = jax.random.permutation(jax.random.fold_in(own, 3), count)
    donor, sink = mixed[0:count // 2 * 2:2], mixed[1:count // 2 * 2:2]
    room = jnp.minimum(lengths[donor] - 1, limit - lengths[sink]) // 2
    room = jnp.where((donor == sequence[0]) | (sink == sequence[0]) | (lengths[sink] == 0), 0, jnp.maximum(room, 0))
    moved = jax.random.randint(jax.random.fold_in(own, 4), (count // 2,), 0, 1 << 20) % (room + 1)
    lengths = lengths.at[donor].add(-moved).at[sink].add(moved)
    labels = jnp.searchsorted(jnp.cumsum(lengths), jnp.arange(rows * top), side="right").astype(jnp.int32)
    listing = labels.reshape(top, rows).T
    listing = listing[jax.random.permutation(jax.random.fold_in(own, 1), rows)]
    offset_by = jax.random.randint(jax.random.fold_in(own, 2), (rows, 1), 0, top)
    return jnp.take_along_axis(listing, (jnp.arange(top)[None, :] + offset_by) % top, axis=1)


def shares(number_of, total, most, slope, full):
    loads = [(1 << 20) // math.isqrt(grade ** slope) + 1 for grade in range(1, number_of + 1)]
    largest = most if full else min(most, max(-(-total // number_of), total * loads[0] // sum(loads)))
    least = 1 if total - largest >= number_of - 1 else 0
    given, surplus = [largest] + [least] * (number_of - 1), total - largest - least * (number_of - 1)
    while surplus > 0:
        free = [i for i in range(1, number_of) if given[i] < largest] or [i for i in range(1, number_of) if given[i] < most]
        mass, remaining = sum([loads[i] for i in free]), surplus
        for i in free:
            addition = min(most - given[i], max(1, remaining * loads[i] // mass), surplus)
            given[i] = given[i] + addition
            surplus = surplus - addition
    return np.array(given)


def bell_draw(stream_key, dims, deviation, limit, cuts=(), kind=jnp.bfloat16):
    result = deviation * jax.random.normal(stream_key, dims, jnp.float32)
    if cuts:
        result = result * level_of(stream_key, dims, cuts, -0.22, 0.18)
    return jnp.clip(result, -limit, limit).astype(kind)


def setup_inputs(seed: int = 0) -> dict:
    arg_keys = jax.random.split(jax.random.key(seed), 12)
    frames = bell_draw(arg_keys[0], (B, FRAMES, H, W * C), 1.0, 6.0, ((0, 2), (2, 4), (3, 16)))
    cache = bell_draw(arg_keys[1], (B, 2, H, W * C), 1.0, 6.0, ((0, 2), (2, 4), (3, 16)))
    norm_gain = jnp.clip(jnp.exp(jax.random.uniform(arg_keys[2], (C,), jnp.float32, math.log(0.5), math.log(2.0))), 0.5, 2.0)
    conv_weight = bell_draw(arg_keys[3], (27, C * C), (27 * C) ** -0.5, 0.125)
    conv_bias = bell_draw(arg_keys[4], (C,), 0.5, 3.0, (), jnp.float32)
    down_weight = bell_draw(arg_keys[5], (9, C * C), (9 * C) ** -0.5, 0.21875)
    down_bias = bell_draw(arg_keys[6], (C,), 0.5, 3.0, (), jnp.float32)
    latent_weight = bell_draw(arg_keys[7], (C, Z), C ** -0.5, 0.625)
    latent_bias = bell_draw(arg_keys[8], (Z,), 0.5, 3.0, (), jnp.float32)
    valid_frames = draw_valid_frames(jax.random.fold_in(arg_keys[11], 71), 0)
    owners_keys = jax.random.split(jax.random.fold_in(arg_keys[10], 1), B * N_HA * N_WA * ROWS_DEV // ROWS_DEV)
    owners_turns = jax.random.permutation(jax.random.fold_in(arg_keys[10], 3), B * N_HA * N_WA * ROWS_DEV // ROWS_DEV)
    owners = jax.vmap(lambda own, number: routed_block(jax.random.fold_in(arg_keys[10], 2), own, number, ROWS_DEV, N_HA, 1, CAP, 2))(owners_keys, owners_turns).reshape((B, N_HA, N_WA, ROWS_DEV, 1))
    return {"frames": frames, "cache": cache, "norm_gain": norm_gain, "conv_weight": conv_weight, "conv_bias": conv_bias, "down_weight": down_weight, "down_bias": down_bias, "latent_weight": latent_weight, "latent_bias": latent_bias, "valid_frames": valid_frames, "owners": owners}


EPS = 1e-06
SHAPES = ('NDHWC', 'DHWIO', 'NDHWC')

def per_clip(inputs):
    frames, cache, valid, norm_gain, conv_weight, conv_bias, down_weight, down_bias, latent_weight, latent_bias = inputs
    as_float = frames.astype(jnp.float32).reshape(FRAMES, H, W, C)
    mean_square = lax.optimization_barrier(jnp.mean(as_float * as_float, axis=-1, keepdims=True))
    normed = as_float * lax.rsqrt(mean_square + EPS) * norm_gain
    activated = jax.nn.silu(normed).astype(jnp.bfloat16)
    stacked = jnp.concatenate([cache.reshape(2, H, W, C), activated], axis=0)
    kernel = conv_weight.astype(jnp.float32).reshape(3, 3, 3, C, C)
    convolved = lax.conv_general_dilated(stacked[None].astype(jnp.float32), kernel, (1, 1, 1), [(0, 0), (1, 1), (1, 1)], dimension_numbers=SHAPES, precision=lax.Precision.HIGHEST)[0]
    hidden = (as_float + convolved + conv_bias).astype(jnp.bfloat16)
    padded = jnp.pad(hidden, ((0, 0), (0, 1), (0, 1), (0, 0)))
    down_kernel = down_weight.astype(jnp.float32).reshape(1, 3, 3, C, C)
    reduced = lax.conv_general_dilated(padded[None].astype(jnp.float32), down_kernel, (1, 2, 2), 'VALID', dimension_numbers=SHAPES, precision=lax.Precision.HIGHEST)[0]
    reduced = (reduced + down_bias).astype(jnp.bfloat16)
    latent = jnp.einsum('fhwc,cz->fhwz', reduced.astype(jnp.float32), latent_weight.astype(jnp.float32), precision=lax.Precision.HIGHEST)
    latent = latent + latent_bias
    present = jnp.arange(FRAMES) < valid
    latent = jnp.where(present[:, None, None, None], latent, 0.0)
    return latent.astype(jnp.bfloat16)

def reference(frames, cache, norm_gain, conv_weight, conv_bias, down_weight, down_bias, latent_weight, latent_bias, valid_frames, owners):

    def one_clip(pair):
        return per_clip((pair[0], pair[1], pair[2], norm_gain, conv_weight, conv_bias, down_weight, down_bias, latent_weight, latent_bias))
    latent = lax.map(one_clip, (frames, cache, valid_frames))
    half_rows = TH // 2
    half_cols = TW // 2
    tiles = latent.reshape(B, FRAMES, N_HA, half_rows, N_WA, half_cols * Z)
    tiles = jnp.transpose(tiles, (0, 2, 4, 1, 3, 5)).reshape(B, N_HA, N_WA, ROWS_DEV, LROW)
    owner_ids = owners[..., 0]
    one_hot = (owner_ids[..., None] == jnp.arange(N_HA, dtype=jnp.int32)).astype(jnp.int32)
    ranking = jnp.cumsum(one_hot, axis=3) - 1
    slot_index = lax.optimization_barrier(jnp.sum(one_hot * ranking, axis=-1))
    target = owner_ids * CAP + slot_index
    selector = (target[..., None, :] == jnp.arange(N_HA * CAP, dtype=jnp.int32)[:, None]).astype(jnp.float32)
    outgoing = jnp.einsum('bijsr,bijrl->bijsl', selector, tiles.astype(jnp.float32), precision=lax.Precision.HIGHEST)
    outgoing = outgoing.reshape(B, N_HA, N_WA, N_HA, CAP, LROW)
    routed = jnp.transpose(outgoing, (0, 3, 2, 1, 4, 5)).reshape(B, N_HA, N_WA, N_HA * CAP, LROW)
    return routed.astype(jnp.bfloat16)
```

```python
import functools

import jax
import jax.numpy as jnp
import numpy as np
from jax import lax
from jax.experimental import pallas as pl
from jax.experimental.pallas import tpu as pltpu
from jax.sharding import PartitionSpec as P

EPS = 1e-06
C = 96
Z = 16
T = 4
TH = 32
TW = 52
OWN = 39
EXT = 42
FS = 48
KK = 27
QB = 8
KD = 1664
F32 = jnp.float32
BF16 = jnp.bfloat16


def lanes(tile, count=1):
    return pl.ds(pl.multiple_of(tile * 128, 128), count * 128)


def kernel(
    n_ha,
    n_wa,
    frames,
    cache,
    owners,
    valid,
    wa_w,
    wb_w,
    wd02,
    wd1,
    gain,
    cbias,
    lbias,
    out,
    ext,
    pack_top,
    pack_bot,
    above,
    below,
    act,
    xf,
    planes,
    ones,
    hp,
    hb,
    l32,
    x32,
    hp32,
    h32,
    vs,
    send,
    local_sem,
    send_sem,
    recv_sem,
    a2a_send,
    a2a_recv,
    self_sem,
):
    ha, wa = lax.axis_index("ha"), lax.axis_index("wa")
    up, down = lax.rem(ha + n_ha - 1, n_ha), lax.rem(ha + 1, n_ha)
    left, right = lax.rem(wa + n_wa - 1, n_wa), lax.rem(wa + 1, n_wa)

    load_cache = pltpu.make_async_copy(
        cache.at[0], ext.at[pl.ds(0, 2), :, pl.ds(0, OWN * 128)], local_sem.at[0]
    )
    load_frames = pltpu.make_async_copy(
        frames.at[0], ext.at[pl.ds(2, T), :, pl.ds(0, OWN * 128)], local_sem.at[1]
    )
    load_cache.start()
    load_frames.start()

    barrier = pltpu.get_barrier_semaphore()
    greeted = [
        {"ha": up, "wa": wa},
        {"ha": down, "wa": wa},
        {"ha": ha, "wa": left},
        {"ha": ha, "wa": right},
        {"ha": up, "wa": left},
        {"ha": up, "wa": right},
        {"ha": down, "wa": left},
        {"ha": down, "wa": right},
        {"ha": lax.rem(ha + 2, n_ha), "wa": wa},
    ]
    for device in greeted:
        pl.semaphore_signal(
            barrier, inc=1, device_id=device, device_id_type=pl.DeviceIdType.MESH
        )

    def remote(src, dst, index, device):
        return pltpu.make_async_remote_copy(
            src_ref=src,
            dst_ref=dst,
            send_sem=send_sem.at[index],
            recv_sem=recv_sem.at[index],
            device_id=device,
            device_id_type=pl.DeviceIdType.MESH,
        )

    load_cache.wait()
    load_frames.wait()

    sub = lax.broadcasted_iota(jnp.int32, (8, 384), 0)

    @pl.loop(0, OWN // 3)
    def _(g):
        win = lanes(3 * g, 3)
        tops = [ext[f, pl.ds(0, 16), win].astype(F32) for f in range(6)]
        bots = [ext[f, pl.ds(16, 16), win].astype(F32) for f in range(6)]
        lo = jnp.zeros((8, 384), F32)
        hi = jnp.zeros((8, 384), F32)
        for t in range(T):
            lo = jnp.where(sub == t, tops[2 + t][0:1], lo)
            lo = jnp.where(sub == 4 + t, tops[2 + t][1:2], lo)
        for t in range(2):
            hi = jnp.where(sub == t, tops[t][0:1], hi)
            hi = jnp.where(sub == 2 + t, tops[t][1:2], hi)
        pack_top[:, win] = jnp.concatenate([lo, hi], axis=0).astype(BF16)
        lo = jnp.zeros((8, 384), F32)
        for t in range(T):
            lo = jnp.where(sub == t, bots[2 + t][15:16], lo)
        for t in range(2):
            lo = jnp.where(sub == 4 + t, bots[t][15:16], lo)
        pack_bot[:, win] = jnp.concatenate([lo, jnp.zeros((8, 384), F32)], axis=0).astype(BF16)

    pl.semaphore_wait(barrier, len(greeted))

    own = pl.ds(0, OWN * 128)
    first, last = pl.ds(0, 256), pl.ds((OWN - 1) * 128, 128)
    from_right, from_left = pl.ds(OWN * 128, 256), pl.ds((OWN + 2) * 128, 128)
    row_copies = [
        remote(pack_top, below.at[:, own], 0, {"ha": up, "wa": wa}),
        remote(pack_bot, above.at[:, own], 1, {"ha": down, "wa": wa}),
        remote(pack_top.at[:, first], below.at[:, from_right], 2, {"ha": up, "wa": left}),
        remote(pack_top.at[:, last], below.at[:, from_left], 3, {"ha": up, "wa": right}),
        remote(pack_bot.at[:, first], above.at[:, from_right], 4, {"ha": down, "wa": left}),
        remote(pack_bot.at[:, last], above.at[:, from_left], 5, {"ha": down, "wa": right}),
    ]
    col_copies = [
        remote(
            frames.at[0, :, :, first],
            ext.at[pl.ds(2, T), :, from_right],
            6,
            {"ha": ha, "wa": left},
        ),
        remote(
            cache.at[0, :, :, first],
            ext.at[pl.ds(0, 2), :, from_right],
            7,
            {"ha": ha, "wa": left},
        ),
        remote(
            frames.at[0, :, :, last],
            ext.at[pl.ds(2, T), :, from_left],
            8,
            {"ha": ha, "wa": right},
        ),
        remote(
            cache.at[0, :, :, last],
            ext.at[pl.ds(0, 2), :, from_left],
            9,
            {"ha": ha, "wa": right},
        ),
    ]
    for copy in row_copies + col_copies:
        copy.start()

    def column_of(axis):
        index = lax.broadcasted_iota(jnp.int32, (384, 384), axis)
        return sum((index >= edge).astype(jnp.int32) for edge in (96, 192, 288))

    ones[...] = jnp.where(column_of(0) == column_of(1), 1.0, 0.0).astype(BF16)

    has_left = jnp.where(wa == 0, 0.0, 1.0).astype(F32)
    has_right = jnp.where(wa == n_wa - 1, 0.0, 1.0).astype(F32)
    has_above = jnp.where(ha == 0, 0.0, 1.0).astype(F32)
    has_below = jnp.where(ha == n_ha - 1, 0.0, 1.0).astype(F32)
    lane = lax.broadcasted_iota(jnp.int32, (1, 128), 1)

    def activate(x):
        squares = jnp.dot((x * x).astype(BF16), ones[...], preferred_element_type=F32)
        v = x * lax.rsqrt(squares * (1.0 / C) + EPS) * gain[...]
        return v / (1.0 + jnp.exp(-v))

    def halo_mask(x):
        return jnp.concatenate([x[:, :256] * has_right, x[:, 256:] * has_left], axis=1)

    def split_rows(tile, even, odd, even_at, odd_at):
        for f in range(6):
            rows = pl.ds(f * 16, 16)
            planes[even, tile + 1, rows] = act[tile, pl.ds(f * FS + even_at, 16, 2)].astype(BF16)
            planes[odd, tile + 1, rows] = act[tile, pl.ds(f * FS + odd_at, 16, 2)].astype(BF16)

    def group(g, edge):
        win = lanes(3 * g, 3)
        x = ext[pl.ds(2, T), :, win].reshape(T * TH, 384).astype(F32)
        earlier = ext[pl.ds(0, 2), :, win].reshape(2 * TH, 384).astype(F32)
        if edge:
            x, earlier = halo_mask(x), halo_mask(earlier)
        activated = activate(x)
        for j in range(3):
            cut = slice(128 * j, 128 * (j + 1))
            for f in range(6):
                source = earlier if f < 2 else activated
                at = (f if f < 2 else f - 2) * TH
                act[3 * g + j, pl.ds(f * FS + 8, TH)] = source[at : at + TH, cut]
            split_rows(3 * g + j, 1, 2, 8, 9)
        before = ext[pl.ds(2, T), :, lanes(jnp.maximum(3 * g - 1, 0))]
        before = pltpu.roll(before.reshape(T * TH, 128).astype(F32), 32, 1)
        for j in range(1 if edge else 3):
            here = pltpu.roll(x[:, 128 * j : 128 * (j + 1)], 32, 1)
            xf[3 * g + j + 1] = jnp.where(lane < 32, before, here)
            before = here

    @pl.loop(0, OWN // 3)
    def _(g):
        group(g, False)

    for copy in col_copies:
        copy.wait_recv()
    group(OWN // 3, True)
    for copy in row_copies:
        copy.wait_recv()

    def halo_group(g, edge):
        win = lanes(3 * g, 3)
        hi = below[:, win].astype(F32) * has_below
        lo = above[:, win].astype(F32) * has_above
        if edge:
            hi, lo = halo_mask(hi), halo_mask(lo)
        activated = activate(jnp.concatenate([hi[:8], lo[:8]], axis=0))
        for j in range(3):
            cut = slice(128 * j, 128 * (j + 1))
            tile = 3 * g + j
            act[tile, pl.ds(2 * FS + 40, T, FS)] = activated[0:4, cut]
            act[tile, pl.ds(2 * FS + 41, T, FS)] = activated[4:8, cut]
            act[tile, pl.ds(2 * FS + 7, T, FS)] = activated[8:12, cut]
            act[tile, pl.ds(40, 2, FS)] = hi[8:10, cut]
            act[tile, pl.ds(41, 2, FS)] = hi[10:12, cut]
            act[tile, pl.ds(7, 2, FS)] = lo[4:6, cut]
            split_rows(tile, 3, 0, 10, 7)
        before = below[:, lanes(jnp.maximum(3 * g - 1, 0))].astype(F32) * has_below
        before = pltpu.roll(before[:8], 32, 1)
        for j in range(1 if edge else 3):
            here = pltpu.roll(hi[:8, 128 * j : 128 * (j + 1)], 32, 1)
            x32[3 * g + j + 1] = jnp.where(lane < 32, before, here)
            before = here

    @pl.loop(0, OWN // 3)
    def _(g):
        halo_group(g, False)

    halo_group(OWN // 3, True)

    @pl.loop(0, 4)
    def _(plane):
        planes[plane, 0] = planes[plane, EXT]

        @pl.loop(0, 14)
        def _(i):
            later = planes[plane, 3 * i + 2].astype(F32)
            sooner = planes[plane, jnp.where(i == 0, 41, 3 * i - 1)].astype(F32)
            planes[plane, EXT + 1 + i] = jnp.where(lane < 64, later, sooner).astype(BF16)

    @pl.loop(0, 14)
    def _(i):
        for a in range(3):
            for r in range(3):
                rows = pl.ds(a * FS + 39 + r, T, FS)
                kk = (3 * a + r) * 3
                here = pl.ds(0, T)
                for j in range(3):
                    l32[0, i, kk + j, here] = act[3 * i + j, rows]
                later = act[3 * i + 1, rows]
                sooner = act[jnp.where(i == 0, 40, 3 * i - 2), rows]
                l32[1, i, kk, here] = jnp.where(lane < 64, later, sooner)
                l32[1, i, kk + 1, here] = act[jnp.where(i == 0, 41, 3 * i - 1), rows]
                l32[1, i, kk + 2, here] = act[3 * i, rows]

    def tile_a(k, j):
        return 3 * k + j + 1

    def tile_b(i, j):
        return EXT + 1 + i if j == 0 else 3 * i + j - 1

    def conv(parity, base, count, tile_of, weights):
        rows = []
        for w in range(count):
            pieces = []
            for a in range(3):
                for r in range(3):
                    for j in range(3):
                        pieces.append(
                            planes[r + parity, tile_of(base + w, j), pl.ds(a * 16, 64)]
                        )
            rows.append(jnp.concatenate(pieces, axis=1))
        return jnp.dot(
            jnp.concatenate(rows, axis=0), weights[...], preferred_element_type=F32
        )

    @pl.loop(0, 4)
    def _(step):
        parity, base = step // 2, (step % 2) * 6
        acc = conv(parity, base, 7, tile_a, wa_w)
        for w in range(7):
            k = base + w
            part = acc[64 * w : 64 * (w + 1)]
            x = xf[3 * k + 2, pl.ds(parity, 64, 2)]
            hb[parity, 3 * k + 2] = (x + part[:, :128] + cbias[1]).astype(BF16)
            hp[parity, k + 1] = part[:, 128:]

    cut_right = jnp.where((lane >= 32) & (wa == n_wa - 1), 0.0, 1.0).astype(F32)

    @pl.loop(0, 4)
    def _(step):
        parity, base = step // 2, (step % 2) * 7
        acc = conv(parity, base, 7, tile_b, wb_w)
        for w in range(7):
            i = base + w
            part = acc[64 * w : 64 * (w + 1)]
            x = xf[3 * i, pl.ds(parity, 64, 2)]
            hb[parity, 3 * i] = (x + part[:, :128] + hp[parity, i] + cbias[2]).astype(BF16)
            x = xf[3 * i + 1, pl.ds(parity, 64, 2)]
            h = x + part[:, 128:] + cbias[0]
            h = h * jnp.where(i == 13, cut_right, 1.0)
            hb[parity, 3 * i + 1] = h.astype(BF16)

    def conv32(side, weights):
        rows = []
        for w in range(14):
            rows.append(jnp.concatenate([l32[side, w, kk] for kk in range(KK)], axis=1))
        lhs = jnp.concatenate(rows, axis=0).astype(BF16)
        return jnp.dot(lhs, weights[...], preferred_element_type=F32)

    def put32(index, value):
        h32[index] = jnp.concatenate([value * has_below, jnp.zeros((8, 128), F32)], axis=0).astype(
            BF16
        )

    acc = conv32(0, wa_w)
    for k in range(13):
        part = acc[8 * k : 8 * (k + 1)]
        put32(3 * k + 2, x32[3 * k + 2] + part[:, :128] + cbias[1])
        hp32[k + 1] = part[:, 128:]
    acc = conv32(1, wb_w)
    for i in range(14):
        part = acc[8 * i : 8 * (i + 1)]
        if i:
            put32(3 * i, x32[3 * i] + part[:, :128] + hp32[i] + cbias[2])
        h = x32[3 * i + 1] + part[:, 128:] + cbias[0]
        put32(3 * i + 1, h * cut_right if i == 13 else h)

    def block(b, count):
        even = jnp.concatenate([hb[0, 12 * b + j + 1] for j in range(count)], axis=1)
        odd = jnp.concatenate([hb[1, 12 * b + j + 1] for j in range(count)], axis=1)
        extra = jnp.concatenate([h32[12 * b + j + 1] for j in range(count)], axis=1)
        return even, extra, odd

    blocks = [block(b, 13) for b in range(3)]
    uv = jnp.dot(
        jnp.concatenate([piece for b in blocks for piece in b[:2]], axis=0),
        wd02[...],
        preferred_element_type=F32,
    )
    u1 = jnp.dot(
        jnp.concatenate([b[2] for b in blocks], axis=0), wd1[...], preferred_element_type=F32
    )
    even, extra, odd = block(3, 4)
    uv_last = jnp.dot(
        jnp.concatenate([even, extra], axis=0), wd02[pl.ds(0, 512)], preferred_element_type=F32
    )
    u1_last = jnp.dot(odd, wd1[pl.ds(0, 512)], preferred_element_type=F32)

    latents = []
    for b in range(4):
        both = uv[80 * b : 80 * (b + 1)] if b < 3 else uv_last
        mid = u1[64 * b : 64 * (b + 1)] if b < 3 else u1_last
        for t in range(T):
            vs[t, pl.ds(0, 16)] = both[16 * t : 16 * (t + 1), 128:]
            vs[t, pl.ds(16, 1)] = both[64 + t : 65 + t, 128:]
        shifted = jnp.concatenate([vs[t, pl.ds(1, 16)] for t in range(T)], axis=0)
        latents.append(both[:64, :128] + mid + shifted)
    latent = jnp.concatenate(latents[:3] + [latents[3][:, :32]], axis=1) + lbias[...]
    frame_of = lax.broadcasted_iota(jnp.int32, (64, 1), 0)
    latent = jnp.where(frame_of < valid[0] * 16, latent, 0.0).astype(BF16)

    row = lax.broadcasted_iota(jnp.int32, (64, 64), 0)
    col = lax.broadcasted_iota(jnp.int32, (64, 64), 1)
    by_row = jnp.broadcast_to(owners[...], (64, 64))
    by_col = jnp.sum(jnp.where(row == col, by_row, 0), axis=0, keepdims=True)
    rank = jnp.sum(jnp.where((by_row == by_col) & (row < col), 1, 0), axis=0, keepdims=True)
    slot = by_col * 32 + rank
    slots = lax.broadcasted_iota(jnp.int32, (128, 64), 0)
    selector = jnp.where(slots == slot, 1.0, 0.0).astype(BF16)
    send[...] = jnp.dot(selector, latent, preferred_element_type=F32).astype(BF16)

    here = pl.ds(pl.multiple_of(ha * 32, 32), 32)
    keep = pltpu.make_async_copy(send.at[here], out.at[0, 0, 0, here], self_sem)
    copies = []
    for d in range(1, n_ha):
        target = lax.rem(ha + d, n_ha)
        copies.append(
            pltpu.make_async_remote_copy(
                src_ref=send.at[pl.ds(pl.multiple_of(target * 32, 32), 32)],
                dst_ref=out.at[0, 0, 0, here],
                send_sem=a2a_send.at[d - 1],
                recv_sem=a2a_recv.at[d - 1],
                device_id={"ha": target, "wa": wa},
                device_id_type=pl.DeviceIdType.MESH,
            )
        )
    for copy in copies:
        copy.start()
    keep.start()
    for copy in row_copies + col_copies:
        copy.wait_send()
    for copy in copies:
        copy.wait()
    keep.wait()


def conv_matrices(conv_weight):
    w = conv_weight.reshape(9, 3, C, C)
    zero = jnp.zeros((9, C, C), conv_weight.dtype)
    taps = [zero] + [w[:, s] for s in range(3)] + [zero]
    rows = [jnp.concatenate([taps[s + 1], taps[s]], axis=2) for s in range(4)]
    window = jnp.concatenate(rows, axis=1)
    first = jnp.pad(window, ((0, 0), (0, 0), (0, 64)))
    second = jnp.pad(jnp.roll(window, 64, axis=1), ((0, 0), (0, 0), (64, 0)))
    return first.reshape(KK * 128, 256), second.reshape(KK * 128, 256)


def down_matrices(down_weight, latent_weight):
    dw = down_weight.reshape(9, C, C)
    fused = jnp.einsum("kio,oz->kiz", dw, latent_weight, preferred_element_type=F32)
    fused = fused.astype(BF16).reshape(3, 3, C, Z)
    place = np.zeros((3, 2 * QB + 1, QB), np.float32)
    for s in range(3):
        for q in range(QB):
            place[s, 2 * q + s, q] = 1.0
    banded = jnp.einsum(
        "scq,rsiz->rciqz", jnp.asarray(place, BF16), fused, preferred_element_type=F32
    ).astype(BF16)
    banded = banded.reshape(3, (2 * QB + 1) * C, QB * Z)
    banded = jnp.pad(banded, ((0, 0), (KD - (2 * QB + 1) * C, 0), (0, 0)))
    return jnp.concatenate([banded[0], banded[2]], axis=1), banded[1]


def per_device(
    n_ha,
    n_wa,
    frames,
    cache,
    norm_gain,
    conv_weight,
    conv_bias,
    down_weight,
    down_bias,
    latent_weight,
    latent_bias,
    valid_frames,
    owners,
):
    wa_w, wb_w = conv_matrices(conv_weight)
    wd02, wd1 = down_matrices(down_weight, latent_weight)
    gain = jnp.tile(norm_gain, 4).reshape(1, 384)
    cbias = jnp.roll(jnp.tile(conv_bias, 4), 32).reshape(3, 1, 128)
    lbias = latent_bias + jnp.sum(down_bias[:, None] * latent_weight.astype(F32), axis=0)
    lbias = jnp.tile(lbias, TW // 2).reshape(1, TW // 2 * Z)
    vmem = pl.BlockSpec(memory_space=pltpu.VMEM)
    anyspace = pl.BlockSpec(memory_space=pl.ANY)
    return pl.pallas_call(
        functools.partial(kernel, n_ha, n_wa),
        out_shape=jax.ShapeDtypeStruct((1, 1, 1, 128, 416), BF16),
        in_specs=[anyspace, anyspace, vmem, pl.BlockSpec(memory_space=pltpu.SMEM)] + [vmem] * 7,
        out_specs=anyspace,
        scratch_shapes=[
            pltpu.VMEM((6, TH, EXT * 128), BF16),
            pltpu.VMEM((16, OWN * 128), BF16),
            pltpu.VMEM((16, OWN * 128), BF16),
            pltpu.VMEM((16, EXT * 128), BF16),
            pltpu.VMEM((16, EXT * 128), BF16),
            pltpu.VMEM((EXT, 6 * FS, 128), F32),
            pltpu.VMEM((41, T * TH, 128), F32),
            pltpu.VMEM((4, EXT + 15, 96, 128), BF16),
            pltpu.VMEM((384, 384), BF16),
            pltpu.VMEM((2, 14, 64, 128), F32),
            pltpu.VMEM((2, 41, 64, 128), BF16),
            pltpu.VMEM((2, 14, KK, 8, 128), F32),
            pltpu.VMEM((41, 8, 128), F32),
            pltpu.VMEM((14, 8, 128), F32),
            pltpu.VMEM((41, 16, 128), BF16),
            pltpu.VMEM((T, 24, 128), F32),
            pltpu.VMEM((128, 416), BF16),
            pltpu.SemaphoreType.DMA((2,)),
            pltpu.SemaphoreType.DMA((10,)),
            pltpu.SemaphoreType.DMA((10,)),
            pltpu.SemaphoreType.DMA((n_ha - 1,)),
            pltpu.SemaphoreType.DMA((n_ha - 1,)),
            pltpu.SemaphoreType.DMA,
        ],
        compiler_params=pltpu.CompilerParams(
            collective_id=0, has_side_effects=True, vmem_limit_bytes=56 * 2**20
        ),
        name="encoder_step",
    )(
        frames,
        cache,
        owners.reshape(64, 1),
        valid_frames,
        wa_w,
        wb_w,
        wd02,
        wd1,
        gain,
        cbias,
        lbias,
    )


def solution(mesh):
    in_specs = (
        P("ba", None, "ha", "wa"),
        P("ba", None, "ha", "wa"),
        P(),
        P(),
        P(),
        P(),
        P(),
        P(),
        P(),
        P("ba"),
        P("ba", "ha", "wa", None, None),
    )
    out_specs = P("ba", "ha", "wa", None, None)
    return jax.shard_map(
        functools.partial(per_device, mesh.shape["ha"], mesh.shape["wa"]),
        mesh=mesh,
        in_specs=in_specs,
        out_specs=out_specs,
        check_vma=False,
    )
```

```python
import functools

import jax
import jax.numpy as jnp
import numpy as np
from jax import lax
from jax.experimental import pallas as pl
from jax.experimental.pallas import tpu as pltpu
from jax.sharding import PartitionSpec as P

EPS = 1e-06
C = 96
Z = 16
T = 4
TH = 32
TW = 52
OWN = 39
EXT = 42
FS = 48
KK = 27
QB = 8
KD = 1664
F32 = jnp.float32
BF16 = jnp.bfloat16


def lanes(tile, count=1):
    return pl.ds(pl.multiple_of(tile * 128, 128), count * 128)


def kernel(
    n_ha,
    n_wa,
    frames,
    cache,
    owners,
    valid,
    norm_gain,
    conv_weight,
    conv_bias,
    down_weight,
    down_bias,
    latent_weight,
    latent_bias,
    out,
    ext,
    pack_top,
    pack_bot,
    above,
    below,
    act,
    xf,
    planes,
    ones,
    hp,
    hb,
    l32,
    x32,
    hp32,
    h32,
    vs,
    taps,
    wa_w,
    wb_w,
    wd02,
    wd1,
    gain,
    cbias,
    send,
    received,
    local_sem,
    send_sem,
    recv_sem,
    a2a_send,
    a2a_recv,
):
    ha, wa = lax.axis_index("ha"), lax.axis_index("wa")
    up, down = lax.rem(ha + n_ha - 1, n_ha), lax.rem(ha + 1, n_ha)
    left, right = lax.rem(wa + n_wa - 1, n_wa), lax.rem(wa + 1, n_wa)

    load_cache = pltpu.make_async_copy(
        cache.at[0], ext.at[pl.ds(0, 2), :, pl.ds(0, OWN * 128)], local_sem.at[0]
    )
    load_frames = pltpu.make_async_copy(
        frames.at[0], ext.at[pl.ds(2, T), :, pl.ds(0, OWN * 128)], local_sem.at[1]
    )
    load_cache.start()
    load_frames.start()

    barrier = pltpu.get_barrier_semaphore()
    greeted = [
        {"ha": up, "wa": wa},
        {"ha": down, "wa": wa},
        {"ha": ha, "wa": left},
        {"ha": ha, "wa": right},
        {"ha": up, "wa": left},
        {"ha": up, "wa": right},
        {"ha": down, "wa": left},
        {"ha": down, "wa": right},
        {"ha": lax.rem(ha + 2, n_ha), "wa": wa},
    ]
    for device in greeted:
        pl.semaphore_signal(
            barrier, inc=1, device_id=device, device_id_type=pl.DeviceIdType.MESH
        )

    def remote(src, dst, index, device):
        return pltpu.make_async_remote_copy(
            src_ref=src,
            dst_ref=dst,
            send_sem=send_sem.at[index],
            recv_sem=recv_sem.at[index],
            device_id=device,
            device_id_type=pl.DeviceIdType.MESH,
        )

    load_cache.wait()
    load_frames.wait()

    sub = lax.broadcasted_iota(jnp.int32, (8, 384), 0)

    @pl.loop(0, OWN // 3)
    def _(g):
        win = lanes(3 * g, 3)
        tops = [ext[f, pl.ds(0, 16), win].astype(F32) for f in range(6)]
        bots = [ext[f, pl.ds(16, 16), win].astype(F32) for f in range(6)]
        lo = jnp.zeros((8, 384), F32)
        hi = jnp.zeros((8, 384), F32)
        for t in range(T):
            lo = jnp.where(sub == t, tops[2 + t][0:1], lo)
            lo = jnp.where(sub == 4 + t, tops[2 + t][1:2], lo)
        for t in range(2):
            hi = jnp.where(sub == t, tops[t][0:1], hi)
            hi = jnp.where(sub == 2 + t, tops[t][1:2], hi)
        pack_top[:, win] = jnp.concatenate([lo, hi], axis=0).astype(BF16)
        lo = jnp.zeros((8, 384), F32)
        for t in range(T):
            lo = jnp.where(sub == t, bots[2 + t][15:16], lo)
        for t in range(2):
            lo = jnp.where(sub == 4 + t, bots[t][15:16], lo)
        pack_bot[:, win] = jnp.concatenate([lo, jnp.zeros((8, 384), F32)], axis=0).astype(BF16)

    pl.semaphore_wait(barrier, len(greeted))

    own = pl.ds(0, OWN * 128)
    first, last = pl.ds(0, 256), pl.ds((OWN - 1) * 128, 128)
    from_right, from_left = pl.ds(OWN * 128, 256), pl.ds((OWN + 2) * 128, 128)
    row_copies = [
        remote(pack_top, below.at[:, own], 0, {"ha": up, "wa": wa}),
        remote(pack_bot, above.at[:, own], 1, {"ha": down, "wa": wa}),
        remote(pack_top.at[:, first], below.at[:, from_right], 2, {"ha": up, "wa": left}),
        remote(pack_top.at[:, last], below.at[:, from_left], 3, {"ha": up, "wa": right}),
        remote(pack_bot.at[:, first], above.at[:, from_right], 4, {"ha": down, "wa": left}),
        remote(pack_bot.at[:, last], above.at[:, from_left], 5, {"ha": down, "wa": right}),
    ]
    col_copies = [
        remote(
            frames.at[0, :, :, first],
            ext.at[pl.ds(2, T), :, from_right],
            6,
            {"ha": ha, "wa": left},
        ),
        remote(
            cache.at[0, :, :, first],
            ext.at[pl.ds(0, 2), :, from_right],
            7,
            {"ha": ha, "wa": left},
        ),
        remote(
            frames.at[0, :, :, last],
            ext.at[pl.ds(2, T), :, from_left],
            8,
            {"ha": ha, "wa": right},
        ),
        remote(
            cache.at[0, :, :, last],
            ext.at[pl.ds(0, 2), :, from_left],
            9,
            {"ha": ha, "wa": right},
        ),
    ]
    for copy in row_copies + col_copies:
        copy.start()

    lane = lax.broadcasted_iota(jnp.int32, (1, 128), 1)

    @pl.loop(0, C // 4)
    def _(g):
        win = lanes(3 * g, 3)
        for weight, count, at in ((conv_weight, 27, 0), (down_weight, 9, 27)):
            x = weight[:, win].astype(F32)
            t0, t1, t2 = (x[:, 128 * j : 128 * (j + 1)] for j in range(3))
            parts = [
                t0,
                jnp.where(lane < 32, pltpu.roll(t0, 32, 1), pltpu.roll(t1, 32, 1)),
                jnp.where(lane < 64, pltpu.roll(t1, 64, 1), pltpu.roll(t2, 64, 1)),
                pltpu.roll(t2, 96, 1),
            ]
            for u in range(4):
                taps[pl.ds(at * C + 4 * g + u, count, C)] = jnp.where(lane < C, parts[u], 0.0)

    @pl.loop(0, 9)
    def _(n):
        w = [taps[pl.ds((3 * n + s) * C, C)] for s in range(3)]
        zero = jnp.zeros((C, 128), F32)
        by96 = [zero] + [pltpu.roll(x, 96, 1) for x in w]
        by64 = [pltpu.roll(x, 64, 1) for x in w] + [zero]
        by32 = [zero] + [pltpu.roll(x, 32, 1) for x in w]
        w = w + [zero]
        for s in range(4):
            rows = pl.ds(pl.multiple_of(n * 384 + s * 96, 32), C)
            wa_w[rows, pl.ds(0, 128)] = jnp.where(lane < 96, w[s], by96[s]).astype(BF16)
            wa_w[rows, pl.ds(128, 128)] = jnp.where(lane < 64, by96[s], 0.0).astype(BF16)
            one = jnp.where(lane < 64, 0.0, by64[s]).astype(BF16)
            two = jnp.where(lane < 32, by64[s], by32[s]).astype(BF16)
            if s < 3:
                rows = pl.ds(pl.multiple_of(n * 384 + s * 96 + 64, 32), C)
                wb_w[rows, pl.ds(0, 128)] = one
                wb_w[rows, pl.ds(128, 128)] = two
            else:
                rows = pl.ds(pl.multiple_of(n * 384 + 352, 32), 32)
                wb_w[rows, pl.ds(0, 128)] = one[:32]
                wb_w[rows, pl.ds(128, 128)] = two[:32]
                rows = pl.ds(pl.multiple_of(n * 384, 32), 64)
                wb_w[rows, pl.ds(0, 128)] = one[32:]
                wb_w[rows, pl.ds(128, 128)] = two[32:]

    by_z = jnp.concatenate([latent_weight[...]] * QB, axis=0)
    by_column = (((1,), (1,)), ((), ()))
    for t in range(9):
        tap = taps[pl.ds((27 + t) * C, C)][:, :C].astype(BF16)
        taps[pl.ds((27 + t) * C, C)] = lax.dot_general(
            tap, by_z, by_column, preferred_element_type=F32
        )
    slot_of = sum((lane >= 16 * q).astype(jnp.int32) for q in range(1, QB))
    for r in range(3):
        target, at = ((wd02, 0), (wd1, 0), (wd02, 128))[r]
        target[pl.ds(0, 32), pl.ds(at, 128)] = jnp.zeros((32, 128), BF16)

        @pl.loop(0, 2 * QB + 1)
        def _(col):
            block = jnp.zeros((C, 128), F32)
            for s in range(3):
                fits = (2 * slot_of + s) == col
                block = jnp.where(fits, taps[pl.ds((27 + 3 * r + s) * C, C)], block)
            rows = pl.ds(pl.multiple_of(32 + C * col, 32), C)
            target[rows, pl.ds(at, 128)] = block.astype(BF16)

    rest = down_bias[...]
    pieces = []
    for _ in range(3):
        piece = rest.astype(BF16)
        pieces.append(piece.astype(F32))
        rest = rest - pieces[-1]
    pieces = jnp.concatenate(pieces + [jnp.zeros((13, C), F32)], axis=0).astype(BF16)
    lbias = jnp.sum(
        lax.dot_general(pieces, by_z, by_column, preferred_element_type=F32),
        axis=0,
        keepdims=True,
    ) + jnp.concatenate([latent_bias[...]] * QB, axis=1)

    gain[...] = jnp.concatenate([norm_gain[...]] * 4, axis=1)
    bias = conv_bias[...]
    bias = jnp.concatenate([bias[:, 64:]] + [bias] * 3 + [bias[:, :64]], axis=1)
    for j in range(3):
        cbias[j] = bias[:, 128 * j : 128 * (j + 1)]

    def column_of(axis):
        index = lax.broadcasted_iota(jnp.int32, (384, 384), axis)
        return sum((index >= edge).astype(jnp.int32) for edge in (96, 192, 288))

    ones[...] = jnp.where(column_of(0) == column_of(1), 1.0, 0.0).astype(BF16)

    has_left = jnp.where(wa == 0, 0.0, 1.0).astype(F32)
    has_right = jnp.where(wa == n_wa - 1, 0.0, 1.0).astype(F32)
    has_above = jnp.where(ha == 0, 0.0, 1.0).astype(F32)
    has_below = jnp.where(ha == n_ha - 1, 0.0, 1.0).astype(F32)

    def activate(x):
        squares = jnp.dot((x * x).astype(BF16), ones[...], preferred_element_type=F32)
        v = x * lax.rsqrt(squares * (1.0 / C) + EPS) * gain[...]
        return v / (1.0 + jnp.exp(-v))

    def halo_mask(x):
        return jnp.concatenate([x[:, :256] * has_right, x[:, 256:] * has_left], axis=1)

    def split_rows(tile, even, odd, even_at, odd_at):
        for f in range(6):
            rows = pl.ds(f * 16, 16)
            planes[even, tile + 1, rows] = act[tile, pl.ds(f * FS + even_at, 16, 2)].astype(BF16)
            planes[odd, tile + 1, rows] = act[tile, pl.ds(f * FS + odd_at, 16, 2)].astype(BF16)

    def group(g, edge):
        win = lanes(3 * g, 3)
        x = ext[pl.ds(2, T), :, win].reshape(T * TH, 384).astype(F32)
        earlier = ext[pl.ds(0, 2), :, win].reshape(2 * TH, 384).astype(F32)
        if edge:
            x, earlier = halo_mask(x), halo_mask(earlier)
        activated = activate(x)
        for j in range(3):
            cut = slice(128 * j, 128 * (j + 1))
            for f in range(6):
                source = earlier if f < 2 else activated
                at = (f if f < 2 else f - 2) * TH
                act[3 * g + j, pl.ds(f * FS + 8, TH)] = source[at : at + TH, cut]
            split_rows(3 * g + j, 1, 2, 8, 9)
        before = ext[pl.ds(2, T), :, lanes(jnp.maximum(3 * g - 1, 0))]
        before = pltpu.roll(before.reshape(T * TH, 128).astype(F32), 32, 1)
        for j in range(1 if edge else 3):
            here = pltpu.roll(x[:, 128 * j : 128 * (j + 1)], 32, 1)
            xf[3 * g + j + 1] = jnp.where(lane < 32, before, here)
            before = here

    @pl.loop(0, OWN // 3)
    def _(g):
        group(g, False)

    for copy in col_copies:
        copy.wait_recv()
    group(OWN // 3, True)
    for copy in row_copies:
        copy.wait_recv()

    def halo_group(g, edge):
        win = lanes(3 * g, 3)
        hi = below[:, win].astype(F32) * has_below
        lo = above[:, win].astype(F32) * has_above
        if edge:
            hi, lo = halo_mask(hi), halo_mask(lo)
        activated = activate(jnp.concatenate([hi[:8], lo[:8]], axis=0))
        for j in range(3):
            cut = slice(128 * j, 128 * (j + 1))
            tile = 3 * g + j
            act[tile, pl.ds(2 * FS + 40, T, FS)] = activated[0:4, cut]
            act[tile, pl.ds(2 * FS + 41, T, FS)] = activated[4:8, cut]
            act[tile, pl.ds(2 * FS + 7, T, FS)] = activated[8:12, cut]
            act[tile, pl.ds(40, 2, FS)] = hi[8:10, cut]
            act[tile, pl.ds(41, 2, FS)] = hi[10:12, cut]
            act[tile, pl.ds(7, 2, FS)] = lo[4:6, cut]
            split_rows(tile, 3, 0, 10, 7)
        before = below[:, lanes(jnp.maximum(3 * g - 1, 0))].astype(F32) * has_below
        before = pltpu.roll(before[:8], 32, 1)
        for j in range(1 if edge else 3):
            here = pltpu.roll(hi[:8, 128 * j : 128 * (j + 1)], 32, 1)
            x32[3 * g + j + 1] = jnp.where(lane < 32, before, here)
            before = here

    @pl.loop(0, OWN // 3)
    def _(g):
        halo_group(g, False)

    halo_group(OWN // 3, True)

    @pl.loop(0, 4)
    def _(plane):
        planes[plane, 0] = planes[plane, EXT]

        @pl.loop(0, 14)
        def _(i):
            later = planes[plane, 3 * i + 2].astype(F32)
            sooner = planes[plane, jnp.where(i == 0, 41, 3 * i - 1)].astype(F32)
            planes[plane, EXT + 1 + i] = jnp.where(lane < 64, later, sooner).astype(BF16)

    @pl.loop(0, 14)
    def _(i):
        for a in range(3):
            for r in range(3):
                rows = pl.ds(a * FS + 39 + r, T, FS)
                kk = (3 * a + r) * 3
                here = pl.ds(0, T)
                for j in range(3):
                    l32[0, i, kk + j, here] = act[3 * i + j, rows]
                later = act[3 * i + 1, rows]
                sooner = act[jnp.where(i == 0, 40, 3 * i - 2), rows]
                l32[1, i, kk, here] = jnp.where(lane < 64, later, sooner)
                l32[1, i, kk + 1, here] = act[jnp.where(i == 0, 41, 3 * i - 1), rows]
                l32[1, i, kk + 2, here] = act[3 * i, rows]

    def tile_a(k, j):
        return 3 * k + j + 1

    def tile_b(i, j):
        return EXT + 1 + i if j == 0 else 3 * i + j - 1

    def conv(parity, base, count, tile_of, weights):
        rows = []
        for w in range(count):
            pieces = []
            for a in range(3):
                for r in range(3):
                    for j in range(3):
                        pieces.append(
                            planes[r + parity, tile_of(base + w, j), pl.ds(a * 16, 64)]
                        )
            rows.append(jnp.concatenate(pieces, axis=1))
        return jnp.dot(
            jnp.concatenate(rows, axis=0), weights[...], preferred_element_type=F32
        )

    @pl.loop(0, 4)
    def _(step):
        parity, base = step // 2, (step % 2) * 6
        acc = conv(parity, base, 7, tile_a, wa_w)
        for w in range(7):
            k = base + w
            part = acc[64 * w : 64 * (w + 1)]
            x = xf[3 * k + 2, pl.ds(parity, 64, 2)]
            hb[parity, 3 * k + 2] = (x + part[:, :128] + cbias[1]).astype(BF16)
            hp[parity, k + 1] = part[:, 128:]

    cut_right = jnp.where((lane >= 32) & (wa == n_wa - 1), 0.0, 1.0).astype(F32)

    @pl.loop(0, 4)
    def _(step):
        parity, base = step // 2, (step % 2) * 7
        acc = conv(parity, base, 7, tile_b, wb_w)
        for w in range(7):
            i = base + w
            part = acc[64 * w : 64 * (w + 1)]
            x = xf[3 * i, pl.ds(parity, 64, 2)]
            hb[parity, 3 * i] = (x + part[:, :128] + hp[parity, i] + cbias[2]).astype(BF16)
            x = xf[3 * i + 1, pl.ds(parity, 64, 2)]
            h = x + part[:, 128:] + cbias[0]
            h = h * jnp.where(i == 13, cut_right, 1.0)
            hb[parity, 3 * i + 1] = h.astype(BF16)

    def conv32(side, weights):
        rows = []
        for w in range(14):
            rows.append(jnp.concatenate([l32[side, w, kk] for kk in range(KK)], axis=1))
        lhs = jnp.concatenate(rows, axis=0).astype(BF16)
        return jnp.dot(lhs, weights[...], preferred_element_type=F32)

    def put32(index, value):
        h32[index] = jnp.concatenate([value * has_below, jnp.zeros((8, 128), F32)], axis=0).astype(
            BF16
        )

    acc = conv32(0, wa_w)
    for k in range(13):
        part = acc[8 * k : 8 * (k + 1)]
        put32(3 * k + 2, x32[3 * k + 2] + part[:, :128] + cbias[1])
        hp32[k + 1] = part[:, 128:]
    acc = conv32(1, wb_w)
    for i in range(14):
        part = acc[8 * i : 8 * (i + 1)]
        if i:
            put32(3 * i, x32[3 * i] + part[:, :128] + hp32[i] + cbias[2])
        h = x32[3 * i + 1] + part[:, 128:] + cbias[0]
        put32(3 * i + 1, h * cut_right if i == 13 else h)

    def block(b, count):
        even = jnp.concatenate([hb[0, 12 * b + j + 1] for j in range(count)], axis=1)
        odd = jnp.concatenate([hb[1, 12 * b + j + 1] for j in range(count)], axis=1)
        extra = jnp.concatenate([h32[12 * b + j + 1] for j in range(count)], axis=1)
        return even, extra, odd

    blocks = [block(b, 13) for b in range(3)]
    uv = jnp.dot(
        jnp.concatenate([piece for b in blocks for piece in b[:2]], axis=0),
        wd02[...],
        preferred_element_type=F32,
    )
    u1 = jnp.dot(
        jnp.concatenate([b[2] for b in blocks], axis=0), wd1[...], preferred_element_type=F32
    )
    even, extra, odd = block(3, 4)
    uv_last = jnp.dot(
        jnp.concatenate([even, extra], axis=0), wd02[pl.ds(0, 512)], preferred_element_type=F32
    )
    u1_last = jnp.dot(odd, wd1[pl.ds(0, 512)], preferred_element_type=F32)

    latents = []
    for b in range(4):
        both = uv[80 * b : 80 * (b + 1)] if b < 3 else uv_last
        mid = u1[64 * b : 64 * (b + 1)] if b < 3 else u1_last
        for t in range(T):
            vs[t, pl.ds(0, 16)] = both[16 * t : 16 * (t + 1), 128:]
            vs[t, pl.ds(16, 1)] = both[64 + t : 65 + t, 128:]
        shifted = jnp.concatenate([vs[t, pl.ds(1, 16)] for t in range(T)], axis=0)
        latents.append(both[:64, :128] + mid + shifted + lbias)
    latent = jnp.concatenate(latents[:3] + [latents[3][:, :32]], axis=1)
    frame_of = lax.broadcasted_iota(jnp.int32, (64, 1), 0)
    latent = jnp.where(frame_of < valid[0] * 16, latent, 0.0).astype(BF16)

    row = lax.broadcasted_iota(jnp.int32, (64, 64), 0)
    col = lax.broadcasted_iota(jnp.int32, (64, 64), 1)
    by_col = jnp.broadcast_to(owners[...], (64, 64))
    by_row = jnp.sum(jnp.where(row == col, by_col, 0), axis=1, keepdims=True)
    rank = jnp.sum(jnp.where((by_row == by_col) & (row < col), 1, 0), axis=0, keepdims=True)
    slot = owners[...] * 32 + rank
    slots = lax.broadcasted_iota(jnp.int32, (128, 64), 0)
    selector = jnp.where(slots == slot, 1.0, 0.0).astype(BF16)
    send[...] = jnp.dot(selector, latent, preferred_element_type=F32).astype(BF16)

    here = pl.ds(pl.multiple_of(ha * 32, 32), 32)
    copies = []
    for d in range(1, n_ha):
        target = lax.rem(ha + d, n_ha)
        copies.append(
            pltpu.make_async_remote_copy(
                src_ref=send.at[pl.ds(pl.multiple_of(target * 32, 32), 32)],
                dst_ref=received.at[here],
                send_sem=a2a_send.at[d - 1],
                recv_sem=a2a_recv.at[d - 1],
                device_id={"ha": target, "wa": wa},
                device_id_type=pl.DeviceIdType.MESH,
            )
        )
    for copy in copies:
        copy.start()
    received[here] = send[here]
    for copy in row_copies + col_copies:
        copy.wait_send()
    for copy in copies:
        copy.wait()
    full = jnp.concatenate([received[...].astype(F32), jnp.zeros((128, 96), F32)], axis=1)
    out[0, 0, 0] = full.T[:416].astype(BF16)


def per_device(
    n_ha,
    n_wa,
    frames,
    cache,
    norm_gain,
    conv_weight,
    conv_bias,
    down_weight,
    down_bias,
    latent_weight,
    latent_bias,
    valid_frames,
    owners,
):
    vmem = pl.BlockSpec(memory_space=pltpu.VMEM)
    anyspace = pl.BlockSpec(memory_space=pl.ANY)
    routed = pl.pallas_call(
        functools.partial(kernel, n_ha, n_wa),
        out_shape=jax.ShapeDtypeStruct((1, 1, 1, 416, 128), BF16),
        in_specs=[anyspace, anyspace, vmem, pl.BlockSpec(memory_space=pltpu.SMEM)] + [vmem] * 7,
        out_specs=vmem,
        scratch_shapes=[
            pltpu.VMEM((6, TH, EXT * 128), BF16),
            pltpu.VMEM((16, OWN * 128), BF16),
            pltpu.VMEM((16, OWN * 128), BF16),
            pltpu.VMEM((16, EXT * 128), BF16),
            pltpu.VMEM((16, EXT * 128), BF16),
            pltpu.VMEM((EXT, 6 * FS, 128), F32),
            pltpu.VMEM((41, T * TH, 128), F32),
            pltpu.VMEM((4, EXT + 15, 96, 128), BF16),
            pltpu.VMEM((384, 384), BF16),
            pltpu.VMEM((2, 14, 64, 128), F32),
            pltpu.VMEM((2, 41, 64, 128), BF16),
            pltpu.VMEM((2, 14, KK, 8, 128), F32),
            pltpu.VMEM((41, 8, 128), F32),
            pltpu.VMEM((14, 8, 128), F32),
            pltpu.VMEM((41, 16, 128), BF16),
            pltpu.VMEM((T, 24, 128), F32),
            pltpu.VMEM((36 * C, 128), F32),
            pltpu.VMEM((KK * 128, 256), BF16),
            pltpu.VMEM((KK * 128, 256), BF16),
            pltpu.VMEM((KD, 256), BF16),
            pltpu.VMEM((KD, 128), BF16),
            pltpu.VMEM((1, 384), F32),
            pltpu.VMEM((3, 1, 128), F32),
            pltpu.VMEM((128, 416), BF16),
            pltpu.VMEM((128, 416), BF16),
            pltpu.SemaphoreType.DMA((2,)),
            pltpu.SemaphoreType.DMA((10,)),
            pltpu.SemaphoreType.DMA((10,)),
            pltpu.SemaphoreType.DMA((n_ha - 1,)),
            pltpu.SemaphoreType.DMA((n_ha - 1,)),
        ],
        compiler_params=pltpu.CompilerParams(
            collective_id=0, has_side_effects=True, vmem_limit_bytes=56 * 2**20
        ),
        name="encoder_step",
    )(
        frames,
        cache,
        owners.reshape(1, 64),
        valid_frames,
        norm_gain.reshape(1, C),
        conv_weight,
        conv_bias.reshape(1, C),
        down_weight,
        down_bias.reshape(1, C),
        latent_weight.T,
        latent_bias.reshape(1, Z),
    )
    return jnp.swapaxes(routed, 3, 4)


def solution(mesh):
    in_specs = (
        P("ba", None, "ha", "wa"),
        P("ba", None, "ha", "wa"),
        P(),
        P(),
        P(),
        P(),
        P(),
        P(),
        P(),
        P("ba"),
        P("ba", "ha", "wa", None, None),
    )
    out_specs = P("ba", "ha", "wa", None, None)
    return jax.shard_map(
        functools.partial(per_device, mesh.shape["ha"], mesh.shape["wa"]),
        mesh=mesh,
        in_specs=in_specs,
        out_specs=out_specs,
        check_vma=False,
    )
```

```python
import functools

import jax
import jax.numpy as jnp
import numpy as np
from jax import lax
from jax.experimental import pallas as pl
from jax.experimental.pallas import tpu as pltpu
from jax.sharding import PartitionSpec as P

EPS = 1e-06
C = 96
Z = 16
T = 4
TH = 32
TW = 52
OWN = 39
EXT = 42
FS = 48
KK = 27
QB = 8
F32 = jnp.float32
BF16 = jnp.bfloat16


def lanes(tile, count=1):
    return pl.ds(pl.multiple_of(tile * 128, 128), count * 128)


def kernel(
    n_ha,
    n_wa,
    frames,
    cache,
    owners,
    valid,
    norm_gain,
    conv_weight,
    conv_bias,
    down_weight,
    down_bias,
    latent_weight,
    latent_bias,
    out,
    ext,
    pack_top,
    pack_bot,
    above,
    below,
    act,
    xf,
    planes,
    ones,
    middle,
    hp,
    hb,
    l32,
    x32,
    hp32,
    h32,
    vs,
    conv_taps,
    down_taps,
    taps,
    wa_w,
    wb_w,
    down_w,
    gain,
    cbias,
    lbias,
    send,
    received,
    local_sem,
    send_sem,
    recv_sem,
    a2a_send,
    a2a_recv,
):
    ha, wa = lax.axis_index("ha"), lax.axis_index("wa")
    up, down = lax.rem(ha + n_ha - 1, n_ha), lax.rem(ha + 1, n_ha)
    left, right = lax.rem(wa + n_wa - 1, n_wa), lax.rem(wa + 1, n_wa)

    load_cache = pltpu.make_async_copy(
        cache.at[0], ext.at[pl.ds(0, 2), :, pl.ds(0, OWN * 128)], local_sem.at[0]
    )
    load_frames = pltpu.make_async_copy(
        frames.at[0], ext.at[pl.ds(2, T), :, pl.ds(0, OWN * 128)], local_sem.at[1]
    )
    load_conv = pltpu.make_async_copy(conv_weight, conv_taps, local_sem.at[2])
    load_down = pltpu.make_async_copy(down_weight, down_taps, local_sem.at[3])
    loads = [load_cache, load_frames, load_conv, load_down]
    for load in loads:
        load.start()

    barrier = pltpu.get_barrier_semaphore()
    greeted = [
        {"ha": up, "wa": wa},
        {"ha": down, "wa": wa},
        {"ha": ha, "wa": left},
        {"ha": ha, "wa": right},
        {"ha": up, "wa": left},
        {"ha": up, "wa": right},
        {"ha": down, "wa": left},
        {"ha": down, "wa": right},
        {"ha": lax.rem(ha + 2, n_ha), "wa": wa},
    ]
    for device in greeted:
        pl.semaphore_signal(
            barrier, inc=1, device_id=device, device_id_type=pl.DeviceIdType.MESH
        )

    def remote(src, dst, index, device):
        return pltpu.make_async_remote_copy(
            src_ref=src,
            dst_ref=dst,
            send_sem=send_sem.at[index],
            recv_sem=recv_sem.at[index],
            device_id=device,
            device_id_type=pl.DeviceIdType.MESH,
        )

    load_cache.wait()
    load_frames.wait()

    sub = lax.broadcasted_iota(jnp.int32, (8, 384), 0)

    @pl.loop(0, OWN // 3)
    def _(g):
        win = lanes(3 * g, 3)
        tops = [ext[f, pl.ds(0, 16), win].astype(F32) for f in range(6)]
        bots = [ext[f, pl.ds(16, 16), win].astype(F32) for f in range(6)]
        lo = jnp.zeros((8, 384), F32)
        hi = jnp.zeros((8, 384), F32)
        for t in range(T):
            lo = jnp.where(sub == t, tops[2 + t][0:1], lo)
            lo = jnp.where(sub == 4 + t, tops[2 + t][1:2], lo)
        for t in range(2):
            hi = jnp.where(sub == t, tops[t][0:1], hi)
            hi = jnp.where(sub == 2 + t, tops[t][1:2], hi)
        pack_top[:, win] = jnp.concatenate([lo, hi], axis=0).astype(BF16)
        lo = jnp.zeros((8, 384), F32)
        for t in range(T):
            lo = jnp.where(sub == t, bots[2 + t][15:16], lo)
        for t in range(2):
            lo = jnp.where(sub == 4 + t, bots[t][15:16], lo)
        pack_bot[:, win] = jnp.concatenate([lo, jnp.zeros((8, 384), F32)], axis=0).astype(BF16)

    pl.semaphore_wait(barrier, len(greeted))

    own = pl.ds(0, OWN * 128)
    first, last = pl.ds(0, 256), pl.ds((OWN - 1) * 128, 128)
    from_right, from_left = pl.ds(OWN * 128, 256), pl.ds((OWN + 2) * 128, 128)
    row_copies = [
        remote(pack_top, below.at[:, own], 0, {"ha": up, "wa": wa}),
        remote(pack_bot, above.at[:, own], 1, {"ha": down, "wa": wa}),
        remote(pack_top.at[:, first], below.at[:, from_right], 2, {"ha": up, "wa": left}),
        remote(pack_top.at[:, last], below.at[:, from_left], 3, {"ha": up, "wa": right}),
        remote(pack_bot.at[:, first], above.at[:, from_right], 4, {"ha": down, "wa": left}),
        remote(pack_bot.at[:, last], above.at[:, from_left], 5, {"ha": down, "wa": right}),
    ]
    col_copies = [
        remote(
            frames.at[0, :, :, first],
            ext.at[pl.ds(2, T), :, from_right],
            6,
            {"ha": ha, "wa": left},
        ),
        remote(
            cache.at[0, :, :, first],
            ext.at[pl.ds(0, 2), :, from_right],
            7,
            {"ha": ha, "wa": left},
        ),
        remote(
            frames.at[0, :, :, last],
            ext.at[pl.ds(2, T), :, from_left],
            8,
            {"ha": ha, "wa": right},
        ),
        remote(
            cache.at[0, :, :, last],
            ext.at[pl.ds(0, 2), :, from_left],
            9,
            {"ha": ha, "wa": right},
        ),
    ]
    for copy in row_copies + col_copies:
        copy.start()

    lane = lax.broadcasted_iota(jnp.int32, (1, 128), 1)

    gain[...] = jnp.concatenate([norm_gain[...]] * 4, axis=1) * (0.5 * C**0.5)

    def column_of(axis):
        index = lax.broadcasted_iota(jnp.int32, (384, 384), axis)
        return sum((index >= edge).astype(jnp.int32) for edge in (96, 192, 288))

    ones[...] = jnp.where(column_of(0) == column_of(1), 1.0, 0.0).astype(BF16)

    has_left = jnp.where(wa == 0, 0.0, 1.0).astype(F32)
    has_right = jnp.where(wa == n_wa - 1, 0.0, 1.0).astype(F32)
    has_above = jnp.where(ha == 0, 0.0, 1.0).astype(F32)
    has_below = jnp.where(ha == n_ha - 1, 0.0, 1.0).astype(F32)

    def activate(x):
        squares = jnp.dot((x * x).astype(BF16), ones[...], preferred_element_type=F32)
        u = x * lax.rsqrt(squares + C * EPS) * gain[...]
        return u + u * jnp.tanh(u)

    def halo_mask(x):
        return jnp.concatenate([x[:, :256] * has_right, x[:, 256:] * has_left], axis=1)

    def groups(gs, edge):
        xs, earlier = [], []
        for g in gs:
            win = lanes(3 * g, 3)
            x = ext[pl.ds(2, T), :, win].reshape(T * TH, 384).astype(F32)
            old = ext[pl.ds(0, 2), :, win].reshape(2 * TH, 384).astype(F32)
            if edge and g == 13:
                x, old = halo_mask(x), halo_mask(old)
            xs.append(x)
            earlier.append(old)
        activated = activate(jnp.concatenate(xs, axis=0))
        for n, g in enumerate(gs):
            before = ext[pl.ds(2, T), :, lanes(jnp.maximum(3 * g - 1, 0))]
            before = pltpu.roll(before.reshape(T * TH, 128).astype(F32), 32, 1)
            for j in range(1 if edge and g == 13 else 3):
                here = pltpu.roll(xs[n][:, 128 * j : 128 * (j + 1)], 32, 1)
                xf[3 * g + j + 1] = jnp.where(lane < 32, before, here)
                before = here
            for j in range(3):
                part = slice(128 * j, 128 * (j + 1))
                tile = 3 * g + j
                for f in range(6):
                    if f < 2:
                        value = earlier[n][f * TH : (f + 1) * TH, part]
                    else:
                        at = n * T * TH + (f - 2) * TH
                        value = activated[at : at + TH, part]
                    act[tile, pl.ds(f * FS + 8, TH)] = value
                for f in range(6):
                    d1 = act[tile, pl.ds(f * FS + 8, 16, 2)]
                    d2 = act[tile, pl.ds(f * FS + 9, 16, 2)]
                    planes[1, tile + 1, pl.ds(f * 16, 16)] = (d1 + d2).astype(BF16)
                    planes[2, tile + 1, pl.ds(f * 16, 16)] = (d2 - d1).astype(BF16)

    @pl.loop(0, 4)
    def _(n):
        groups([3 * n, 3 * n + 1, 3 * n + 2], False)

    load_conv.wait()
    load_down.wait()

    @pl.loop(0, C // 4)
    def _(g):
        win = lanes(3 * g, 3)
        for weight, count, at in ((conv_taps, 27, 0), (down_taps, 9, 27)):
            x = weight[:, win].astype(F32)
            t0, t1, t2 = (x[:, 128 * j : 128 * (j + 1)] for j in range(3))
            parts = [
                t0,
                jnp.where(lane < 32, pltpu.roll(t0, 32, 1), pltpu.roll(t1, 32, 1)),
                jnp.where(lane < 64, pltpu.roll(t1, 64, 1), pltpu.roll(t2, 64, 1)),
                pltpu.roll(t2, 96, 1),
            ]
            for u in range(4):
                taps[pl.ds(at * C + 4 * g + u, count, C)] = jnp.where(lane < C, parts[u], 0.0)

    @pl.loop(0, 3)
    def _(a):
        for m in range(4):
            w = []
            for s in range(3):
                g0, g1, g2 = (taps[pl.ds((9 * a + 3 * r + s) * C, C)] for r in range(3))
                if m == 0:
                    w.append(g0)
                elif m == 1:
                    w.append(0.5 * (g0 + g2 + g1))
                elif m == 2:
                    w.append(0.5 * (g0 + g2 - g1))
                else:
                    w.append(g2)
            zero = jnp.zeros((C, 128), F32)
            by96 = [zero] + [pltpu.roll(x, 96, 1) for x in w]
            by64 = [pltpu.roll(x, 64, 1) for x in w] + [zero]
            by32 = [zero] + [pltpu.roll(x, 32, 1) for x in w]
            w = w + [zero]
            at = m * 1152 + a * 384
            for s in range(4):
                rows = pl.ds(pl.multiple_of(at + s * 96, 32), C)
                wa_w[rows, pl.ds(0, 128)] = jnp.where(lane < 96, w[s], by96[s]).astype(BF16)
                wa_w[rows, pl.ds(128, 128)] = jnp.where(lane < 64, by96[s], 0.0).astype(BF16)
                one = jnp.where(lane < 64, 0.0, by64[s]).astype(BF16)
                two = jnp.where(lane < 32, by64[s], by32[s]).astype(BF16)
                if s < 3:
                    rows = pl.ds(pl.multiple_of(at + s * 96 + 64, 32), C)
                    wb_w[rows, pl.ds(0, 128)] = one
                    wb_w[rows, pl.ds(128, 128)] = two
                else:
                    rows = pl.ds(pl.multiple_of(at + 352, 32), 32)
                    wb_w[rows, pl.ds(0, 128)] = one[:32]
                    wb_w[rows, pl.ds(128, 128)] = two[:32]
                    rows = pl.ds(pl.multiple_of(at, 32), 64)
                    wb_w[rows, pl.ds(0, 128)] = one[32:]
                    wb_w[rows, pl.ds(128, 128)] = two[32:]

    by_z = jnp.concatenate([latent_weight[...]] * QB, axis=0)
    by_column = (((1,), (1,)), ((), ()))
    fused = lax.dot_general(
        taps[pl.ds(27 * C, 9 * C)][:, :C].astype(BF16),
        by_z,
        by_column,
        preferred_element_type=F32,
    )
    down_w[...] = jnp.zeros((1024, 128), BF16)
    for r in range(3):
        first = (0, 0, 2)[r]
        for col in range(5):
            block = jnp.zeros((C, 128), F32)
            for s in range(3):
                q = col - s
                if q in (0, 2):
                    tap = fused[(3 * r + s) * C : (3 * r + s + 1) * C]
                    place = first + q // 2
                    block = jnp.where((lane >= 16 * place) & (lane < 16 * (place + 1)), tap, block)
            rows = pl.ds((512 if r == 1 else 0) + 32 + C * col, C)
            if r == 2:
                block = block + down_w[rows].astype(F32)
            down_w[rows] = block.astype(BF16)

    rest = down_bias[...]
    pieces = []
    for _ in range(3):
        piece = rest.astype(BF16)
        pieces.append(piece.astype(F32))
        rest = rest - pieces[-1]
    pieces = jnp.concatenate(pieces + [jnp.zeros((13, C), F32)], axis=0).astype(BF16)
    lbias_row = jnp.sum(
        lax.dot_general(pieces, by_z, by_column, preferred_element_type=F32),
        axis=0,
        keepdims=True,
    ) + jnp.concatenate([latent_bias[...]] * QB, axis=1)

    lbias[...] = lbias_row
    bias = conv_bias[...]
    bias = jnp.concatenate([bias[:, 64:]] + [bias] * 3 + [bias[:, :64]], axis=1)
    for j in range(3):
        cbias[j] = bias[:, 128 * j : 128 * (j + 1)]

    for copy in col_copies:
        copy.wait_recv()
    groups([12, 13], True)
    for copy in row_copies:
        copy.wait_recv()

    @pl.loop(0, 2)
    def _(half):
        his, los = [], []
        for n in range(7):
            g = 7 * half + n
            win = lanes(3 * g, 3)
            hi = below[:, win].astype(F32) * has_below
            lo = above[:, win].astype(F32) * has_above
            if n == 6:
                right_on = jnp.where(half == 1, has_right, 1.0)
                left_on = jnp.where(half == 1, has_left, 1.0)
                hi, lo = (
                    jnp.concatenate([x[:, :256] * right_on, x[:, 256:] * left_on], axis=1)
                    for x in (hi, lo)
                )
            his.append(hi)
            los.append(lo)
        activated = activate(
            jnp.concatenate([x[:8] for pair in zip(his, los) for x in pair], axis=0)
        )
        before = below[:, lanes(jnp.maximum(21 * half - 1, 0))].astype(F32) * has_below
        before = pltpu.roll(before[:8], 32, 1)
        for n in range(7):
            for j in range(3):
                part = slice(128 * j, 128 * (j + 1))
                tile = 21 * half + 3 * n + j
                new = activated[16 * n : 16 * (n + 1), part]
                act[tile, pl.ds(2 * FS + 40, T, FS)] = new[0:4]
                act[tile, pl.ds(2 * FS + 41, T, FS)] = new[4:8]
                act[tile, pl.ds(2 * FS + 7, T, FS)] = new[8:12]
                act[tile, pl.ds(40, 2, FS)] = his[n][8:10, part]
                act[tile, pl.ds(41, 2, FS)] = his[n][10:12, part]
                act[tile, pl.ds(7, 2, FS)] = los[n][4:6, part]
                here = pltpu.roll(his[n][:8, part], 32, 1)
                x32[tile + 1] = jnp.where(lane < 32, before, here)
                before = here

    @pl.loop(0, EXT // 3)
    def _(g):
        for j in range(3):
            tile = 3 * g + j
            for f in range(6):
                d0, d1, d2, d3 = (act[tile, pl.ds(f * FS + 7 + r, 16, 2)] for r in range(4))
                planes[0, tile + 1, pl.ds(f * 16, 16)] = (d0 - d2).astype(BF16)
                planes[3, tile + 1, pl.ds(f * 16, 16)] = (d1 - d3).astype(BF16)

            for a in range(3):
                d0, d1, d2 = (act[tile, pl.ds(a * FS + 39 + r, T, FS)] for r in range(3))
                l32[tile, a, pl.ds(0, T)] = d0 - d2
                l32[tile, 3 + a, pl.ds(0, T)] = d1 + d2
                l32[tile, 6 + a, pl.ds(0, T)] = d2 - d1

    @pl.loop(0, 4)
    def _(plane):
        planes[plane, 0] = planes[plane, EXT]
        for i in range(14):
            later = planes[plane, 3 * i + 2]
            sooner = planes[plane, 41 if i == 0 else 3 * i - 1]
            planes[plane, EXT + 1 + i] = jnp.where(lane < 64, later, sooner)

    for i in range(14):
        sooner = 40 if i == 0 else 3 * i - 2
        for n in range(9):
            l32[EXT + i, n] = jnp.where(lane < 64, l32[3 * i + 1, n], l32[sooner, n])

    def tile_a(k, j):
        return 3 * k + j + 1

    def tile_b(i, j):
        return EXT + 1 + i if j == 0 else 3 * i + j - 1

    def conv(base, count, tile_of, weights):
        def product(m):
            rows = []
            for w in range(count):
                pieces = [
                    planes[m, tile_of(base + w, j), pl.ds(a * 16, 64)]
                    for a in range(3)
                    for j in range(3)
                ]
                rows.append(jnp.concatenate(pieces, axis=1))
            return jnp.dot(
                jnp.concatenate(rows, axis=0),
                weights[pl.ds(m * 1152, 1152)],
                preferred_element_type=F32,
            )

        middle[0] = product(1)
        middle[1] = product(2)
        even = product(0) + (middle[0] + middle[1])
        return even, (middle[0] - middle[1]) - product(3)

    @pl.loop(0, 2)
    def _(step):
        base = step * 6
        both = conv(base, 7, tile_a, wa_w)
        for parity in range(2):
            for w in range(7):
                k = base + w
                part = both[parity][64 * w : 64 * (w + 1)]
                x = xf[3 * k + 2, pl.ds(parity, 64, 2)]
                hb[parity, 3 * k + 2] = (x + part[:, :128] + cbias[1]).astype(BF16)
                hp[parity, k + 1] = part[:, 128:]

    cut_right = jnp.where((lane >= 32) & (wa == n_wa - 1), 0.0, 1.0).astype(F32)

    @pl.loop(0, 2)
    def _(step):
        base = step * 7
        both = conv(base, 7, tile_b, wb_w)
        for parity in range(2):
            for w in range(7):
                i = base + w
                part = both[parity][64 * w : 64 * (w + 1)]
                x = xf[3 * i, pl.ds(parity, 64, 2)]
                hb[parity, 3 * i] = (x + part[:, :128] + hp[parity, i] + cbias[2]).astype(BF16)
                x = xf[3 * i + 1, pl.ds(parity, 64, 2)]
                h = x + part[:, 128:] + cbias[0]
                if w == 6:
                    h = h * jnp.where(i == 13, cut_right, 1.0)
                hb[parity, 3 * i + 1] = h.astype(BF16)

    def tile32_a(k, j):
        return 3 * k + j

    def tile32_b(i, j):
        return EXT + i if j == 0 else (41 if i == 0 and j == 1 else 3 * i + j - 2)

    def conv32(tile_of, weights):
        rows = []
        for w in range(14):
            pieces = [l32[tile_of(w, j), n] for n in range(9) for j in range(3)]
            rows.append(jnp.concatenate(pieces, axis=1))
        lhs = jnp.concatenate(rows, axis=0).astype(BF16)
        return jnp.dot(lhs, weights[pl.ds(0, KK * 128)], preferred_element_type=F32)

    acc = conv32(tile32_a, wa_w)
    for k in range(13):
        part = acc[8 * k : 8 * (k + 1)]
        h32[3 * k + 2] = (x32[3 * k + 2] + part[:, :128] + cbias[1]) * has_below
        hp32[k + 1] = part[:, 128:]
    acc = conv32(tile32_b, wb_w)
    for i in range(14):
        part = acc[8 * i : 8 * (i + 1)]
        if i:
            h = x32[3 * i] + part[:, :128] + hp32[i] + cbias[2]
            h32[3 * i] = h * has_below
        h = (x32[3 * i + 1] + part[:, 128:] + cbias[0]) * has_below
        h32[3 * i + 1] = h * cut_right if i == 13 else h

    rows = []
    for k in range(13):
        pieces = [hb[parity, 3 * k + j + 1] for parity in range(2) for j in range(4)]
        rows.append(jnp.concatenate(pieces, axis=1))
    main = jnp.dot(jnp.concatenate(rows, axis=0), down_w[...], preferred_element_type=F32)
    rows = [
        jnp.concatenate([h32[3 * min(k, 12) + j + 1] for j in range(4)], axis=1) for k in range(14)
    ]
    extra = jnp.dot(
        jnp.concatenate(rows, axis=0).astype(BF16),
        down_w[pl.ds(0, 512)],
        preferred_element_type=F32,
    )
    blocks = []
    for b in range(4):
        here = jnp.zeros((64, 128), F32)
        over = jnp.zeros((64, 128), F32)
        over32 = jnp.zeros((8, 128), F32)
        for j in range(4 if b < 3 else 1):
            k = 4 * b + j
            fits = (lane >= 32 * j) & (lane < 32 * (j + 1))
            part = main[64 * k : 64 * (k + 1)]
            turned = pltpu.roll(part, 32 * j, 1) if j else part
            here = jnp.where(fits, turned, here)
            turned = pltpu.roll(part, (32 * j + 96) % 128, 1) if j != 1 else part
            over = jnp.where(fits, turned, over)
            part = extra[8 * k : 8 * (k + 1)]
            turned = pltpu.roll(part, (32 * j + 96) % 128, 1) if j != 1 else part
            over32 = jnp.where(fits, turned, over32)
        for t in range(T):
            vs[t, pl.ds(0, 16)] = over[16 * t : 16 * (t + 1)]
            vs[t, pl.ds(16, 1)] = over32[t : t + 1]
        shifted = jnp.concatenate([vs[t, pl.ds(1, 16)] for t in range(T)], axis=0)
        blocks.append(here + shifted + lbias[...])
    latent = jnp.concatenate(blocks[:3] + [blocks[3][:, :32]], axis=1)
    frame_of = lax.broadcasted_iota(jnp.int32, (64, 1), 0)
    latent = jnp.where(frame_of < valid[0] * 16, latent, 0.0).astype(BF16)

    row = lax.broadcasted_iota(jnp.int32, (64, 64), 0)
    col = lax.broadcasted_iota(jnp.int32, (64, 64), 1)
    by_col = jnp.broadcast_to(owners[...], (64, 64))
    by_row = jnp.sum(jnp.where(row == col, by_col, 0), axis=1, keepdims=True)
    rank = jnp.sum(jnp.where((by_row == by_col) & (row < col), 1, 0), axis=0, keepdims=True)
    slot = owners[...] * 32 + rank
    slots = lax.broadcasted_iota(jnp.int32, (128, 64), 0)
    selector = jnp.where(slots == slot, 1.0, 0.0).astype(BF16)
    send[...] = jnp.dot(selector, latent, preferred_element_type=F32).astype(BF16)

    here = pl.ds(pl.multiple_of(ha * 32, 32), 32)
    copies = []
    for d in range(1, n_ha):
        target = lax.rem(ha + d, n_ha)
        copies.append(
            pltpu.make_async_remote_copy(
                src_ref=send.at[pl.ds(pl.multiple_of(target * 32, 32), 32)],
                dst_ref=received.at[here],
                send_sem=a2a_send.at[d - 1],
                recv_sem=a2a_recv.at[d - 1],
                device_id={"ha": target, "wa": wa},
                device_id_type=pl.DeviceIdType.MESH,
            )
        )
    for copy in copies:
        copy.start()
    received[here] = send[here]
    for copy in row_copies + col_copies:
        copy.wait_send()
    for copy in copies:
        copy.wait()
    full = jnp.concatenate([received[...].astype(F32), jnp.zeros((128, 96), F32)], axis=1)
    out[0, 0, 0] = full.T[:416].astype(BF16)


def per_device(
    n_ha,
    n_wa,
    frames,
    cache,
    norm_gain,
    conv_weight,
    conv_bias,
    down_weight,
    down_bias,
    latent_weight,
    latent_bias,
    valid_frames,
    owners,
):
    vmem = pl.BlockSpec(memory_space=pltpu.VMEM)
    hbm = pl.BlockSpec(memory_space=pltpu.HBM)
    routed = pl.pallas_call(
        functools.partial(kernel, n_ha, n_wa),
        out_shape=jax.ShapeDtypeStruct((1, 1, 1, 416, 128), BF16),
        in_specs=[hbm, hbm, vmem, pl.BlockSpec(memory_space=pltpu.SMEM), vmem, hbm, vmem, hbm]
        + [vmem] * 3,
        out_specs=vmem,
        scratch_shapes=[
            pltpu.VMEM((6, TH, EXT * 128), BF16),
            pltpu.VMEM((16, OWN * 128), BF16),
            pltpu.VMEM((16, OWN * 128), BF16),
            pltpu.VMEM((16, EXT * 128), BF16),
            pltpu.VMEM((16, EXT * 128), BF16),
            pltpu.VMEM((EXT, 6 * FS, 128), F32),
            pltpu.VMEM((41, T * TH, 128), F32),
            pltpu.VMEM((4, EXT + 15, 96, 128), BF16),
            pltpu.VMEM((384, 384), BF16),
            pltpu.VMEM((2, 448, 256), F32),
            pltpu.VMEM((2, 14, 64, 128), F32),
            pltpu.VMEM((2, 41, 64, 128), BF16),
            pltpu.VMEM((EXT + 14, 9, 8, 128), F32),
            pltpu.VMEM((EXT + 1, 8, 128), F32),
            pltpu.VMEM((14, 8, 128), F32),
            pltpu.VMEM((41, 8, 128), F32),
            pltpu.VMEM((T, 24, 128), F32),
            pltpu.VMEM((27, C * C), BF16),
            pltpu.VMEM((9, C * C), BF16),
            pltpu.VMEM((36 * C, 128), F32),
            pltpu.VMEM((4608, 256), BF16),
            pltpu.VMEM((4608, 256), BF16),
            pltpu.VMEM((1024, 128), BF16),
            pltpu.VMEM((1, 384), F32),
            pltpu.VMEM((3, 1, 128), F32),
            pltpu.VMEM((1, 128), F32),
            pltpu.VMEM((128, 416), BF16),
            pltpu.VMEM((128, 416), BF16),
            pltpu.SemaphoreType.DMA((4,)),
            pltpu.SemaphoreType.DMA((10,)),
            pltpu.SemaphoreType.DMA((10,)),
            pltpu.SemaphoreType.DMA((n_ha - 1,)),
            pltpu.SemaphoreType.DMA((n_ha - 1,)),
        ],
        compiler_params=pltpu.CompilerParams(
            collective_id=0, has_side_effects=True, vmem_limit_bytes=56 * 2**20
        ),
        name="encoder_step",
    )(
        frames,
        cache,
        owners.reshape(1, 64),
        valid_frames,
        norm_gain.reshape(1, C),
        conv_weight,
        conv_bias.reshape(1, C),
        down_weight,
        down_bias.reshape(1, C),
        latent_weight.T,
        latent_bias.reshape(1, Z),
    )
    return jnp.swapaxes(routed, 3, 4)


def solution(mesh):
    in_specs = (
        P("ba", None, "ha", "wa"),
        P("ba", None, "ha", "wa"),
        P(),
        P(),
        P(),
        P(),
        P(),
        P(),
        P(),
        P("ba"),
        P("ba", "ha", "wa", None, None),
    )
    out_specs = P("ba", "ha", "wa", None, None)
    return jax.shard_map(
        functools.partial(per_device, mesh.shape["ha"], mesh.shape["wa"]),
        mesh=mesh,
        in_specs=in_specs,
        out_specs=out_specs,
        check_vma=False,
    )
```

```python
import functools

import jax
import jax.numpy as jnp
import numpy as np
from jax import lax
from jax.experimental import pallas as pl
from jax.experimental.pallas import tpu as pltpu
from jax.sharding import PartitionSpec as P

EPS = 1e-06
C = 96
Z = 16
T = 4
TH = 32
TW = 52
OWN = 39
EXT = 42
FS = 48
KK = 27
QB = 8
F32 = jnp.float32
BF16 = jnp.bfloat16


def lanes(tile, count=1):
    return pl.ds(pl.multiple_of(tile * 128, 128), count * 128)


def kernel(
    n_ha,
    n_wa,
    frames,
    cache,
    owners,
    valid,
    norm_gain,
    conv_weight,
    conv_bias,
    down_weight,
    down_bias,
    latent_weight,
    latent_bias,
    out,
    ext,
    pack_top,
    pack_bot,
    above,
    below,
    act,
    xf,
    inner,
    outer,
    ones,
    middle,
    hp,
    hb,
    l32,
    x32,
    hp32,
    h32,
    vs,
    conv_taps,
    down_taps,
    taps,
    wa_w,
    wb_w,
    down_w,
    gain,
    cbias,
    lbias,
    send,
    received,
    local_sem,
    send_sem,
    recv_sem,
    a2a_send,
    a2a_recv,
):
    ha, wa = lax.axis_index("ha"), lax.axis_index("wa")
    up, down = lax.rem(ha + n_ha - 1, n_ha), lax.rem(ha + 1, n_ha)
    left, right = lax.rem(wa + n_wa - 1, n_wa), lax.rem(wa + 1, n_wa)

    load_cache = pltpu.make_async_copy(
        cache.at[0], ext.at[pl.ds(0, 2), :, pl.ds(0, OWN * 128)], local_sem.at[0]
    )
    load_frames = pltpu.make_async_copy(
        frames.at[0], ext.at[pl.ds(2, T), :, pl.ds(0, OWN * 128)], local_sem.at[1]
    )
    load_conv = pltpu.make_async_copy(conv_weight, conv_taps, local_sem.at[2])
    load_down = pltpu.make_async_copy(down_weight, down_taps, local_sem.at[3])
    loads = [load_cache, load_frames, load_conv, load_down]
    for load in loads:
        load.start()

    barrier = pltpu.get_barrier_semaphore()
    greeted = [
        {"ha": up, "wa": wa},
        {"ha": down, "wa": wa},
        {"ha": ha, "wa": left},
        {"ha": ha, "wa": right},
        {"ha": up, "wa": left},
        {"ha": up, "wa": right},
        {"ha": down, "wa": left},
        {"ha": down, "wa": right},
        {"ha": lax.rem(ha + 2, n_ha), "wa": wa},
    ]
    for device in greeted:
        pl.semaphore_signal(
            barrier, inc=1, device_id=device, device_id_type=pl.DeviceIdType.MESH
        )

    def remote(src, dst, index, device):
        return pltpu.make_async_remote_copy(
            src_ref=src,
            dst_ref=dst,
            send_sem=send_sem.at[index],
            recv_sem=recv_sem.at[index],
            device_id=device,
            device_id_type=pl.DeviceIdType.MESH,
        )

    load_cache.wait()
    load_frames.wait()

    sub = lax.broadcasted_iota(jnp.int32, (8, 384), 0)

    @pl.loop(0, OWN // 3, unroll=True)
    def _(g):
        win = lanes(3 * g, 3)
        tops = [ext[f, pl.ds(0, 16), win].astype(F32) for f in range(6)]
        bots = [ext[f, pl.ds(16, 16), win].astype(F32) for f in range(6)]
        lo = jnp.zeros((8, 384), F32)
        hi = jnp.zeros((8, 384), F32)
        for t in range(T):
            lo = jnp.where(sub == t, tops[2 + t][0:1], lo)
            lo = jnp.where(sub == 4 + t, tops[2 + t][1:2], lo)
        for t in range(2):
            hi = jnp.where(sub == t, tops[t][0:1], hi)
            hi = jnp.where(sub == 2 + t, tops[t][1:2], hi)
        pack_top[:, win] = jnp.concatenate([lo, hi], axis=0).astype(BF16)
        lo = jnp.zeros((8, 384), F32)
        for t in range(T):
            lo = jnp.where(sub == t, bots[2 + t][15:16], lo)
        for t in range(2):
            lo = jnp.where(sub == 4 + t, bots[t][15:16], lo)
        pack_bot[:, win] = jnp.concatenate([lo, jnp.zeros((8, 384), F32)], axis=0).astype(BF16)

    pl.semaphore_wait(barrier, len(greeted))

    own = pl.ds(0, OWN * 128)
    first, last = pl.ds(0, 256), pl.ds((OWN - 1) * 128, 128)
    from_right, from_left = pl.ds(OWN * 128, 256), pl.ds((OWN + 2) * 128, 128)
    row_copies = [
        remote(pack_top, below.at[:, own], 0, {"ha": up, "wa": wa}),
        remote(pack_bot, above.at[:, own], 1, {"ha": down, "wa": wa}),
        remote(pack_top.at[:, first], below.at[:, from_right], 2, {"ha": up, "wa": left}),
        remote(pack_top.at[:, last], below.at[:, from_left], 3, {"ha": up, "wa": right}),
        remote(pack_bot.at[:, first], above.at[:, from_right], 4, {"ha": down, "wa": left}),
        remote(pack_bot.at[:, last], above.at[:, from_left], 5, {"ha": down, "wa": right}),
    ]
    col_copies = [
        remote(
            frames.at[0, :, :, first],
            ext.at[pl.ds(2, T), :, from_right],
            6,
            {"ha": ha, "wa": left},
        ),
        remote(
            cache.at[0, :, :, first],
            ext.at[pl.ds(0, 2), :, from_right],
            7,
            {"ha": ha, "wa": left},
        ),
        remote(
            frames.at[0, :, :, last],
            ext.at[pl.ds(2, T), :, from_left],
            8,
            {"ha": ha, "wa": right},
        ),
        remote(
            cache.at[0, :, :, last],
            ext.at[pl.ds(0, 2), :, from_left],
            9,
            {"ha": ha, "wa": right},
        ),
    ]
    for copy in row_copies + col_copies:
        copy.start()

    lane = lax.broadcasted_iota(jnp.int32, (1, 128), 1)

    gain[...] = jnp.concatenate([norm_gain[...]] * 4, axis=1) * (0.5 * C**0.5)

    load_conv.wait()
    load_down.wait()

    @pl.loop(0, C // 4, unroll=4)
    def _(g):
        win = lanes(3 * g, 3)
        for weight, count, at in ((conv_taps, 27, 0), (down_taps, 9, 27)):
            x = weight[:, win].astype(F32)
            t0, t1, t2 = (x[:, 128 * j : 128 * (j + 1)] for j in range(3))
            parts = [
                t0,
                jnp.where(lane < 32, pltpu.roll(t0, 32, 1), pltpu.roll(t1, 32, 1)),
                jnp.where(lane < 64, pltpu.roll(t1, 64, 1), pltpu.roll(t2, 64, 1)),
                pltpu.roll(t2, 96, 1),
            ]
            for u in range(4):
                taps[pl.ds(at * C + 4 * g + u, count, C)] = jnp.where(lane < C, parts[u], 0.0)

    @pl.loop(0, 3)
    def _(a):
        for m in range(4):
            w = []
            for s in range(3):
                g0, g1, g2 = (taps[pl.ds((9 * a + 3 * r + s) * C, C)] for r in range(3))
                if m == 0:
                    w.append(g0)
                elif m == 1:
                    w.append(0.5 * (g0 + g2 + g1))
                elif m == 2:
                    w.append(0.5 * (g0 + g2 - g1))
                else:
                    w.append(g2)
            zero = jnp.zeros((C, 128), F32)
            by96 = [zero] + [pltpu.roll(x, 96, 1) for x in w]
            by64 = [pltpu.roll(x, 64, 1) for x in w] + [zero]
            by32 = [zero] + [pltpu.roll(x, 32, 1) for x in w]
            w = w + [zero]
            at = m * 1152 + a * 384
            for s in range(4):
                rows = pl.ds(pl.multiple_of(at + s * 96, 32), C)
                wa_w[rows, pl.ds(0, 128)] = jnp.where(lane < 96, w[s], by96[s]).astype(BF16)
                wa_w[rows, pl.ds(128, 128)] = jnp.where(lane < 64, by96[s], 0.0).astype(BF16)
                one = jnp.where(lane < 64, 0.0, by64[s]).astype(BF16)
                two = jnp.where(lane < 32, by64[s], by32[s]).astype(BF16)
                if s < 3:
                    rows = pl.ds(pl.multiple_of(at + s * 96 + 64, 32), C)
                    wb_w[rows, pl.ds(0, 128)] = one
                    wb_w[rows, pl.ds(128, 128)] = two
                else:
                    rows = pl.ds(pl.multiple_of(at + 352, 32), 32)
                    wb_w[rows, pl.ds(0, 128)] = one[:32]
                    wb_w[rows, pl.ds(128, 128)] = two[:32]
                    rows = pl.ds(pl.multiple_of(at, 32), 64)
                    wb_w[rows, pl.ds(0, 128)] = one[32:]
                    wb_w[rows, pl.ds(128, 128)] = two[32:]

    by_z = jnp.concatenate([latent_weight[...]] * QB, axis=0)
    by_column = (((1,), (1,)), ((), ()))
    fused = lax.dot_general(
        taps[pl.ds(27 * C, 9 * C)][:, :C].astype(BF16),
        by_z,
        by_column,
        preferred_element_type=F32,
    )
    down_w[...] = jnp.zeros((1024, 128), BF16)
    for r in range(3):
        first = (0, 0, 2)[r]
        for col in range(5):
            block = jnp.zeros((C, 128), F32)
            for s in range(3):
                q = col - s
                if q in (0, 2):
                    tap = fused[(3 * r + s) * C : (3 * r + s + 1) * C]
                    place = first + q // 2
                    block = jnp.where((lane >= 16 * place) & (lane < 16 * (place + 1)), tap, block)
            rows = pl.ds((512 if r == 1 else 0) + 32 + C * col, C)
            if r == 2:
                block = block + down_w[rows].astype(F32)
            down_w[rows] = block.astype(BF16)

    rest = down_bias[...]
    pieces = []
    for _ in range(3):
        piece = rest.astype(BF16)
        pieces.append(piece.astype(F32))
        rest = rest - pieces[-1]
    pieces = jnp.concatenate(pieces + [jnp.zeros((13, C), F32)], axis=0).astype(BF16)
    lbias_row = jnp.sum(
        lax.dot_general(pieces, by_z, by_column, preferred_element_type=F32),
        axis=0,
        keepdims=True,
    ) + jnp.concatenate([latent_bias[...]] * QB, axis=1)

    lbias[...] = lbias_row
    bias = conv_bias[...]
    bias = jnp.concatenate([bias[:, 64:]] + [bias] * 3 + [bias[:, :64]], axis=1)
    for j in range(3):
        cbias[j] = bias[:, 128 * j : 128 * (j + 1)]

    def column_of(axis):
        index = lax.broadcasted_iota(jnp.int32, (384, 384), axis)
        return sum((index >= edge).astype(jnp.int32) for edge in (96, 192, 288))

    ones[...] = jnp.where(column_of(0) == column_of(1), 1.0, 0.0).astype(BF16)

    has_left = jnp.where(wa == 0, 0.0, 1.0).astype(F32)
    has_right = jnp.where(wa == n_wa - 1, 0.0, 1.0).astype(F32)
    has_above = jnp.where(ha == 0, 0.0, 1.0).astype(F32)
    has_below = jnp.where(ha == n_ha - 1, 0.0, 1.0).astype(F32)

    def activate(x):
        squares = jnp.dot((x * x).astype(BF16), ones[...], preferred_element_type=F32)
        u = x * lax.rsqrt(squares + C * EPS) * gain[...]
        return u + u * jnp.tanh(u)

    def halo_mask(x):
        return jnp.concatenate([x[:, :256] * has_right, x[:, 256:] * has_left], axis=1)

    def groups(gs, edge):
        xs, earlier = [], []
        for g in gs:
            win = lanes(3 * g, 3)
            x = ext[pl.ds(2, T), :, win].reshape(T * TH, 384).astype(F32)
            old = ext[pl.ds(0, 2), :, win].reshape(2 * TH, 384).astype(F32)
            if edge and g == 13:
                x, old = halo_mask(x), halo_mask(old)
            xs.append(x)
            earlier.append(old)
        activated = activate(jnp.concatenate(xs, axis=0))
        for n, g in enumerate(gs):
            before = ext[pl.ds(2, T), :, lanes(jnp.maximum(3 * g - 1, 0))]
            before = pltpu.roll(before.reshape(T * TH, 128).astype(F32), 32, 1)
            for j in range(1 if edge and g == 13 else 3):
                here = pltpu.roll(xs[n][:, 128 * j : 128 * (j + 1)], 32, 1)
                xf[3 * g + j + 1] = jnp.where(lane < 32, before, here)
                before = here
            for j in range(3):
                part = slice(128 * j, 128 * (j + 1))
                tile = 3 * g + j
                for f in range(6):
                    if f < 2:
                        value = earlier[n][f * TH : (f + 1) * TH, part]
                    else:
                        at = n * T * TH + (f - 2) * TH
                        value = activated[at : at + TH, part]
                    act[tile, pl.ds(f * FS + 8, TH)] = value
                for f in range(6):
                    d1 = act[tile, pl.ds(f * FS + 8, 16, 2)]
                    d2 = act[tile, pl.ds(f * FS + 9, 16, 2)]
                    inner[0, tile + 1, pl.ds(f * 16, 16)] = (d1 + d2).astype(BF16)
                    inner[1, tile + 1, pl.ds(f * 16, 16)] = (d2 - d1).astype(BF16)

    @pl.loop(0, 4)
    def _(n):
        groups([3 * n, 3 * n + 1, 3 * n + 2], False)

    for copy in col_copies:
        copy.wait_recv()
    groups([12, 13], True)
    for copy in row_copies:
        copy.wait_recv()

    @pl.loop(0, 2)
    def _(half):
        his, los = [], []
        for n in range(7):
            g = 7 * half + n
            win = lanes(3 * g, 3)
            hi = below[:, win].astype(F32) * has_below
            lo = above[:, win].astype(F32) * has_above
            if n == 6:
                right_on = jnp.where(half == 1, has_right, 1.0)
                left_on = jnp.where(half == 1, has_left, 1.0)
                hi, lo = (
                    jnp.concatenate([x[:, :256] * right_on, x[:, 256:] * left_on], axis=1)
                    for x in (hi, lo)
                )
            his.append(hi)
            los.append(lo)
        activated = activate(
            jnp.concatenate([x[:8] for pair in zip(his, los) for x in pair], axis=0)
        )
        before = below[:, lanes(jnp.maximum(21 * half - 1, 0))].astype(F32) * has_below
        before = pltpu.roll(before[:8], 32, 1)
        for n in range(7):
            for j in range(3):
                part = slice(128 * j, 128 * (j + 1))
                tile = 21 * half + 3 * n + j
                new = activated[16 * n : 16 * (n + 1), part]
                act[tile, pl.ds(2 * FS + 40, T, FS)] = new[0:4]
                act[tile, pl.ds(2 * FS + 41, T, FS)] = new[4:8]
                act[tile, pl.ds(2 * FS + 7, T, FS)] = new[8:12]
                act[tile, pl.ds(40, 2, FS)] = his[n][8:10, part]
                act[tile, pl.ds(41, 2, FS)] = his[n][10:12, part]
                act[tile, pl.ds(7, 2, FS)] = los[n][4:6, part]
                here = pltpu.roll(his[n][:8, part], 32, 1)
                x32[tile + 1] = jnp.where(lane < 32, before, here)
                before = here

    def tile_a(k, j):
        return 3 * k + j + 1

    def tile_b(i, j):
        return EXT + 1 + i if j == 0 else 3 * i + j - 1

    def join(planes):
        @pl.loop(0, 2)
        def _(m):
            planes[m, 0] = planes[m, EXT]
            for i in range(14):
                later = planes[m, 3 * i + 2]
                sooner = planes[m, 41 if i == 0 else 3 * i - 1]
                planes[m, EXT + 1 + i] = jnp.where(lane < 64, later, sooner)

    def product(planes, m, at, base, tile_of, weights):
        rows = []
        for w in range(7):
            pieces = [
                planes[m, tile_of(base + w, j), pl.ds(a * 16, 64)]
                for a in range(3)
                for j in range(3)
            ]
            rows.append(jnp.concatenate(pieces, axis=1))
        return jnp.dot(
            jnp.concatenate(rows, axis=0),
            weights[pl.ds(at * 1152, 1152)],
            preferred_element_type=F32,
        )

    def outer_planes(tile):
        for f in range(6):
            d0, d1, d2, d3 = (act[tile, pl.ds(f * FS + 7 + r, 16, 2)] for r in range(4))
            outer[0, tile + 1, pl.ds(f * 16, 16)] = (d0 - d2).astype(BF16)
            outer[1, tile + 1, pl.ds(f * 16, 16)] = (d1 - d3).astype(BF16)

        for a in range(3):
            d0, d1, d2 = (act[tile, pl.ds(a * FS + 39 + r, T, FS)] for r in range(3))
            l32[tile, a, pl.ds(0, T)] = d0 - d2
            l32[tile, 3 + a, pl.ds(0, T)] = d1 + d2
            l32[tile, 6 + a, pl.ds(0, T)] = d2 - d1

    join(inner)

    @pl.loop(0, 2)
    def _(step):
        for n in range(21):
            outer_planes(21 * step + n)
        for m in range(2):
            middle[step, 0, m] = product(inner, m, 1 + m, 6 * step, tile_a, wa_w)
            middle[step, 1, m] = product(inner, m, 1 + m, 7 * step, tile_b, wb_w)

    join(outer)
    cut_right = jnp.where((lane >= 32) & (wa == n_wa - 1), 0.0, 1.0).astype(F32)

    def both_rows(step, side, base, tile_of, weights):
        one, two = middle[step, side, 0], middle[step, side, 1]
        even = product(outer, 0, 0, base, tile_of, weights) + (one + two)
        return even, (one - two) - product(outer, 1, 3, base, tile_of, weights)

    @pl.loop(0, 2)
    def _(step):
        base = step * 6
        both = both_rows(step, 0, base, tile_a, wa_w)
        for parity in range(2):
            for w in range(7):
                k = base + w
                part = both[parity][64 * w : 64 * (w + 1)]
                x = xf[3 * k + 2, pl.ds(parity, 64, 2)]
                hb[parity, 3 * k + 2] = (x + part[:, :128] + cbias[1]).astype(BF16)
                hp[parity, k + 1] = part[:, 128:]
        base = step * 7
        both = both_rows(step, 1, base, tile_b, wb_w)
        for parity in range(2):
            for w in range(7):
                i = base + w
                part = both[parity][64 * w : 64 * (w + 1)]
                x = xf[3 * i, pl.ds(parity, 64, 2)]
                hb[parity, 3 * i] = (x + part[:, :128] + hp[parity, i] + cbias[2]).astype(BF16)
                x = xf[3 * i + 1, pl.ds(parity, 64, 2)]
                h = x + part[:, 128:] + cbias[0]
                if w == 6:
                    h = h * jnp.where(i == 13, cut_right, 1.0)
                hb[parity, 3 * i + 1] = h.astype(BF16)

    for i in range(14):
        sooner = 40 if i == 0 else 3 * i - 2
        for n in range(9):
            l32[EXT + i, n] = jnp.where(lane < 64, l32[3 * i + 1, n], l32[sooner, n])

    def tile32_a(k, j):
        return 3 * k + j

    def tile32_b(i, j):
        return EXT + i if j == 0 else (41 if i == 0 and j == 1 else 3 * i + j - 2)

    def conv32(tile_of, weights):
        rows = []
        for w in range(14):
            pieces = [l32[tile_of(w, j), n] for n in range(9) for j in range(3)]
            rows.append(jnp.concatenate(pieces, axis=1))
        lhs = jnp.concatenate(rows, axis=0).astype(BF16)
        return jnp.dot(lhs, weights[pl.ds(0, KK * 128)], preferred_element_type=F32)

    acc = conv32(tile32_a, wa_w)
    for k in range(13):
        part = acc[8 * k : 8 * (k + 1)]
        h32[3 * k + 2] = (x32[3 * k + 2] + part[:, :128] + cbias[1]) * has_below
        hp32[k + 1] = part[:, 128:]
    acc = conv32(tile32_b, wb_w)
    for i in range(14):
        part = acc[8 * i : 8 * (i + 1)]
        if i:
            h = x32[3 * i] + part[:, :128] + hp32[i] + cbias[2]
            h32[3 * i] = h * has_below
        h = (x32[3 * i + 1] + part[:, 128:] + cbias[0]) * has_below
        h32[3 * i + 1] = h * cut_right if i == 13 else h

    rows = []
    for k in range(13):
        pieces = [hb[parity, 3 * k + j + 1] for parity in range(2) for j in range(4)]
        rows.append(jnp.concatenate(pieces, axis=1))
    main = jnp.dot(jnp.concatenate(rows, axis=0), down_w[...], preferred_element_type=F32)
    rows = [
        jnp.concatenate([h32[3 * min(k, 12) + j + 1] for j in range(4)], axis=1) for k in range(14)
    ]
    extra = jnp.dot(
        jnp.concatenate(rows, axis=0).astype(BF16),
        down_w[pl.ds(0, 512)],
        preferred_element_type=F32,
    )
    blocks = []
    for b in range(4):
        here = jnp.zeros((64, 128), F32)
        over = jnp.zeros((64, 128), F32)
        over32 = jnp.zeros((8, 128), F32)
        for j in range(4 if b < 3 else 1):
            k = 4 * b + j
            fits = (lane >= 32 * j) & (lane < 32 * (j + 1))
            part = main[64 * k : 64 * (k + 1)]
            turned = pltpu.roll(part, 32 * j, 1) if j else part
            here = jnp.where(fits, turned, here)
            turned = pltpu.roll(part, (32 * j + 96) % 128, 1) if j != 1 else part
            over = jnp.where(fits, turned, over)
            part = extra[8 * k : 8 * (k + 1)]
            turned = pltpu.roll(part, (32 * j + 96) % 128, 1) if j != 1 else part
            over32 = jnp.where(fits, turned, over32)
        for t in range(T):
            vs[t, pl.ds(0, 16)] = over[16 * t : 16 * (t + 1)]
            vs[t, pl.ds(16, 1)] = over32[t : t + 1]
        shifted = jnp.concatenate([vs[t, pl.ds(1, 16)] for t in range(T)], axis=0)
        blocks.append(here + shifted + lbias[...])
    latent = jnp.concatenate(blocks[:3] + [blocks[3][:, :32]], axis=1)
    frame_of = lax.broadcasted_iota(jnp.int32, (64, 1), 0)
    latent = jnp.where(frame_of < valid[0] * 16, latent, 0.0).astype(BF16)

    row = lax.broadcasted_iota(jnp.int32, (64, 64), 0)
    col = lax.broadcasted_iota(jnp.int32, (64, 64), 1)
    by_col = jnp.broadcast_to(owners[...], (64, 64))
    by_row = jnp.sum(jnp.where(row == col, by_col, 0), axis=1, keepdims=True)
    rank = jnp.sum(jnp.where((by_row == by_col) & (row < col), 1, 0), axis=0, keepdims=True)
    slot = owners[...] * 32 + rank
    slots = lax.broadcasted_iota(jnp.int32, (128, 64), 0)
    selector = jnp.where(slots == slot, 1.0, 0.0).astype(BF16)
    send[...] = jnp.dot(selector, latent, preferred_element_type=F32).astype(BF16)

    here = pl.ds(pl.multiple_of(ha * 32, 32), 32)
    copies = []
    for d in range(1, n_ha):
        target = lax.rem(ha + d, n_ha)
        copies.append(
            pltpu.make_async_remote_copy(
                src_ref=send.at[pl.ds(pl.multiple_of(target * 32, 32), 32)],
                dst_ref=received.at[here],
                send_sem=a2a_send.at[d - 1],
                recv_sem=a2a_recv.at[d - 1],
                device_id={"ha": target, "wa": wa},
                device_id_type=pl.DeviceIdType.MESH,
            )
        )
    for copy in copies:
        copy.start()
    received[here] = send[here]
    for copy in row_copies + col_copies:
        copy.wait_send()
    for copy in copies:
        copy.wait()
    full = jnp.concatenate([received[...].astype(F32), jnp.zeros((128, 96), F32)], axis=1)
    out[0, 0, 0] = full.T[:416].astype(BF16)


def per_device(
    n_ha,
    n_wa,
    frames,
    cache,
    norm_gain,
    conv_weight,
    conv_bias,
    down_weight,
    down_bias,
    latent_weight,
    latent_bias,
    valid_frames,
    owners,
):
    vmem = pl.BlockSpec(memory_space=pltpu.VMEM)
    hbm = pl.BlockSpec(memory_space=pltpu.HBM)
    routed = pl.pallas_call(
        functools.partial(kernel, n_ha, n_wa),
        out_shape=jax.ShapeDtypeStruct((1, 1, 1, 416, 128), BF16),
        in_specs=[hbm, hbm, vmem, pl.BlockSpec(memory_space=pltpu.SMEM), vmem, hbm, vmem, hbm]
        + [vmem] * 3,
        out_specs=vmem,
        scratch_shapes=[
            pltpu.VMEM((6, TH, EXT * 128), BF16),
            pltpu.VMEM((16, OWN * 128), BF16),
            pltpu.VMEM((16, OWN * 128), BF16),
            pltpu.VMEM((16, EXT * 128), BF16),
            pltpu.VMEM((16, EXT * 128), BF16),
            pltpu.VMEM((EXT, 6 * FS, 128), F32),
            pltpu.VMEM((41, T * TH, 128), F32),
            pltpu.VMEM((2, EXT + 15, 96, 128), BF16),
            pltpu.VMEM((2, EXT + 15, 96, 128), BF16),
            pltpu.VMEM((384, 384), BF16),
            pltpu.VMEM((2, 2, 2, 448, 256), F32),
            pltpu.VMEM((2, 14, 64, 128), F32),
            pltpu.VMEM((2, 41, 64, 128), BF16),
            pltpu.VMEM((EXT + 14, 9, 8, 128), F32),
            pltpu.VMEM((EXT + 1, 8, 128), F32),
            pltpu.VMEM((14, 8, 128), F32),
            pltpu.VMEM((41, 8, 128), F32),
            pltpu.VMEM((T, 24, 128), F32),
            pltpu.VMEM((27, C * C), BF16),
            pltpu.VMEM((9, C * C), BF16),
            pltpu.VMEM((36 * C, 128), F32),
            pltpu.VMEM((4608, 256), BF16),
            pltpu.VMEM((4608, 256), BF16),
            pltpu.VMEM((1024, 128), BF16),
            pltpu.VMEM((1, 384), F32),
            pltpu.VMEM((3, 1, 128), F32),
            pltpu.VMEM((1, 128), F32),
            pltpu.VMEM((128, 416), BF16),
            pltpu.VMEM((128, 416), BF16),
            pltpu.SemaphoreType.DMA((4,)),
            pltpu.SemaphoreType.DMA((10,)),
            pltpu.SemaphoreType.DMA((10,)),
            pltpu.SemaphoreType.DMA((n_ha - 1,)),
            pltpu.SemaphoreType.DMA((n_ha - 1,)),
        ],
        compiler_params=pltpu.CompilerParams(
            collective_id=0, has_side_effects=True, vmem_limit_bytes=56 * 2**20
        ),
        name="encoder_step",
    )(
        frames,
        cache,
        owners.reshape(1, 64),
        valid_frames,
        norm_gain.reshape(1, C),
        conv_weight,
        conv_bias.reshape(1, C),
        down_weight,
        down_bias.reshape(1, C),
        latent_weight.T,
        latent_bias.reshape(1, Z),
    )
    return jnp.swapaxes(routed, 3, 4)


def solution(mesh):
    in_specs = (
        P("ba", None, "ha", "wa"),
        P("ba", None, "ha", "wa"),
        P(),
        P(),
        P(),
        P(),
        P(),
        P(),
        P(),
        P("ba"),
        P("ba", "ha", "wa", None, None),
    )
    out_specs = P("ba", "ha", "wa", None, None)
    return jax.shard_map(
        functools.partial(per_device, mesh.shape["ha"], mesh.shape["wa"]),
        mesh=mesh,
        in_specs=in_specs,
        out_specs=out_specs,
        check_vma=False,
    )
```

```python
import functools

import jax
import jax.numpy as jnp
import numpy as np
from jax import lax
from jax.experimental import pallas as pl
from jax.experimental.pallas import tpu as pltpu
from jax.sharding import PartitionSpec as P

EPS = 1e-06
C = 96
Z = 16
T = 4
TH = 32
TW = 52
OWN = 39
EXT = 42
KK = 27
QB = 8
F32 = jnp.float32
BF16 = jnp.bfloat16


def lanes(tile, count=1):
    return pl.ds(pl.multiple_of(tile * 128, 128), count * 128)


def kernel(
    n_ha,
    n_wa,
    frames,
    cache,
    owners,
    valid,
    norm_gain,
    conv_weight,
    conv_bias,
    down_weight,
    down_bias,
    latent_weight,
    latent_bias,
    mixer,
    out,
    ext,
    pack_top,
    pack_bot,
    above,
    below,
    stacked,
    xf,
    planes,
    ones,
    middle,
    hp,
    hb,
    l32,
    x32,
    hp32,
    h32,
    vs,
    conv_taps,
    down_taps,
    swap_conv,
    swap_down,
    taps,
    wa_w,
    wb_w,
    down_w,
    gain,
    cbias,
    lbias,
    send,
    received,
    local_sem,
    send_sem,
    recv_sem,
    a2a_send,
    a2a_recv,
):
    ha, wa = lax.axis_index("ha"), lax.axis_index("wa")
    up, down = lax.rem(ha + n_ha - 1, n_ha), lax.rem(ha + 1, n_ha)
    left, right = lax.rem(wa + n_wa - 1, n_wa), lax.rem(wa + 1, n_wa)

    load_cache = pltpu.make_async_copy(
        cache.at[0], ext.at[pl.ds(0, 2), :, pl.ds(0, OWN * 128)], local_sem.at[0]
    )
    load_frames = pltpu.make_async_copy(
        frames.at[0], ext.at[pl.ds(2, T), :, pl.ds(0, OWN * 128)], local_sem.at[1]
    )
    load_conv = pltpu.make_async_copy(conv_weight, conv_taps, local_sem.at[2])
    load_down = pltpu.make_async_copy(down_weight, down_taps, local_sem.at[3])
    loads = [load_cache, load_frames, load_conv, load_down]
    for load in loads:
        load.start()

    barrier = pltpu.get_barrier_semaphore()
    greeted = [
        {"ha": up, "wa": wa},
        {"ha": down, "wa": wa},
        {"ha": ha, "wa": left},
        {"ha": ha, "wa": right},
        {"ha": up, "wa": left},
        {"ha": up, "wa": right},
        {"ha": down, "wa": left},
        {"ha": down, "wa": right},
        {"ha": lax.rem(ha + 2, n_ha), "wa": wa},
    ]
    for device in greeted:
        pl.semaphore_signal(
            barrier, inc=1, device_id=device, device_id_type=pl.DeviceIdType.MESH
        )

    def remote(src, dst, index, device):
        return pltpu.make_async_remote_copy(
            src_ref=src,
            dst_ref=dst,
            send_sem=send_sem.at[index],
            recv_sem=recv_sem.at[index],
            device_id=device,
            device_id_type=pl.DeviceIdType.MESH,
        )

    load_cache.wait()
    load_frames.wait()

    sub = lax.broadcasted_iota(jnp.int32, (8, 384), 0)

    @pl.loop(0, OWN // 3, unroll=True)
    def _(g):
        win = lanes(3 * g, 3)
        tops = [ext[f, pl.ds(0, 16), win].astype(F32) for f in range(6)]
        bots = [ext[f, pl.ds(16, 16), win].astype(F32) for f in range(6)]
        lo = jnp.zeros((8, 384), F32)
        hi = jnp.zeros((8, 384), F32)
        for t in range(T):
            lo = jnp.where(sub == t, tops[2 + t][0:1], lo)
            lo = jnp.where(sub == 4 + t, tops[2 + t][1:2], lo)
        for t in range(2):
            hi = jnp.where(sub == t, tops[t][0:1], hi)
            hi = jnp.where(sub == 2 + t, tops[t][1:2], hi)
        pack_top[:, win] = jnp.concatenate([lo, hi], axis=0).astype(BF16)
        lo = jnp.zeros((8, 384), F32)
        for t in range(T):
            lo = jnp.where(sub == t, bots[2 + t][15:16], lo)
        for t in range(2):
            lo = jnp.where(sub == 4 + t, bots[t][15:16], lo)
        pack_bot[:, win] = jnp.concatenate([lo, jnp.zeros((8, 384), F32)], axis=0).astype(BF16)

    pl.semaphore_wait(barrier, len(greeted))

    own = pl.ds(0, OWN * 128)
    first, last = pl.ds(0, 256), pl.ds((OWN - 1) * 128, 128)
    from_right, from_left = pl.ds(OWN * 128, 256), pl.ds((OWN + 2) * 128, 128)
    row_copies = [
        remote(pack_top, below.at[:, own], 0, {"ha": up, "wa": wa}),
        remote(pack_bot, above.at[:, own], 1, {"ha": down, "wa": wa}),
        remote(pack_top.at[:, first], below.at[:, from_right], 2, {"ha": up, "wa": left}),
        remote(pack_top.at[:, last], below.at[:, from_left], 3, {"ha": up, "wa": right}),
        remote(pack_bot.at[:, first], above.at[:, from_right], 4, {"ha": down, "wa": left}),
        remote(pack_bot.at[:, last], above.at[:, from_left], 5, {"ha": down, "wa": right}),
    ]
    col_copies = [
        remote(
            frames.at[0, :, :, first],
            ext.at[pl.ds(2, T), :, from_right],
            6,
            {"ha": ha, "wa": left},
        ),
        remote(
            cache.at[0, :, :, first],
            ext.at[pl.ds(0, 2), :, from_right],
            7,
            {"ha": ha, "wa": left},
        ),
        remote(
            frames.at[0, :, :, last],
            ext.at[pl.ds(2, T), :, from_left],
            8,
            {"ha": ha, "wa": right},
        ),
        remote(
            cache.at[0, :, :, last],
            ext.at[pl.ds(0, 2), :, from_left],
            9,
            {"ha": ha, "wa": right},
        ),
    ]
    for copy in row_copies + col_copies:
        copy.start()

    lane = lax.broadcasted_iota(jnp.int32, (1, 128), 1)

    gain[...] = jnp.concatenate([norm_gain[...]] * 4, axis=1) * (0.5 * C**0.5)

    load_conv.wait()
    load_down.wait()

    def swap(taps_log, count_log):
        row = lax.broadcasted_iota(jnp.int32, (256, 256), 0)
        col = lax.broadcasted_iota(jnp.int32, (256, 256), 1)
        source = ((row & ((1 << count_log) - 1)) << taps_log) + (row >> count_log)
        return jnp.where(col == source, 1.0, 0.0).astype(BF16)

    swap_conv[...] = swap(5, 3)
    swap_down[...] = swap(4, 4)

    def channels(weight, count, rows, tile):
        x = weight[:, lanes(tile, 3)].astype(F32)
        x = jnp.concatenate([x, jnp.zeros((rows - count, 384), F32)], axis=0)
        t0, t1, t2 = (x[:, 128 * j : 128 * (j + 1)] for j in range(3))
        parts = [
            t0,
            jnp.where(lane < 32, pltpu.roll(t0, 32, 1), pltpu.roll(t1, 32, 1)),
            jnp.where(lane < 64, pltpu.roll(t1, 64, 1), pltpu.roll(t2, 64, 1)),
            pltpu.roll(t2, 96, 1),
        ]
        return [jnp.where(lane < C, part, 0.0) for part in parts]

    @pl.loop(0, 6)
    def _(n):
        parts = [x for g in range(4) for x in channels(conv_taps, 27, 32, 12 * n + 3 * g)]
        pair = [jnp.concatenate(parts[8 * b : 8 * (b + 1)], axis=0) for b in range(2)]
        swapped = jnp.dot(
            swap_conv[...],
            jnp.concatenate(pair, axis=1).astype(BF16),
            preferred_element_type=F32,
        )
        for tap in range(27):
            for b in range(2):
                at = pl.multiple_of(tap * C + 16 * n + 8 * b, 8)
                taps[pl.ds(at, 8)] = swapped[8 * tap : 8 * (tap + 1), 128 * b : 128 * (b + 1)]
        parts = [x for g in range(4) for x in channels(down_taps, 9, 16, 12 * n + 3 * g)]
        swapped = jnp.dot(
            swap_down[...],
            jnp.concatenate(parts, axis=0).astype(BF16),
            preferred_element_type=F32,
        )
        for tap in range(9):
            at = pl.multiple_of((27 + tap) * C + 16 * n, 8)
            taps[pl.ds(at, 16)] = swapped[16 * tap : 16 * (tap + 1)]

    @pl.loop(0, 3)
    def _(a):
        for m in range(4):
            w = []
            for s in range(3):
                g0, g1, g2 = (taps[pl.ds((9 * a + 3 * r + s) * C, C)] for r in range(3))
                if m == 0:
                    w.append(g0)
                elif m == 1:
                    w.append(0.5 * (g0 + g2 + g1))
                elif m == 2:
                    w.append(0.5 * (g0 + g2 - g1))
                else:
                    w.append(g2)
            zero = jnp.zeros((C, 128), F32)
            by96 = [zero] + [pltpu.roll(x, 96, 1) for x in w]
            by64 = [pltpu.roll(x, 64, 1) for x in w] + [zero]
            by32 = [zero] + [pltpu.roll(x, 32, 1) for x in w]
            w = w + [zero]
            at = m * 1152 + a * 384
            for s in range(4):
                rows = pl.ds(pl.multiple_of(at + s * 96, 32), C)
                wa_w[rows, pl.ds(0, 128)] = jnp.where(lane < 96, w[s], by96[s]).astype(BF16)
                wa_w[rows, pl.ds(128, 128)] = jnp.where(lane < 64, by96[s], 0.0).astype(BF16)
                one = jnp.where(lane < 64, 0.0, by64[s]).astype(BF16)
                two = jnp.where(lane < 32, by64[s], by32[s]).astype(BF16)
                if s < 3:
                    rows = pl.ds(pl.multiple_of(at + s * 96 + 64, 32), C)
                    wb_w[rows, pl.ds(0, 128)] = one
                    wb_w[rows, pl.ds(128, 128)] = two
                else:
                    rows = pl.ds(pl.multiple_of(at + 352, 32), 32)
                    wb_w[rows, pl.ds(0, 128)] = one[:32]
                    wb_w[rows, pl.ds(128, 128)] = two[:32]
                    rows = pl.ds(pl.multiple_of(at, 32), 64)
                    wb_w[rows, pl.ds(0, 128)] = one[32:]
                    wb_w[rows, pl.ds(128, 128)] = two[32:]

    by_z = jnp.concatenate([latent_weight[...]] * QB, axis=0)
    by_column = (((1,), (1,)), ((), ()))
    fused = lax.dot_general(
        taps[pl.ds(27 * C, 9 * C)][:, :C].astype(BF16),
        by_z,
        by_column,
        preferred_element_type=F32,
    )
    down_w[...] = jnp.zeros((1024, 128), BF16)
    for r in range(3):
        first = (0, 0, 2)[r]
        for col in range(5):
            block = jnp.zeros((C, 128), F32)
            for s in range(3):
                q = col - s
                if q in (0, 2):
                    tap = fused[(3 * r + s) * C : (3 * r + s + 1) * C]
                    place = first + q // 2
                    block = jnp.where((lane >= 16 * place) & (lane < 16 * (place + 1)), tap, block)
            rows = pl.ds((512 if r == 1 else 0) + 32 + C * col, C)
            if r == 2:
                block = block + down_w[rows].astype(F32)
            down_w[rows] = block.astype(BF16)

    rest = down_bias[...]
    pieces = []
    for _ in range(3):
        piece = rest.astype(BF16)
        pieces.append(piece.astype(F32))
        rest = rest - pieces[-1]
    pieces = jnp.concatenate(pieces + [jnp.zeros((13, C), F32)], axis=0).astype(BF16)
    lbias_row = jnp.sum(
        lax.dot_general(pieces, by_z, by_column, preferred_element_type=F32),
        axis=0,
        keepdims=True,
    ) + jnp.concatenate([latent_bias[...]] * QB, axis=1)

    lbias[...] = lbias_row
    bias = conv_bias[...]
    bias = jnp.concatenate([bias[:, 64:]] + [bias] * 3 + [bias[:, :64]], axis=1)
    for j in range(3):
        cbias[j] = bias[:, 128 * j : 128 * (j + 1)]

    def column_of(axis):
        index = lax.broadcasted_iota(jnp.int32, (384, 384), axis)
        return sum((index >= edge).astype(jnp.int32) for edge in (96, 192, 288))

    ones[...] = jnp.where(column_of(0) == column_of(1), 1.0, 0.0).astype(BF16)

    has_left = jnp.where(wa == 0, 0.0, 1.0).astype(F32)
    has_right = jnp.where(wa == n_wa - 1, 0.0, 1.0).astype(F32)
    has_above = jnp.where(ha == 0, 0.0, 1.0).astype(F32)
    has_below = jnp.where(ha == n_ha - 1, 0.0, 1.0).astype(F32)

    def activate(x):
        squares = jnp.dot((x * x).astype(BF16), ones[...], preferred_element_type=F32)
        u = x * lax.rsqrt(squares + C * EPS) * gain[...]
        return u + u * jnp.tanh(u)

    def halo_mask(x):
        return jnp.concatenate([x[:, :256] * has_right, x[:, 256:] * has_left], axis=1)

    def groups(gs, edge):
        xs = []
        for g in gs:
            win = lanes(3 * g, 3)
            x = ext[pl.ds(2, T), :, win].reshape(T * TH, 384).astype(F32)
            old = ext[pl.ds(0, 2), :, win].reshape(2 * TH, 384)
            if edge and g == 13:
                x, old = halo_mask(x), halo_mask(old.astype(F32)).astype(BF16)
            xs.append(x)
            for j in range(3):
                stacked[3 * g + j, pl.ds(0, 2 * TH)] = old[:, 128 * j : 128 * (j + 1)]
        activated = activate(jnp.concatenate(xs, axis=0)).astype(BF16)
        for n, g in enumerate(gs):
            before = ext[pl.ds(2, T), :, lanes(jnp.maximum(3 * g - 1, 0))]
            before = pltpu.roll(before.reshape(T * TH, 128).astype(F32), 32, 1)
            for j in range(1 if edge and g == 13 else 3):
                here = pltpu.roll(xs[n][:, 128 * j : 128 * (j + 1)], 32, 1)
                xf[3 * g + j + 1] = jnp.where(lane < 32, before, here)
                before = here
            for j in range(3):
                stacked[3 * g + j, pl.ds(2 * TH, T * TH)] = activated[
                    n * T * TH : (n + 1) * T * TH, 128 * j : 128 * (j + 1)
                ]

    @pl.loop(0, 4)
    def _(n):
        groups([3 * n, 3 * n + 1, 3 * n + 2], False)

    for copy in col_copies:
        copy.wait_recv()
    groups([12, 13], True)
    for copy in row_copies:
        copy.wait_recv()

    @pl.loop(0, 2)
    def _(half):
        his, los = [], []
        for n in range(7):
            g = 7 * half + n
            win = lanes(3 * g, 3)
            hi = below[:, win].astype(F32) * has_below
            lo = above[:, win].astype(F32) * has_above
            if n == 6:
                right_on = jnp.where(half == 1, has_right, 1.0)
                left_on = jnp.where(half == 1, has_left, 1.0)
                hi, lo = (
                    jnp.concatenate([x[:, :256] * right_on, x[:, 256:] * left_on], axis=1)
                    for x in (hi, lo)
                )
            his.append(hi)
            los.append(lo)
        activated = activate(
            jnp.concatenate([x[:8] for pair in zip(his, los) for x in pair], axis=0)
        )
        before = below[:, lanes(jnp.maximum(21 * half - 1, 0))].astype(F32) * has_below
        before = pltpu.roll(before[:8], 32, 1)
        for n in range(7):
            for j in range(3):
                part = slice(128 * j, 128 * (j + 1))
                tile = 21 * half + 3 * n + j
                new = activated[16 * n : 16 * (n + 1), part]
                low = jnp.concatenate([new[:8], his[n][8:, part]], axis=0)
                stacked[tile, pl.ds(6 * TH, 16)] = low.astype(BF16)
                high = jnp.where(sub[:, :128] < 4, new[8:], los[n][:8, part])
                high = jnp.concatenate([high, jnp.zeros((8, 128), F32)], axis=0)
                stacked[tile, pl.ds(6 * TH + 16, 16)] = high.astype(BF16)
                here = pltpu.roll(his[n][:8, part], 32, 1)
                x32[tile + 1] = jnp.where(lane < 32, before, here)
                before = here

    def tile_a(k, j):
        return 3 * k + j + 1

    def tile_b(i, j):
        return EXT + 1 + i if j == 0 else 3 * i + j - 1

    def join():
        @pl.loop(0, 4)
        def _(m):
            planes[m, 0] = planes[m, EXT]
            for i in range(14):
                later = planes[m, 3 * i + 2]
                sooner = planes[m, 41 if i == 0 else 3 * i - 1]
                planes[m, EXT + 1 + i] = jnp.where(lane < 64, later, sooner)

    def product(m, base, tile_of, weights):
        rows = []
        for w in range(7):
            pieces = [
                planes[m, tile_of(base + w, j), pl.ds(a * 16, 64)]
                for a in range(3)
                for j in range(3)
            ]
            rows.append(jnp.concatenate(pieces, axis=1))
        return jnp.dot(
            jnp.concatenate(rows, axis=0),
            weights[pl.ds(m * 1152, 1152)],
            preferred_element_type=F32,
        )

    @pl.loop(0, EXT // 2)
    def _(q):
        both = jnp.concatenate([stacked[2 * q], stacked[2 * q + 1]], axis=1)
        rows = jnp.dot(mixer[...], both, preferred_element_type=F32)
        for h in range(2):
            part = rows[:, 128 * h : 128 * (h + 1)]
            for m in range(4):
                planes[m, 2 * q + h + 1] = part[96 * m : 96 * (m + 1)].astype(BF16)
            l32[2 * q + h] = part[384:].reshape(9, 8, 128)

    join()
    cut_right = jnp.where((lane >= 32) & (wa == n_wa - 1), 0.0, 1.0).astype(F32)

    def both_rows(side, base, tile_of, weights):
        middle[side, 0] = product(1, base, tile_of, weights)
        middle[side, 1] = product(2, base, tile_of, weights)
        one, two = middle[side, 0], middle[side, 1]
        even = product(0, base, tile_of, weights) + (one + two)
        return even, (one - two) - product(3, base, tile_of, weights)

    @pl.loop(0, 2)
    def _(step):
        base = step * 6
        both = both_rows(0, base, tile_a, wa_w)
        for parity in range(2):
            for w in range(7):
                k = base + w
                part = both[parity][64 * w : 64 * (w + 1)]
                x = xf[3 * k + 2, pl.ds(parity, 64, 2)]
                hb[parity, 3 * k + 2] = (x + part[:, :128] + cbias[1]).astype(BF16)
                hp[parity, k + 1] = part[:, 128:]
        base = step * 7
        both = both_rows(1, base, tile_b, wb_w)
        for parity in range(2):
            for w in range(7):
                i = base + w
                part = both[parity][64 * w : 64 * (w + 1)]
                x = xf[3 * i, pl.ds(parity, 64, 2)]
                hb[parity, 3 * i] = (x + part[:, :128] + hp[parity, i] + cbias[2]).astype(BF16)
                x = xf[3 * i + 1, pl.ds(parity, 64, 2)]
                h = x + part[:, 128:] + cbias[0]
                if w == 6:
                    h = h * jnp.where(i == 13, cut_right, 1.0)
                hb[parity, 3 * i + 1] = h.astype(BF16)

    for i in range(14):
        sooner = 40 if i == 0 else 3 * i - 2
        for n in range(9):
            l32[EXT + i, n] = jnp.where(lane < 64, l32[3 * i + 1, n], l32[sooner, n])

    def tile32_a(k, j):
        return 3 * k + j

    def tile32_b(i, j):
        return EXT + i if j == 0 else (41 if i == 0 and j == 1 else 3 * i + j - 2)

    def conv32(tile_of, weights):
        rows = []
        for w in range(14):
            pieces = [l32[tile_of(w, j), n] for n in range(9) for j in range(3)]
            rows.append(jnp.concatenate(pieces, axis=1))
        lhs = jnp.concatenate(rows, axis=0).astype(BF16)
        return jnp.dot(lhs, weights[pl.ds(0, KK * 128)], preferred_element_type=F32)

    acc = conv32(tile32_a, wa_w)
    for k in range(13):
        part = acc[8 * k : 8 * (k + 1)]
        h32[3 * k + 2] = (x32[3 * k + 2] + part[:, :128] + cbias[1]) * has_below
        hp32[k + 1] = part[:, 128:]
    acc = conv32(tile32_b, wb_w)
    for i in range(14):
        part = acc[8 * i : 8 * (i + 1)]
        if i:
            h = x32[3 * i] + part[:, :128] + hp32[i] + cbias[2]
            h32[3 * i] = h * has_below
        h = (x32[3 * i + 1] + part[:, 128:] + cbias[0]) * has_below
        h32[3 * i + 1] = h * cut_right if i == 13 else h

    rows = []
    for k in range(13):
        pieces = [hb[parity, 3 * k + j + 1] for parity in range(2) for j in range(4)]
        rows.append(jnp.concatenate(pieces, axis=1))
    main = jnp.dot(jnp.concatenate(rows, axis=0), down_w[...], preferred_element_type=F32)
    rows = [
        jnp.concatenate([h32[3 * min(k, 12) + j + 1] for j in range(4)], axis=1) for k in range(14)
    ]
    extra = jnp.dot(
        jnp.concatenate(rows, axis=0).astype(BF16),
        down_w[pl.ds(0, 512)],
        preferred_element_type=F32,
    )
    blocks = []
    for b in range(4):
        here = jnp.zeros((64, 128), F32)
        over = jnp.zeros((64, 128), F32)
        over32 = jnp.zeros((8, 128), F32)
        for j in range(4 if b < 3 else 1):
            k = 4 * b + j
            fits = (lane >= 32 * j) & (lane < 32 * (j + 1))
            part = main[64 * k : 64 * (k + 1)]
            turned = pltpu.roll(part, 32 * j, 1) if j else part
            here = jnp.where(fits, turned, here)
            turned = pltpu.roll(part, (32 * j + 96) % 128, 1) if j != 1 else part
            over = jnp.where(fits, turned, over)
            part = extra[8 * k : 8 * (k + 1)]
            turned = pltpu.roll(part, (32 * j + 96) % 128, 1) if j != 1 else part
            over32 = jnp.where(fits, turned, over32)
        for t in range(T):
            vs[t, pl.ds(0, 16)] = over[16 * t : 16 * (t + 1)]
            vs[t, pl.ds(16, 1)] = over32[t : t + 1]
        shifted = jnp.concatenate([vs[t, pl.ds(1, 16)] for t in range(T)], axis=0)
        blocks.append(here + shifted + lbias[...])
    latent = jnp.concatenate(blocks[:3] + [blocks[3][:, :32]], axis=1)
    frame_of = lax.broadcasted_iota(jnp.int32, (64, 1), 0)
    latent = jnp.where(frame_of < valid[0] * 16, latent, 0.0).astype(BF16)

    row = lax.broadcasted_iota(jnp.int32, (64, 64), 0)
    col = lax.broadcasted_iota(jnp.int32, (64, 64), 1)
    by_col = jnp.broadcast_to(owners[...], (64, 64))
    by_row = jnp.sum(jnp.where(row == col, by_col, 0), axis=1, keepdims=True)
    rank = jnp.sum(jnp.where((by_row == by_col) & (row < col), 1, 0), axis=0, keepdims=True)
    slot = owners[...] * 32 + rank
    slots = lax.broadcasted_iota(jnp.int32, (128, 64), 0)
    selector = jnp.where(slots == slot, 1.0, 0.0).astype(BF16)
    send[...] = jnp.dot(selector, latent, preferred_element_type=F32).astype(BF16)

    here = pl.ds(pl.multiple_of(ha * 32, 32), 32)
    copies = []
    for d in range(1, n_ha):
        target = lax.rem(ha + d, n_ha)
        copies.append(
            pltpu.make_async_remote_copy(
                src_ref=send.at[pl.ds(pl.multiple_of(target * 32, 32), 32)],
                dst_ref=received.at[here],
                send_sem=a2a_send.at[d - 1],
                recv_sem=a2a_recv.at[d - 1],
                device_id={"ha": target, "wa": wa},
                device_id_type=pl.DeviceIdType.MESH,
            )
        )
    for copy in copies:
        copy.start()
    received[here] = send[here]
    for copy in row_copies + col_copies:
        copy.wait_send()
    for copy in copies:
        copy.wait()
    full = jnp.concatenate([received[...].astype(F32), jnp.zeros((128, 96), F32)], axis=1)
    out[0, 0, 0] = full.T[:416].astype(BF16)


def row_mixer():
    def at(f, h):
        if 0 <= h < TH:
            return f * TH + h
        if h < 0:
            return 6 * TH + 16 + (4 + f if f < 2 else f - 2)
        return 6 * TH + (8 + 2 * (h - TH) + f if f < 2 else 4 * (h - TH) + f - 2)

    def terms(m, h):
        d = [h - 1, h, h + 1, h + 2]
        return ((d[0], 1, d[2], -1), (d[1], 1, d[2], 1), (d[2], 1, d[1], -1), (d[1], 1, d[3], -1))[m]

    mixer = np.zeros((384 + 72, 6 * TH + 32), np.float32)

    def put(row, f, m, h):
        one, sign, two, other = terms(m, h)
        mixer[row, at(f, one)] += sign
        mixer[row, at(f, two)] += other

    for m in range(4):
        for f in range(6):
            for p in range(16):
                put(96 * m + 16 * f + p, f, m, 2 * p)
    for m in range(3):
        for a in range(3):
            for t in range(T):
                put(384 + 8 * (3 * m + a) + t, a + t, m, TH)
    return mixer


def per_device(
    n_ha,
    n_wa,
    frames,
    cache,
    norm_gain,
    conv_weight,
    conv_bias,
    down_weight,
    down_bias,
    latent_weight,
    latent_bias,
    valid_frames,
    owners,
):
    vmem = pl.BlockSpec(memory_space=pltpu.VMEM)
    hbm = pl.BlockSpec(memory_space=pltpu.HBM)
    routed = pl.pallas_call(
        functools.partial(kernel, n_ha, n_wa),
        out_shape=jax.ShapeDtypeStruct((1, 1, 1, 416, 128), BF16),
        in_specs=[hbm, hbm, vmem, pl.BlockSpec(memory_space=pltpu.SMEM), vmem, hbm, vmem, hbm]
        + [vmem] * 4,
        out_specs=vmem,
        scratch_shapes=[
            pltpu.VMEM((6, TH, EXT * 128), BF16),
            pltpu.VMEM((16, OWN * 128), BF16),
            pltpu.VMEM((16, OWN * 128), BF16),
            pltpu.VMEM((16, EXT * 128), BF16),
            pltpu.VMEM((16, EXT * 128), BF16),
            pltpu.VMEM((EXT, 6 * TH + 32, 128), BF16),
            pltpu.VMEM((41, T * TH, 128), F32),
            pltpu.VMEM((4, EXT + 15, 96, 128), BF16),
            pltpu.VMEM((384, 384), BF16),
            pltpu.VMEM((2, 2, 448, 256), F32),
            pltpu.VMEM((2, 14, 64, 128), F32),
            pltpu.VMEM((2, 41, 64, 128), BF16),
            pltpu.VMEM((EXT + 14, 9, 8, 128), F32),
            pltpu.VMEM((EXT + 1, 8, 128), F32),
            pltpu.VMEM((14, 8, 128), F32),
            pltpu.VMEM((41, 8, 128), F32),
            pltpu.VMEM((T, 24, 128), F32),
            pltpu.VMEM((27, C * C), BF16),
            pltpu.VMEM((9, C * C), BF16),
            pltpu.VMEM((256, 256), BF16),
            pltpu.VMEM((256, 256), BF16),
            pltpu.VMEM((36 * C, 128), F32),
            pltpu.VMEM((4608, 256), BF16),
            pltpu.VMEM((4608, 256), BF16),
            pltpu.VMEM((1024, 128), BF16),
            pltpu.VMEM((1, 384), F32),
            pltpu.VMEM((3, 1, 128), F32),
            pltpu.VMEM((1, 128), F32),
            pltpu.VMEM((128, 416), BF16),
            pltpu.VMEM((128, 416), BF16),
            pltpu.SemaphoreType.DMA((4,)),
            pltpu.SemaphoreType.DMA((10,)),
            pltpu.SemaphoreType.DMA((10,)),
            pltpu.SemaphoreType.DMA((n_ha - 1,)),
            pltpu.SemaphoreType.DMA((n_ha - 1,)),
        ],
        compiler_params=pltpu.CompilerParams(
            collective_id=0, has_side_effects=True, vmem_limit_bytes=54784 * 2**10
        ),
        name="encoder_step",
    )(
        frames,
        cache,
        owners.reshape(1, 64),
        valid_frames,
        norm_gain.reshape(1, C),
        conv_weight,
        conv_bias.reshape(1, C),
        down_weight,
        down_bias.reshape(1, C),
        latent_weight.T,
        latent_bias.reshape(1, Z),
        jnp.asarray(row_mixer(), BF16),
    )
    return jnp.swapaxes(routed, 3, 4)


def solution(mesh):
    in_specs = (
        P("ba", None, "ha", "wa"),
        P("ba", None, "ha", "wa"),
        P(),
        P(),
        P(),
        P(),
        P(),
        P(),
        P(),
        P("ba"),
        P("ba", "ha", "wa", None, None),
    )
    out_specs = P("ba", "ha", "wa", None, None)
    return jax.shard_map(
        functools.partial(per_device, mesh.shape["ha"], mesh.shape["wa"]),
        mesh=mesh,
        in_specs=in_specs,
        out_specs=out_specs,
        check_vma=False,
    )
```

```python
import functools

import jax
import jax.numpy as jnp
import numpy as np
from jax import lax
from jax.experimental import pallas as pl
from jax.experimental.pallas import tpu as pltpu
from jax.sharding import PartitionSpec as P

EPS = 1e-06
C = 96
Z = 16
T = 4
TH = 32
TW = 52
OWN = 39
EXT = 42
FS = 48
KK = 27
QB = 8
F32 = jnp.float32
BF16 = jnp.bfloat16


def lanes(tile, count=1):
    return pl.ds(pl.multiple_of(tile * 128, 128), count * 128)


def kernel(
    n_ha,
    n_wa,
    frames,
    cache,
    owners_in,
    valid,
    norm_gain_in,
    conv_weight,
    conv_bias_in,
    down_weight,
    down_bias_in,
    latent_weight_in,
    latent_bias_in,
    out,
    owners,
    norm_gain,
    conv_bias,
    down_bias,
    latent_weight,
    latent_bias,
    selector,
    ext,
    pack_top,
    pack_bot,
    above,
    below,
    act,
    xf,
    inner,
    outer,
    ones,
    middle,
    hp,
    hb,
    l32,
    x32,
    hp32,
    h32,
    vs,
    conv_taps,
    down_taps,
    taps,
    wa_w,
    wb_w,
    down_w,
    gain,
    cbias,
    lbias,
    send,
    local_sem,
    send_sem,
    recv_sem,
    a2a_send,
    a2a_recv,
):
    ha, wa = lax.axis_index("ha"), lax.axis_index("wa")
    up, down = lax.rem(ha + n_ha - 1, n_ha), lax.rem(ha + 1, n_ha)
    left, right = lax.rem(wa + n_wa - 1, n_wa), lax.rem(wa + 1, n_wa)

    own = pl.ds(0, OWN * 128)
    loads = [
        pltpu.make_async_copy(frames.at[0, t], ext.at[2 + t, :, own], local_sem.at[t])
        for t in range(T)
    ]
    loads += [
        pltpu.make_async_copy(cache.at[0, t], ext.at[t, :, own], local_sem.at[T + t])
        for t in range(2)
    ]
    small = [
        pltpu.make_async_copy(source, target, local_sem.at[8 + n])
        for n, (source, target) in enumerate(
            (
                (owners_in, owners),
                (norm_gain_in, norm_gain),
                (conv_bias_in, conv_bias),
                (down_bias_in, down_bias),
                (latent_weight_in, latent_weight),
                (latent_bias_in, latent_bias),
            )
        )
    ]
    load_conv = pltpu.make_async_copy(conv_weight, conv_taps, local_sem.at[6])
    load_down = pltpu.make_async_copy(down_weight, down_taps, local_sem.at[7])
    for load in loads + small + [load_conv, load_down]:
        load.start()

    barrier = pltpu.get_barrier_semaphore()
    greeted = [
        {"ha": up, "wa": wa},
        {"ha": down, "wa": wa},
        {"ha": ha, "wa": left},
        {"ha": ha, "wa": right},
        {"ha": up, "wa": left},
        {"ha": up, "wa": right},
        {"ha": down, "wa": left},
        {"ha": down, "wa": right},
        {"ha": lax.rem(ha + 2, n_ha), "wa": wa},
    ]
    for device in greeted:
        pl.semaphore_signal(
            barrier, inc=1, device_id=device, device_id_type=pl.DeviceIdType.MESH
        )

    def remote(src, dst, index, device):
        return pltpu.make_async_remote_copy(
            src_ref=src,
            dst_ref=dst,
            send_sem=send_sem.at[index],
            recv_sem=recv_sem.at[index],
            device_id=device,
            device_id_type=pl.DeviceIdType.MESH,
        )

    def column_of(axis):
        index = lax.broadcasted_iota(jnp.int32, (384, 384), axis)
        return sum((index >= edge).astype(jnp.int32) for edge in (96, 192, 288))

    ones[...] = jnp.where(column_of(0) == column_of(1), 1.0, 0.0).astype(BF16)

    for load in small:
        load.wait()
    by_column = (((1,), (1,)), ((), ()))
    by_z = jnp.concatenate([latent_weight[...]] * QB, axis=0)
    rest = down_bias[...]
    pieces = []
    for _ in range(3):
        piece = rest.astype(BF16)
        pieces.append(piece.astype(F32))
        rest = rest - pieces[-1]
    pieces = jnp.concatenate(pieces + [jnp.zeros((13, C), F32)], axis=0).astype(BF16)
    lbias_row = jnp.sum(
        lax.dot_general(pieces, by_z, by_column, preferred_element_type=F32),
        axis=0,
        keepdims=True,
    ) + jnp.concatenate([latent_bias[...]] * QB, axis=1)

    lbias[...] = lbias_row
    bias = conv_bias[...]
    bias = jnp.concatenate([bias[:, 64:]] + [bias] * 3 + [bias[:, :64]], axis=1)
    for j in range(3):
        cbias[j] = bias[:, 128 * j : 128 * (j + 1)]

    gain[...] = jnp.concatenate([norm_gain[...]] * 4, axis=1) * (0.5 * C**0.5)
    row = lax.broadcasted_iota(jnp.int32, (64, 64), 0)
    col = lax.broadcasted_iota(jnp.int32, (64, 64), 1)
    by_col = jnp.broadcast_to(owners[...], (64, 64))
    by_row = jnp.sum(jnp.where(row == col, by_col, 0), axis=1, keepdims=True)
    rank = jnp.sum(jnp.where((by_row == by_col) & (row < col), 1, 0), axis=0, keepdims=True)
    slot = owners[...] * 32 + rank
    slots = lax.broadcasted_iota(jnp.int32, (128, 64), 0)
    selector[...] = jnp.where(slots == slot, 1.0, 0.0).astype(BF16)
    for load in loads:
        load.wait()

    sub = lax.broadcasted_iota(jnp.int32, (8, 384), 0)

    @pl.loop(0, OWN // 3, unroll=True)
    def _(g):
        win = lanes(3 * g, 3)
        tops = [ext[f, pl.ds(0, 16), win].astype(F32) for f in range(6)]
        bots = [ext[f, pl.ds(16, 16), win].astype(F32) for f in range(6)]
        lo = jnp.zeros((8, 384), F32)
        hi = jnp.zeros((8, 384), F32)
        for t in range(T):
            lo = jnp.where(sub == t, tops[2 + t][0:1], lo)
            lo = jnp.where(sub == 4 + t, tops[2 + t][1:2], lo)
        for t in range(2):
            hi = jnp.where(sub == t, tops[t][0:1], hi)
            hi = jnp.where(sub == 2 + t, tops[t][1:2], hi)
        pack_top[:, win] = jnp.concatenate([lo, hi], axis=0).astype(BF16)
        lo = jnp.zeros((8, 384), F32)
        for t in range(T):
            lo = jnp.where(sub == t, bots[2 + t][15:16], lo)
        for t in range(2):
            lo = jnp.where(sub == 4 + t, bots[t][15:16], lo)
        pack_bot[:, win] = jnp.concatenate([lo, jnp.zeros((8, 384), F32)], axis=0).astype(BF16)

    pl.semaphore_wait(barrier, len(greeted))

    first, last = pl.ds(0, 256), pl.ds((OWN - 1) * 128, 128)
    from_right, from_left = pl.ds(OWN * 128, 256), pl.ds((OWN + 2) * 128, 128)
    row_copies = [
        remote(pack_top, below.at[:, own], 0, {"ha": up, "wa": wa}),
        remote(pack_bot, above.at[:, own], 1, {"ha": down, "wa": wa}),
        remote(pack_top.at[:, first], below.at[:, from_right], 2, {"ha": up, "wa": left}),
        remote(pack_top.at[:, last], below.at[:, from_left], 3, {"ha": up, "wa": right}),
        remote(pack_bot.at[:, first], above.at[:, from_right], 4, {"ha": down, "wa": left}),
        remote(pack_bot.at[:, last], above.at[:, from_left], 5, {"ha": down, "wa": right}),
    ]
    col_copies = [
        remote(
            frames.at[0, :, :, first],
            ext.at[pl.ds(2, T), :, from_right],
            6,
            {"ha": ha, "wa": left},
        ),
        remote(
            cache.at[0, :, :, first],
            ext.at[pl.ds(0, 2), :, from_right],
            7,
            {"ha": ha, "wa": left},
        ),
        remote(
            frames.at[0, :, :, last],
            ext.at[pl.ds(2, T), :, from_left],
            8,
            {"ha": ha, "wa": right},
        ),
        remote(
            cache.at[0, :, :, last],
            ext.at[pl.ds(0, 2), :, from_left],
            9,
            {"ha": ha, "wa": right},
        ),
    ]
    for copy in row_copies + col_copies:
        copy.start()

    lane = lax.broadcasted_iota(jnp.int32, (1, 128), 1)


    load_conv.wait()
    load_down.wait()

    @pl.loop(0, C // 4, unroll=4)
    def _(g):
        win = lanes(3 * g, 3)
        for weight, count, at in ((conv_taps, 27, 0), (down_taps, 9, 27)):
            x = weight[:, win].astype(F32)
            t0, t1, t2 = (x[:, 128 * j : 128 * (j + 1)] for j in range(3))
            parts = [
                t0,
                jnp.where(lane < 32, pltpu.roll(t0, 32, 1), pltpu.roll(t1, 32, 1)),
                jnp.where(lane < 64, pltpu.roll(t1, 64, 1), pltpu.roll(t2, 64, 1)),
                pltpu.roll(t2, 96, 1),
            ]
            for u in range(4):
                taps[pl.ds(at * C + 4 * g + u, count, C)] = jnp.where(lane < C, parts[u], 0.0)

    @pl.loop(0, 3)
    def _(a):
        for m in range(4):
            w = []
            for s in range(3):
                g0, g1, g2 = (taps[pl.ds((9 * a + 3 * r + s) * C, C)] for r in range(3))
                if m == 0:
                    w.append(g0)
                elif m == 1:
                    w.append(0.5 * (g0 + g2 + g1))
                elif m == 2:
                    w.append(0.5 * (g0 + g2 - g1))
                else:
                    w.append(g2)
            zero = jnp.zeros((C, 128), F32)
            by96 = [zero] + [pltpu.roll(x, 96, 1) for x in w]
            by64 = [pltpu.roll(x, 64, 1) for x in w] + [zero]
            by32 = [zero] + [pltpu.roll(x, 32, 1) for x in w]
            w = w + [zero]
            at = m * 1152 + a * 384
            for s in range(4):
                rows = pl.ds(pl.multiple_of(at + s * 96, 32), C)
                wa_w[rows, pl.ds(0, 128)] = jnp.where(lane < 96, w[s], by96[s]).astype(BF16)
                wa_w[rows, pl.ds(128, 128)] = jnp.where(lane < 64, by96[s], 0.0).astype(BF16)
                one = jnp.where(lane < 64, 0.0, by64[s]).astype(BF16)
                two = jnp.where(lane < 32, by64[s], by32[s]).astype(BF16)
                if s < 3:
                    rows = pl.ds(pl.multiple_of(at + s * 96 + 64, 32), C)
                    wb_w[rows, pl.ds(0, 128)] = one
                    wb_w[rows, pl.ds(128, 128)] = two
                else:
                    rows = pl.ds(pl.multiple_of(at + 352, 32), 32)
                    wb_w[rows, pl.ds(0, 128)] = one[:32]
                    wb_w[rows, pl.ds(128, 128)] = two[:32]
                    rows = pl.ds(pl.multiple_of(at, 32), 64)
                    wb_w[rows, pl.ds(0, 128)] = one[32:]
                    wb_w[rows, pl.ds(128, 128)] = two[32:]

    fused = lax.dot_general(
        taps[pl.ds(27 * C, 9 * C)][:, :C].astype(BF16),
        by_z,
        by_column,
        preferred_element_type=F32,
    )
    down_w[...] = jnp.zeros((1024, 128), BF16)
    for r in range(3):
        first = (0, 0, 2)[r]
        for col in range(5):
            block = jnp.zeros((C, 128), F32)
            for s in range(3):
                q = col - s
                if q in (0, 2):
                    tap = fused[(3 * r + s) * C : (3 * r + s + 1) * C]
                    place = first + q // 2
                    block = jnp.where((lane >= 16 * place) & (lane < 16 * (place + 1)), tap, block)
            rows = pl.ds((512 if r == 1 else 0) + 32 + C * col, C)
            if r == 2:
                block = block + down_w[rows].astype(F32)
            down_w[rows] = block.astype(BF16)

    has_left = jnp.where(wa == 0, 0.0, 1.0).astype(F32)
    has_right = jnp.where(wa == n_wa - 1, 0.0, 1.0).astype(F32)
    has_above = jnp.where(ha == 0, 0.0, 1.0).astype(F32)
    has_below = jnp.where(ha == n_ha - 1, 0.0, 1.0).astype(F32)

    def activate(x):
        squares = jnp.dot((x * x).astype(BF16), ones[...], preferred_element_type=F32)
        u = x * lax.rsqrt(squares + C * EPS) * gain[...]
        return u + u * jnp.tanh(u)

    def halo_mask(x):
        return jnp.concatenate([x[:, :256] * has_right, x[:, 256:] * has_left], axis=1)

    def groups(gs, edge):
        xs, earlier = [], []
        for g in gs:
            win = lanes(3 * g, 3)
            x = ext[pl.ds(2, T), :, win].reshape(T * TH, 384).astype(F32)
            old = ext[pl.ds(0, 2), :, win].reshape(2 * TH, 384).astype(F32)
            if edge and g == 13:
                x, old = halo_mask(x), halo_mask(old)
            xs.append(x)
            earlier.append(old)
        activated = activate(jnp.concatenate(xs, axis=0))
        for n, g in enumerate(gs):
            before = ext[pl.ds(2, T), :, lanes(jnp.maximum(3 * g - 1, 0))]
            before = pltpu.roll(before.reshape(T * TH, 128).astype(F32), 32, 1)
            for j in range(1 if edge and g == 13 else 3):
                here = pltpu.roll(xs[n][:, 128 * j : 128 * (j + 1)], 32, 1)
                xf[3 * g + j + 1] = jnp.where(lane < 32, before, here)
                before = here
            for j in range(3):
                part = slice(128 * j, 128 * (j + 1))
                tile = 3 * g + j
                for f in range(6):
                    if f < 2:
                        value = earlier[n][f * TH : (f + 1) * TH, part]
                    else:
                        at = n * T * TH + (f - 2) * TH
                        value = activated[at : at + TH, part]
                    act[tile, pl.ds(f * FS + 8, TH)] = value
                for f in range(6):
                    d1 = act[tile, pl.ds(f * FS + 8, 16, 2)]
                    d2 = act[tile, pl.ds(f * FS + 9, 16, 2)]
                    inner[0, tile + 1, pl.ds(f * 16, 16)] = (d1 + d2).astype(BF16)
                    inner[1, tile + 1, pl.ds(f * 16, 16)] = (d2 - d1).astype(BF16)

    for n in range(4):
        groups([3 * n, 3 * n + 1, 3 * n + 2], False)

    for copy in col_copies:
        copy.wait_recv()
    groups([12, 13], True)
    for copy in row_copies:
        copy.wait_recv()

    @pl.loop(0, 2)
    def _(half):
        his, los = [], []
        for n in range(7):
            g = 7 * half + n
            win = lanes(3 * g, 3)
            hi = below[:, win].astype(F32) * has_below
            lo = above[:, win].astype(F32) * has_above
            if n == 6:
                right_on = jnp.where(half == 1, has_right, 1.0)
                left_on = jnp.where(half == 1, has_left, 1.0)
                hi, lo = (
                    jnp.concatenate([x[:, :256] * right_on, x[:, 256:] * left_on], axis=1)
                    for x in (hi, lo)
                )
            his.append(hi)
            los.append(lo)
        activated = activate(
            jnp.concatenate([x[:8] for pair in zip(his, los) for x in pair], axis=0)
        )
        before = below[:, lanes(jnp.maximum(21 * half - 1, 0))].astype(F32) * has_below
        before = pltpu.roll(before[:8], 32, 1)
        for n in range(7):
            for j in range(3):
                part = slice(128 * j, 128 * (j + 1))
                tile = 21 * half + 3 * n + j
                new = activated[16 * n : 16 * (n + 1), part]
                act[tile, pl.ds(2 * FS + 40, T, FS)] = new[0:4]
                act[tile, pl.ds(2 * FS + 41, T, FS)] = new[4:8]
                act[tile, pl.ds(2 * FS + 7, T, FS)] = new[8:12]
                act[tile, pl.ds(40, 2, FS)] = his[n][8:10, part]
                act[tile, pl.ds(41, 2, FS)] = his[n][10:12, part]
                act[tile, pl.ds(7, 2, FS)] = los[n][4:6, part]
                here = pltpu.roll(his[n][:8, part], 32, 1)
                x32[tile + 1] = jnp.where(lane < 32, before, here)
                before = here

    def tile_a(k, j):
        return 3 * k + j + 1

    def tile_b(i, j):
        return EXT + 1 + i if j == 0 else 3 * i + j - 1

    def join(planes):
        @pl.loop(0, 2)
        def _(m):
            planes[m, 0] = planes[m, EXT]
            for i in range(14):
                later = planes[m, 3 * i + 2]
                sooner = planes[m, 41 if i == 0 else 3 * i - 1]
                planes[m, EXT + 1 + i] = jnp.where(lane < 64, later, sooner)

    def product(planes, m, at, base, tile_of, weights):
        rows = []
        for w in range(7):
            pieces = [
                planes[m, tile_of(base + w, j), pl.ds(a * 16, 64)]
                for a in range(3)
                for j in range(3)
            ]
            rows.append(jnp.concatenate(pieces, axis=1))
        return jnp.dot(
            jnp.concatenate(rows, axis=0),
            weights[pl.ds(at * 1152, 1152)],
            preferred_element_type=F32,
        )

    def outer_planes(tile):
        for f in range(6):
            d0, d1, d2, d3 = (act[tile, pl.ds(f * FS + 7 + r, 16, 2)] for r in range(4))
            outer[0, tile + 1, pl.ds(f * 16, 16)] = (d0 - d2).astype(BF16)
            outer[1, tile + 1, pl.ds(f * 16, 16)] = (d1 - d3).astype(BF16)

        for a in range(3):
            d0, d1, d2 = (act[tile, pl.ds(a * FS + 39 + r, T, FS)] for r in range(3))
            l32[tile, a, pl.ds(0, T)] = d0 - d2
            l32[tile, 3 + a, pl.ds(0, T)] = d1 + d2
            l32[tile, 6 + a, pl.ds(0, T)] = d2 - d1

    join(inner)

    for step in range(2):
        for n in range(21):
            outer_planes(21 * step + n)
        for m in range(2):
            middle[step, 0, m] = product(inner, m, 1 + m, 6 * step, tile_a, wa_w)
            middle[step, 1, m] = product(inner, m, 1 + m, 7 * step, tile_b, wb_w)

    join(outer)
    cut_right = jnp.where((lane >= 32) & (wa == n_wa - 1), 0.0, 1.0).astype(F32)

    def both_rows(step, side, base, tile_of, weights):
        one, two = middle[step, side, 0], middle[step, side, 1]
        even = product(outer, 0, 0, base, tile_of, weights) + (one + two)
        return even, (one - two) - product(outer, 1, 3, base, tile_of, weights)

    for step in range(2):
        base = step * 6
        both = both_rows(step, 0, base, tile_a, wa_w)
        for parity in range(2):
            for w in range(7):
                k = base + w
                part = both[parity][64 * w : 64 * (w + 1)]
                x = xf[3 * k + 2, pl.ds(parity, 64, 2)]
                hb[parity, 3 * k + 2] = (x + part[:, :128] + cbias[1]).astype(BF16)
                hp[parity, k + 1] = part[:, 128:]
        base = step * 7
        both = both_rows(step, 1, base, tile_b, wb_w)
        for parity in range(2):
            for w in range(7):
                i = base + w
                part = both[parity][64 * w : 64 * (w + 1)]
                x = xf[3 * i, pl.ds(parity, 64, 2)]
                hb[parity, 3 * i] = (x + part[:, :128] + hp[parity, i] + cbias[2]).astype(BF16)
                x = xf[3 * i + 1, pl.ds(parity, 64, 2)]
                h = x + part[:, 128:] + cbias[0]
                if w == 6:
                    h = h * cut_right if i == 13 else h
                hb[parity, 3 * i + 1] = h.astype(BF16)

    for i in range(14):
        sooner = 40 if i == 0 else 3 * i - 2
        for n in range(9):
            l32[EXT + i, n] = jnp.where(lane < 64, l32[3 * i + 1, n], l32[sooner, n])

    def tile32_a(k, j):
        return 3 * k + j

    def tile32_b(i, j):
        return EXT + i if j == 0 else (41 if i == 0 and j == 1 else 3 * i + j - 2)

    def conv32(tile_of, weights):
        rows = []
        for w in range(14):
            pieces = [l32[tile_of(w, j), n] for n in range(9) for j in range(3)]
            rows.append(jnp.concatenate(pieces, axis=1))
        lhs = jnp.concatenate(rows, axis=0).astype(BF16)
        return jnp.dot(lhs, weights[pl.ds(0, KK * 128)], preferred_element_type=F32)

    acc = conv32(tile32_a, wa_w)
    for k in range(13):
        part = acc[8 * k : 8 * (k + 1)]
        h32[3 * k + 2] = (x32[3 * k + 2] + part[:, :128] + cbias[1]) * has_below
        hp32[k + 1] = part[:, 128:]
    acc = conv32(tile32_b, wb_w)
    for i in range(14):
        part = acc[8 * i : 8 * (i + 1)]
        if i:
            h = x32[3 * i] + part[:, :128] + hp32[i] + cbias[2]
            h32[3 * i] = h * has_below
        h = (x32[3 * i + 1] + part[:, 128:] + cbias[0]) * has_below
        h32[3 * i + 1] = h * cut_right if i == 13 else h

    rows = []
    for k in range(13):
        pieces = [hb[parity, 3 * k + j + 1] for parity in range(2) for j in range(4)]
        rows.append(jnp.concatenate(pieces, axis=1))
    main = jnp.dot(jnp.concatenate(rows, axis=0), down_w[...], preferred_element_type=F32)
    rows = [
        jnp.concatenate([h32[3 * min(k, 12) + j + 1] for j in range(4)], axis=1) for k in range(14)
    ]
    extra = jnp.dot(
        jnp.concatenate(rows, axis=0).astype(BF16),
        down_w[pl.ds(0, 512)],
        preferred_element_type=F32,
    )
    blocks = []
    for b in range(4):
        here = jnp.zeros((64, 128), F32)
        over = jnp.zeros((64, 128), F32)
        over32 = jnp.zeros((8, 128), F32)
        for j in range(4 if b < 3 else 1):
            k = 4 * b + j
            fits = (lane >= 32 * j) & (lane < 32 * (j + 1))
            part = main[64 * k : 64 * (k + 1)]
            turned = pltpu.roll(part, 32 * j, 1) if j else part
            here = jnp.where(fits, turned, here)
            turned = pltpu.roll(part, (32 * j + 96) % 128, 1) if j != 1 else part
            over = jnp.where(fits, turned, over)
            part = extra[8 * k : 8 * (k + 1)]
            turned = pltpu.roll(part, (32 * j + 96) % 128, 1) if j != 1 else part
            over32 = jnp.where(fits, turned, over32)
        for t in range(T):
            vs[t, pl.ds(0, 16)] = over[16 * t : 16 * (t + 1)]
            vs[t, pl.ds(16, 1)] = over32[t : t + 1]
        shifted = jnp.concatenate([vs[t, pl.ds(1, 16)] for t in range(T)], axis=0)
        blocks.append(here + shifted + lbias[...])
    latent = jnp.concatenate(blocks[:3] + [blocks[3][:, :32]], axis=1)
    frame_of = lax.broadcasted_iota(jnp.int32, (64, 1), 0)
    latent = jnp.where(frame_of < valid[0] * 16, latent, 0.0).astype(BF16)

    send[...] = jnp.dot(selector[...], latent, preferred_element_type=F32).astype(BF16)

    here = pl.ds(pl.multiple_of(ha * 32, 32), 32)
    keep = pltpu.make_async_copy(send.at[here], out.at[0, 0, 0, here], local_sem.at[0])
    copies = []
    for d in range(1, n_ha):
        target = lax.rem(ha + d, n_ha)
        copies.append(
            pltpu.make_async_remote_copy(
                src_ref=send.at[pl.ds(pl.multiple_of(target * 32, 32), 32)],
                dst_ref=out.at[0, 0, 0, here],
                send_sem=a2a_send.at[d - 1],
                recv_sem=a2a_recv.at[d - 1],
                device_id={"ha": target, "wa": wa},
                device_id_type=pl.DeviceIdType.MESH,
            )
        )
    for copy in copies:
        copy.start()
    keep.start()
    for copy in row_copies + col_copies:
        copy.wait_send()
    for copy in copies:
        copy.wait()
    keep.wait()


def per_device(
    n_ha,
    n_wa,
    frames,
    cache,
    norm_gain,
    conv_weight,
    conv_bias,
    down_weight,
    down_bias,
    latent_weight,
    latent_bias,
    valid_frames,
    owners,
):
    hbm = pl.BlockSpec(memory_space=pltpu.HBM)
    return pl.pallas_call(
        functools.partial(kernel, n_ha, n_wa),
        out_shape=jax.ShapeDtypeStruct((1, 1, 1, 128, 416), BF16),
        in_specs=[hbm, hbm, hbm, pl.BlockSpec(memory_space=pltpu.SMEM)] + [hbm] * 7,
        out_specs=hbm,
        scratch_shapes=[
            pltpu.VMEM((1, 64), jnp.int32),
            pltpu.VMEM((1, C), F32),
            pltpu.VMEM((1, C), F32),
            pltpu.VMEM((1, C), F32),
            pltpu.VMEM((Z, C), BF16),
            pltpu.VMEM((1, Z), F32),
            pltpu.VMEM((128, 64), BF16),
            pltpu.VMEM((6, TH, EXT * 128), BF16),
            pltpu.VMEM((16, OWN * 128), BF16),
            pltpu.VMEM((16, OWN * 128), BF16),
            pltpu.VMEM((16, EXT * 128), BF16),
            pltpu.VMEM((16, EXT * 128), BF16),
            pltpu.VMEM((EXT, 6 * FS, 128), F32),
            pltpu.VMEM((41, T * TH, 128), F32),
            pltpu.VMEM((2, EXT + 15, 96, 128), BF16),
            pltpu.VMEM((2, EXT + 15, 96, 128), BF16),
            pltpu.VMEM((384, 384), BF16),
            pltpu.VMEM((2, 2, 2, 448, 256), F32),
            pltpu.VMEM((2, 14, 64, 128), F32),
            pltpu.VMEM((2, 41, 64, 128), BF16),
            pltpu.VMEM((EXT + 14, 9, 8, 128), F32),
            pltpu.VMEM((EXT + 1, 8, 128), F32),
            pltpu.VMEM((14, 8, 128), F32),
            pltpu.VMEM((41, 8, 128), F32),
            pltpu.VMEM((T, 24, 128), F32),
            pltpu.VMEM((27, C * C), BF16),
            pltpu.VMEM((9, C * C), BF16),
            pltpu.VMEM((36 * C, 128), F32),
            pltpu.VMEM((4608, 256), BF16),
            pltpu.VMEM((4608, 256), BF16),
            pltpu.VMEM((1024, 128), BF16),
            pltpu.VMEM((1, 384), F32),
            pltpu.VMEM((3, 1, 128), F32),
            pltpu.VMEM((1, 128), F32),
            pltpu.VMEM((128, 416), BF16),
            pltpu.SemaphoreType.DMA((14,)),
            pltpu.SemaphoreType.DMA((10,)),
            pltpu.SemaphoreType.DMA((10,)),
            pltpu.SemaphoreType.DMA((n_ha - 1,)),
            pltpu.SemaphoreType.DMA((n_ha - 1,)),
        ],
        compiler_params=pltpu.CompilerParams(
            collective_id=0, has_side_effects=True, vmem_limit_bytes=56 * 2**20
        ),
        name="encoder_step",
    )(
        frames,
        cache,
        owners.reshape(1, 64),
        valid_frames,
        norm_gain.reshape(1, C),
        conv_weight,
        conv_bias.reshape(1, C),
        down_weight,
        down_bias.reshape(1, C),
        latent_weight.T,
        latent_bias.reshape(1, Z),
    )


def solution(mesh):
    in_specs = (
        P("ba", None, "ha", "wa"),
        P("ba", None, "ha", "wa"),
        P(),
        P(),
        P(),
        P(),
        P(),
        P(),
        P(),
        P("ba"),
        P("ba", "ha", "wa", None, None),
    )
    out_specs = P("ba", "ha", "wa", None, None)
    return jax.shard_map(
        functools.partial(per_device, mesh.shape["ha"], mesh.shape["wa"]),
        mesh=mesh,
        in_specs=in_specs,
        out_specs=out_specs,
        check_vma=False,
    )
```

```python
import functools

import jax
import jax.numpy as jnp
import numpy as np
from jax import lax
from jax.experimental import pallas as pl
from jax.experimental.pallas import tpu as pltpu
from jax.sharding import PartitionSpec as P

EPS = 1e-06
C = 96
Z = 16
T = 4
TH = 32
TW = 52
OWN = 39
EXT = 42
FS = 48
KK = 27
QB = 8
F32 = jnp.float32
BF16 = jnp.bfloat16


def lanes(tile, count=1):
    return pl.ds(pl.multiple_of(tile * 128, 128), count * 128)


def kernel(
    n_ha,
    n_wa,
    frames,
    cache,
    owners_in,
    valid,
    norm_gain_in,
    conv_weight,
    conv_bias_in,
    down_weight,
    down_bias_in,
    latent_weight_in,
    latent_bias_in,
    out,
    owners,
    norm_gain,
    conv_bias,
    down_bias,
    latent_weight,
    latent_bias,
    selector,
    ext,
    pack_top,
    pack_bot,
    above,
    below,
    act,
    xf,
    inner,
    outer,
    ones,
    squares,
    sums,
    prod,
    hb,
    l32,
    x32,
    hp32,
    h32,
    vs,
    conv_taps,
    down_taps,
    taps,
    wa_w,
    wb_w,
    down_w,
    gain,
    cbias,
    lbias,
    send,
    local_sem,
    send_sem,
    recv_sem,
    a2a_send,
    a2a_recv,
):
    ha, wa = lax.axis_index("ha"), lax.axis_index("wa")
    up, down = lax.rem(ha + n_ha - 1, n_ha), lax.rem(ha + 1, n_ha)
    left, right = lax.rem(wa + n_wa - 1, n_wa), lax.rem(wa + 1, n_wa)

    own = pl.ds(0, OWN * 128)
    loads = [
        pltpu.make_async_copy(frames.at[0, t], ext.at[2 + t, :, own], local_sem.at[t])
        for t in range(T)
    ]
    loads += [
        pltpu.make_async_copy(cache.at[0, t], ext.at[t, :, own], local_sem.at[T + t])
        for t in range(2)
    ]
    small = [
        pltpu.make_async_copy(source, target, local_sem.at[8 + n])
        for n, (source, target) in enumerate(
            (
                (owners_in, owners),
                (norm_gain_in, norm_gain),
                (conv_bias_in, conv_bias),
                (down_bias_in, down_bias),
                (latent_weight_in, latent_weight),
                (latent_bias_in, latent_bias),
            )
        )
    ]
    load_conv = pltpu.make_async_copy(conv_weight, conv_taps, local_sem.at[6])
    load_down = pltpu.make_async_copy(down_weight, down_taps, local_sem.at[7])
    for load in loads + small + [load_conv, load_down]:
        load.start()

    barrier = pltpu.get_barrier_semaphore()
    greeted = [
        {"ha": up, "wa": wa},
        {"ha": down, "wa": wa},
        {"ha": ha, "wa": left},
        {"ha": ha, "wa": right},
        {"ha": up, "wa": left},
        {"ha": up, "wa": right},
        {"ha": down, "wa": left},
        {"ha": down, "wa": right},
        {"ha": lax.rem(ha + 2, n_ha), "wa": wa},
    ]
    for device in greeted:
        pl.semaphore_signal(
            barrier, inc=1, device_id=device, device_id_type=pl.DeviceIdType.MESH
        )

    def remote(src, dst, index, device):
        return pltpu.make_async_remote_copy(
            src_ref=src,
            dst_ref=dst,
            send_sem=send_sem.at[index],
            recv_sem=recv_sem.at[index],
            device_id=device,
            device_id_type=pl.DeviceIdType.MESH,
        )

    def column_of(axis):
        index = lax.broadcasted_iota(jnp.int32, (384, 384), axis)
        return sum((index >= edge).astype(jnp.int32) for edge in (96, 192, 288))

    ones[...] = jnp.where(column_of(0) == column_of(1), 1.0, 0.0).astype(BF16)

    for load in small:
        load.wait()
    by_column = (((1,), (1,)), ((), ()))
    by_z = jnp.concatenate([latent_weight[...]] * QB, axis=0)
    rest = down_bias[...]
    pieces = []
    for _ in range(3):
        piece = rest.astype(BF16)
        pieces.append(piece.astype(F32))
        rest = rest - pieces[-1]
    pieces = jnp.concatenate(pieces + [jnp.zeros((13, C), F32)], axis=0).astype(BF16)
    lbias_row = jnp.sum(
        lax.dot_general(pieces, by_z, by_column, preferred_element_type=F32),
        axis=0,
        keepdims=True,
    ) + jnp.concatenate([latent_bias[...]] * QB, axis=1)

    lbias[...] = lbias_row
    bias = conv_bias[...]
    bias = jnp.concatenate([bias[:, 64:]] + [bias] * 3 + [bias[:, :64]], axis=1)
    for j in range(3):
        cbias[j] = bias[:, 128 * j : 128 * (j + 1)]

    gain[...] = jnp.concatenate([norm_gain[...]] * 4, axis=1) * (0.5 * C**0.5)
    row = lax.broadcasted_iota(jnp.int32, (64, 64), 0)
    col = lax.broadcasted_iota(jnp.int32, (64, 64), 1)
    by_col = jnp.broadcast_to(owners[...], (64, 64))
    by_row = jnp.sum(jnp.where(row == col, by_col, 0), axis=1, keepdims=True)
    rank = jnp.sum(jnp.where((by_row == by_col) & (row < col), 1, 0), axis=0, keepdims=True)
    slot = owners[...] * 32 + rank
    slots = lax.broadcasted_iota(jnp.int32, (128, 64), 0)
    selector[...] = jnp.where(slots == slot, 1.0, 0.0).astype(BF16)
    for load in loads:
        load.wait()

    sub = lax.broadcasted_iota(jnp.int32, (8, 384), 0)

    @pl.loop(0, OWN // 3, unroll=True)
    def _(g):
        win = lanes(3 * g, 3)
        tops = [ext[f, pl.ds(0, 16), win].astype(F32) for f in range(6)]
        bots = [ext[f, pl.ds(16, 16), win].astype(F32) for f in range(6)]
        lo = jnp.zeros((8, 384), F32)
        hi = jnp.zeros((8, 384), F32)
        for t in range(T):
            lo = jnp.where(sub == t, tops[2 + t][0:1], lo)
            lo = jnp.where(sub == 4 + t, tops[2 + t][1:2], lo)
        for t in range(2):
            hi = jnp.where(sub == t, tops[t][0:1], hi)
            hi = jnp.where(sub == 2 + t, tops[t][1:2], hi)
        pack_top[:, win] = jnp.concatenate([lo, hi], axis=0).astype(BF16)
        lo = jnp.zeros((8, 384), F32)
        for t in range(T):
            lo = jnp.where(sub == t, bots[2 + t][15:16], lo)
        for t in range(2):
            lo = jnp.where(sub == 4 + t, bots[t][15:16], lo)
        pack_bot[:, win] = jnp.concatenate([lo, jnp.zeros((8, 384), F32)], axis=0).astype(BF16)

    pl.semaphore_wait(barrier, len(greeted))

    first, last = pl.ds(0, 256), pl.ds((OWN - 1) * 128, 128)
    from_right, from_left = pl.ds(OWN * 128, 256), pl.ds((OWN + 2) * 128, 128)
    row_copies = [
        remote(pack_top, below.at[:, own], 0, {"ha": up, "wa": wa}),
        remote(pack_bot, above.at[:, own], 1, {"ha": down, "wa": wa}),
        remote(pack_top.at[:, first], below.at[:, from_right], 2, {"ha": up, "wa": left}),
        remote(pack_top.at[:, last], below.at[:, from_left], 3, {"ha": up, "wa": right}),
        remote(pack_bot.at[:, first], above.at[:, from_right], 4, {"ha": down, "wa": left}),
        remote(pack_bot.at[:, last], above.at[:, from_left], 5, {"ha": down, "wa": right}),
    ]
    col_copies = [
        remote(
            frames.at[0, :, :, first],
            ext.at[pl.ds(2, T), :, from_right],
            6,
            {"ha": ha, "wa": left},
        ),
        remote(
            cache.at[0, :, :, first],
            ext.at[pl.ds(0, 2), :, from_right],
            7,
            {"ha": ha, "wa": left},
        ),
        remote(
            frames.at[0, :, :, last],
            ext.at[pl.ds(2, T), :, from_left],
            8,
            {"ha": ha, "wa": right},
        ),
        remote(
            cache.at[0, :, :, last],
            ext.at[pl.ds(0, 2), :, from_left],
            9,
            {"ha": ha, "wa": right},
        ),
    ]
    for copy in row_copies + col_copies:
        copy.start()

    lane = lax.broadcasted_iota(jnp.int32, (1, 128), 1)


    load_conv.wait()
    load_down.wait()

    @pl.loop(0, C // 4, unroll=4)
    def _(g):
        win = lanes(3 * g, 3)
        for weight, count, at in ((conv_taps, 27, 0), (down_taps, 9, 27)):
            x = weight[:, win].astype(F32)
            t0, t1, t2 = (x[:, 128 * j : 128 * (j + 1)] for j in range(3))
            parts = [
                t0,
                jnp.where(lane < 32, pltpu.roll(t0, 32, 1), pltpu.roll(t1, 32, 1)),
                jnp.where(lane < 64, pltpu.roll(t1, 64, 1), pltpu.roll(t2, 64, 1)),
                pltpu.roll(t2, 96, 1),
            ]
            for u in range(4):
                taps[pl.ds(at * C + 4 * g + u, count, C)] = jnp.where(lane < C, parts[u], 0.0)

    @pl.loop(0, 3)
    def _(a):
        for c in range(0, C, 16):
            g = [
                [taps[pl.ds((9 * a + 3 * r + s) * C + c, 16)] for s in range(3)] for r in range(3)
            ]
            for m in range(4):
                if m == 0:
                    w = g[0]
                elif m == 3:
                    w = g[2]
                else:
                    sign = 1.0 if m == 1 else -1.0
                    w = [0.5 * (g[0][s] + g[2][s] + sign * g[1][s]) for s in range(3)]
                zero = jnp.zeros((16, 128), F32)
                by96 = [zero] + [pltpu.roll(x, 96, 1) for x in w]
                by64 = [pltpu.roll(x, 64, 1) for x in w] + [zero]
                by32 = [zero] + [pltpu.roll(x, 32, 1) for x in w]
                w = list(w) + [zero]
                at = m * 1152 + a * 384
                for s in range(4):
                    rows = pl.ds(pl.multiple_of(at + s * 96 + c, 16), 16)
                    wa_w[rows, pl.ds(0, 128)] = jnp.where(lane < 96, w[s], by96[s]).astype(BF16)
                    wa_w[rows, pl.ds(128, 128)] = jnp.where(lane < 64, by96[s], 0.0).astype(BF16)
                    rows = pl.ds(pl.multiple_of(at + (s * 96 + c + 64) % 384, 16), 16)
                    wb_w[rows, pl.ds(0, 128)] = jnp.where(lane < 64, 0.0, by64[s]).astype(BF16)
                    wb_w[rows, pl.ds(128, 128)] = jnp.where(lane < 32, by64[s], by32[s]).astype(BF16)

    fused = lax.dot_general(
        taps[pl.ds(27 * C, 9 * C)][:, :C].astype(BF16),
        by_z,
        by_column,
        preferred_element_type=F32,
    )
    down_w[...] = jnp.zeros((1024, 128), BF16)
    for r in range(3):
        first = (0, 0, 2)[r]
        for col in range(5):
            block = jnp.zeros((C, 128), F32)
            for s in range(3):
                q = col - s
                if q in (0, 2):
                    tap = fused[(3 * r + s) * C : (3 * r + s + 1) * C]
                    place = first + q // 2
                    block = jnp.where((lane >= 16 * place) & (lane < 16 * (place + 1)), tap, block)
            rows = pl.ds((512 if r == 1 else 0) + 32 + C * col, C)
            if r == 2:
                block = block + down_w[rows].astype(F32)
            down_w[rows] = block.astype(BF16)

    has_left = jnp.where(wa == 0, 0.0, 1.0).astype(F32)
    has_right = jnp.where(wa == n_wa - 1, 0.0, 1.0).astype(F32)
    has_above = jnp.where(ha == 0, 0.0, 1.0).astype(F32)
    has_below = jnp.where(ha == n_ha - 1, 0.0, 1.0).astype(F32)

    def activate(x):
        squares = jnp.dot((x * x).astype(BF16), ones[...], preferred_element_type=F32)
        u = x * lax.rsqrt(squares + C * EPS) * gain[...]
        return u + u * jnp.tanh(u)

    def piece(g, f, j, edge):
        x = ext[f, :, lanes(3 * g + j)].astype(F32)
        if edge and g == 13:
            x = x * (has_right if j < 2 else has_left)
        return x

    def groups(gs, edge):
        for g in gs:
            for f in range(T):
                for j in range(3):
                    x = piece(g, 2 + f, j, edge)
                    squares[g, pl.ds(f * TH, TH), pl.ds(128 * j, 128)] = (x * x).astype(BF16)
        sums[pl.ds(gs[0], len(gs))] = jnp.dot(
            squares[pl.ds(gs[0], len(gs))].reshape(len(gs) * T * TH, 384),
            ones[...],
            preferred_element_type=F32,
        ).reshape(len(gs), T * TH, 384)
        for g in gs:
            for f in range(6):
                rows = pl.ds((f - 2) * TH, TH)
                if f >= 2:
                    before = pltpu.roll(piece(max(g - 1, 0), f, 2, edge), 32, 1)
                for j in range(3):
                    tile = 3 * g + j
                    x = piece(g, f, j, edge)
                    if f >= 2:
                        if tile < 40:
                            here = pltpu.roll(x, 32, 1)
                            xf[tile + 1, rows] = jnp.where(lane < 32, before, here)
                            before = here
                        total = sums[g, rows, pl.ds(128 * j, 128)]
                        u = x * lax.rsqrt(total + C * EPS) * gain[:, 128 * j : 128 * (j + 1)]
                        x = u + u * jnp.tanh(u)
                    act[tile, pl.ds(f * FS + 8, TH)] = x
                    d1 = act[tile, pl.ds(f * FS + 8, 16, 2)]
                    d2 = act[tile, pl.ds(f * FS + 9, 16, 2)]
                    inner[0, tile + 1, pl.ds(f * 16, 16)] = (d1 + d2).astype(BF16)
                    inner[1, tile + 1, pl.ds(f * 16, 16)] = (d2 - d1).astype(BF16)

    for n in range(4):
        groups([3 * n, 3 * n + 1, 3 * n + 2], False)

    for copy in col_copies:
        copy.wait_recv()
    groups([12, 13], True)
    for copy in row_copies:
        copy.wait_recv()

    @pl.loop(0, 2)
    def _(half):
        his, los = [], []
        for n in range(7):
            g = 7 * half + n
            win = lanes(3 * g, 3)
            hi = below[:, win].astype(F32) * has_below
            lo = above[:, win].astype(F32) * has_above
            if n == 6:
                right_on = jnp.where(half == 1, has_right, 1.0)
                left_on = jnp.where(half == 1, has_left, 1.0)
                hi, lo = (
                    jnp.concatenate([x[:, :256] * right_on, x[:, 256:] * left_on], axis=1)
                    for x in (hi, lo)
                )
            his.append(hi)
            los.append(lo)
        activated = activate(
            jnp.concatenate([x[:8] for pair in zip(his, los) for x in pair], axis=0)
        )
        before = below[:, lanes(jnp.maximum(21 * half - 1, 0))].astype(F32) * has_below
        before = pltpu.roll(before[:8], 32, 1)
        for n in range(7):
            for j in range(3):
                part = slice(128 * j, 128 * (j + 1))
                tile = 21 * half + 3 * n + j
                new = activated[16 * n : 16 * (n + 1), part]
                act[tile, pl.ds(2 * FS + 40, T, FS)] = new[0:4]
                act[tile, pl.ds(2 * FS + 41, T, FS)] = new[4:8]
                act[tile, pl.ds(2 * FS + 7, T, FS)] = new[8:12]
                act[tile, pl.ds(40, 2, FS)] = his[n][8:10, part]
                act[tile, pl.ds(41, 2, FS)] = his[n][10:12, part]
                act[tile, pl.ds(7, 2, FS)] = los[n][4:6, part]
                here = pltpu.roll(his[n][:8, part], 32, 1)
                x32[tile + 1] = jnp.where(lane < 32, before, here)
                before = here

    def tile_a(k, j):
        return 3 * k + j + 1

    def tile_b(i, j):
        return EXT + 1 + i if j == 0 else 3 * i + j - 1

    def join(planes):
        @pl.loop(0, 2)
        def _(m):
            planes[m, 0] = planes[m, EXT]
            for i in range(14):
                later = planes[m, 3 * i + 2]
                sooner = planes[m, 41 if i == 0 else 3 * i - 1]
                planes[m, EXT + 1 + i] = jnp.where(lane < 64, later, sooner)

    def product(planes, m, at, base, tile_of, weights):
        rows = []
        for w in range(7):
            pieces = [
                planes[m, tile_of(base + w, j), pl.ds(a * 16, 64)]
                for a in range(3)
                for j in range(3)
            ]
            rows.append(jnp.concatenate(pieces, axis=1))
        return jnp.dot(
            jnp.concatenate(rows, axis=0),
            weights[pl.ds(at * 1152, 1152)],
            preferred_element_type=F32,
        )

    def outer_planes(tile):
        for f in range(6):
            d0, d1, d2, d3 = (act[tile, pl.ds(f * FS + 7 + r, 16, 2)] for r in range(4))
            outer[0, tile + 1, pl.ds(f * 16, 16)] = (d0 - d2).astype(BF16)
            outer[1, tile + 1, pl.ds(f * 16, 16)] = (d1 - d3).astype(BF16)

        for a in range(3):
            d0, d1, d2 = (act[tile, pl.ds(a * FS + 39 + r, T, FS)] for r in range(3))
            l32[tile, a, pl.ds(0, T)] = d0 - d2
            l32[tile, 3 + a, pl.ds(0, T)] = d1 + d2
            l32[tile, 6 + a, pl.ds(0, T)] = d2 - d1

    join(inner)

    for step in range(2):
        for n in range(21):
            outer_planes(21 * step + n)
        rows = pl.ds(448 * step, 448)
        for m in range(2):
            prod[0, 1 + m, rows] = product(inner, m, 1 + m, 6 * step, tile_a, wa_w)
            prod[1, 1 + m, rows] = product(inner, m, 1 + m, 7 * step, tile_b, wb_w)

    join(outer)
    cut_right = jnp.where((lane >= 32) & (wa == n_wa - 1), 0.0, 1.0).astype(F32)

    for step in range(2):
        rows = pl.ds(448 * step, 448)
        for m in range(2):
            prod[0, 3 * m, rows] = product(outer, m, 3 * m, 6 * step, tile_a, wa_w)
            prod[1, 3 * m, rows] = product(outer, m, 3 * m, 7 * step, tile_b, wb_w)

        def both_rows(side, window, half, at):
            row = 64 * window + (64 if side == 0 and window > 6 else 0) + at
            cut = (pl.ds(row, 32), pl.ds(128 * half, 128))
            p0, p1, p2, p3 = (prod[(side, m) + cut] for m in range(4))
            return p0 + (p1 + p2), (p1 - p2) - p3

        def put(tile, at, values, mask=None):
            for parity in range(2):
                x = xf[tile + 1, pl.ds(2 * at + parity, 32, 2)]
                h = x + values[parity] + cbias[tile % 3]
                h = h if mask is None else h * mask
                hb[parity, tile + 1, pl.ds(at, 32)] = h.astype(BF16)

        for at in range(0, 64, 32):
            for k in range(7 * step, 7 + 6 * step):
                put(3 * k + 1, at, both_rows(0, k, 0, at))
            for i in range(7 * step, 7 * step + 7):
                if i:
                    one, two = both_rows(0, i - 1, 1, at), both_rows(1, i, 0, at)
                    put(3 * i - 1, at, (one[0] + two[0], one[1] + two[1]))
                put(3 * i, at, both_rows(1, i, 1, at), cut_right if i == 13 else None)

    for i in range(14):
        sooner = 40 if i == 0 else 3 * i - 2
        for n in range(9):
            l32[EXT + i, n] = jnp.where(lane < 64, l32[3 * i + 1, n], l32[sooner, n])

    def tile32_a(k, j):
        return 3 * k + j

    def tile32_b(i, j):
        return EXT + i if j == 0 else (41 if i == 0 and j == 1 else 3 * i + j - 2)

    def conv32(tile_of, weights):
        rows = []
        for w in range(14):
            pieces = [l32[tile_of(w, j), n] for n in range(9) for j in range(3)]
            rows.append(jnp.concatenate(pieces, axis=1))
        lhs = jnp.concatenate(rows, axis=0).astype(BF16)
        return jnp.dot(lhs, weights[pl.ds(0, KK * 128)], preferred_element_type=F32)

    acc = conv32(tile32_a, wa_w)
    for k in range(13):
        part = acc[8 * k : 8 * (k + 1)]
        h32[3 * k + 2] = (x32[3 * k + 2] + part[:, :128] + cbias[1]) * has_below
        hp32[k + 1] = part[:, 128:]
    acc = conv32(tile32_b, wb_w)
    for i in range(14):
        part = acc[8 * i : 8 * (i + 1)]
        if i:
            h = x32[3 * i] + part[:, :128] + hp32[i] + cbias[2]
            h32[3 * i] = h * has_below
        h = (x32[3 * i + 1] + part[:, 128:] + cbias[0]) * has_below
        h32[3 * i + 1] = h * cut_right if i == 13 else h

    rows = []
    for k in range(13):
        pieces = [hb[parity, 3 * k + j + 1] for parity in range(2) for j in range(4)]
        rows.append(jnp.concatenate(pieces, axis=1))
    main = jnp.dot(jnp.concatenate(rows, axis=0), down_w[...], preferred_element_type=F32)
    rows = [
        jnp.concatenate([h32[3 * min(k, 12) + j + 1] for j in range(4)], axis=1) for k in range(14)
    ]
    extra = jnp.dot(
        jnp.concatenate(rows, axis=0).astype(BF16),
        down_w[pl.ds(0, 512)],
        preferred_element_type=F32,
    )
    blocks = []
    for b in range(4):
        here = jnp.zeros((64, 128), F32)
        over = jnp.zeros((64, 128), F32)
        over32 = jnp.zeros((8, 128), F32)
        for j in range(4 if b < 3 else 1):
            k = 4 * b + j
            fits = (lane >= 32 * j) & (lane < 32 * (j + 1))
            part = main[64 * k : 64 * (k + 1)]
            turned = pltpu.roll(part, 32 * j, 1) if j else part
            here = jnp.where(fits, turned, here)
            turned = pltpu.roll(part, (32 * j + 96) % 128, 1) if j != 1 else part
            over = jnp.where(fits, turned, over)
            part = extra[8 * k : 8 * (k + 1)]
            turned = pltpu.roll(part, (32 * j + 96) % 128, 1) if j != 1 else part
            over32 = jnp.where(fits, turned, over32)
        for t in range(T):
            vs[t, pl.ds(0, 16)] = over[16 * t : 16 * (t + 1)]
            vs[t, pl.ds(16, 1)] = over32[t : t + 1]
        shifted = jnp.concatenate([vs[t, pl.ds(1, 16)] for t in range(T)], axis=0)
        blocks.append(here + shifted + lbias[...])
    latent = jnp.concatenate(blocks[:3] + [blocks[3][:, :32]], axis=1)
    frame_of = lax.broadcasted_iota(jnp.int32, (64, 1), 0)
    latent = jnp.where(frame_of < valid[0] * 16, latent, 0.0).astype(BF16)

    send[...] = jnp.dot(selector[...], latent, preferred_element_type=F32).astype(BF16)

    here = pl.ds(pl.multiple_of(ha * 32, 32), 32)
    keep = pltpu.make_async_copy(send.at[here], out.at[0, 0, 0, here], local_sem.at[0])
    copies = []
    for d in range(1, n_ha):
        target = lax.rem(ha + d, n_ha)
        copies.append(
            pltpu.make_async_remote_copy(
                src_ref=send.at[pl.ds(pl.multiple_of(target * 32, 32), 32)],
                dst_ref=out.at[0, 0, 0, here],
                send_sem=a2a_send.at[d - 1],
                recv_sem=a2a_recv.at[d - 1],
                device_id={"ha": target, "wa": wa},
                device_id_type=pl.DeviceIdType.MESH,
            )
        )
    for copy in copies:
        copy.start()
    keep.start()
    for copy in row_copies + col_copies:
        copy.wait_send()
    for copy in copies:
        copy.wait()
    keep.wait()


def per_device(
    n_ha,
    n_wa,
    frames,
    cache,
    norm_gain,
    conv_weight,
    conv_bias,
    down_weight,
    down_bias,
    latent_weight,
    latent_bias,
    valid_frames,
    owners,
):
    hbm = pl.BlockSpec(memory_space=pltpu.HBM)
    return pl.pallas_call(
        functools.partial(kernel, n_ha, n_wa),
        out_shape=jax.ShapeDtypeStruct((1, 1, 1, 128, 416), BF16),
        in_specs=[hbm, hbm, hbm, pl.BlockSpec(memory_space=pltpu.SMEM)] + [hbm] * 7,
        out_specs=hbm,
        scratch_shapes=[
            pltpu.VMEM((1, 64), jnp.int32),
            pltpu.VMEM((1, C), F32),
            pltpu.VMEM((1, C), F32),
            pltpu.VMEM((1, C), F32),
            pltpu.VMEM((Z, C), BF16),
            pltpu.VMEM((1, Z), F32),
            pltpu.VMEM((128, 64), BF16),
            pltpu.VMEM((6, TH, EXT * 128), BF16),
            pltpu.VMEM((16, OWN * 128), BF16),
            pltpu.VMEM((16, OWN * 128), BF16),
            pltpu.VMEM((16, EXT * 128), BF16),
            pltpu.VMEM((16, EXT * 128), BF16),
            pltpu.VMEM((EXT, 6 * FS, 128), F32),
            pltpu.VMEM((41, T * TH, 128), F32),
            pltpu.VMEM((2, EXT + 15, 96, 128), BF16),
            pltpu.VMEM((2, EXT + 15, 96, 128), BF16),
            pltpu.VMEM((384, 384), BF16),
            pltpu.VMEM((14, T * TH, 384), BF16),
            pltpu.VMEM((14, T * TH, 384), F32),
            pltpu.VMEM((2, 4, 896, 256), F32),
            pltpu.VMEM((2, 41, 64, 128), BF16),
            pltpu.VMEM((EXT + 14, 9, 8, 128), F32),
            pltpu.VMEM((EXT + 1, 8, 128), F32),
            pltpu.VMEM((14, 8, 128), F32),
            pltpu.VMEM((41, 8, 128), F32),
            pltpu.VMEM((T, 24, 128), F32),
            pltpu.VMEM((27, C * C), BF16),
            pltpu.VMEM((9, C * C), BF16),
            pltpu.VMEM((36 * C, 128), F32),
            pltpu.VMEM((4608, 256), BF16),
            pltpu.VMEM((4608, 256), BF16),
            pltpu.VMEM((1024, 128), BF16),
            pltpu.VMEM((1, 384), F32),
            pltpu.VMEM((3, 1, 128), F32),
            pltpu.VMEM((1, 128), F32),
            pltpu.VMEM((128, 416), BF16),
            pltpu.SemaphoreType.DMA((14,)),
            pltpu.SemaphoreType.DMA((10,)),
            pltpu.SemaphoreType.DMA((10,)),
            pltpu.SemaphoreType.DMA((n_ha - 1,)),
            pltpu.SemaphoreType.DMA((n_ha - 1,)),
        ],
        compiler_params=pltpu.CompilerParams(
            collective_id=0, has_side_effects=True, vmem_limit_bytes=56 * 2**20
        ),
        name="encoder_step",
    )(
        frames,
        cache,
        owners.reshape(1, 64),
        valid_frames,
        norm_gain.reshape(1, C),
        conv_weight,
        conv_bias.reshape(1, C),
        down_weight,
        down_bias.reshape(1, C),
        latent_weight.T,
        latent_bias.reshape(1, Z),
    )


def solution(mesh):
    in_specs = (
        P("ba", None, "ha", "wa"),
        P("ba", None, "ha", "wa"),
        P(),
        P(),
        P(),
        P(),
        P(),
        P(),
        P(),
        P("ba"),
        P("ba", "ha", "wa", None, None),
    )
    out_specs = P("ba", "ha", "wa", None, None)
    return jax.shard_map(
        functools.partial(per_device, mesh.shape["ha"], mesh.shape["wa"]),
        mesh=mesh,
        in_specs=in_specs,
        out_specs=out_specs,
        check_vma=False,
    )
```

```python
import functools

import jax
import jax.numpy as jnp
import numpy as np
from jax import lax
from jax.experimental import pallas as pl
from jax.experimental.pallas import tpu as pltpu
from jax.sharding import PartitionSpec as P

EPS = 1e-06
C = 96
Z = 16
T = 4
TH = 32
TW = 52
TOP_TILES = 30
BOTTOM_TILES = 20
OWN = 39
EXT = 42
FS = 48
KK = 27
QB = 8
F32 = jnp.float32
BF16 = jnp.bfloat16


def lanes(tile, count=1):
    return pl.ds(pl.multiple_of(tile * 128, 128), count * 128)


def kernel(
    n_ha,
    n_wa,
    frames,
    cache,
    owners_in,
    valid,
    norm_gain_in,
    conv_weight,
    conv_bias_in,
    down_weight,
    down_bias_in,
    latent_weight_in,
    latent_bias_in,
    out,
    owners,
    norm_gain,
    conv_bias,
    down_bias,
    latent_weight,
    latent_bias,
    selector,
    ext,
    pack_top,
    pack_bot,
    corner_top,
    corner_bot,
    above,
    above_side,
    below,
    below_side,
    act,
    xf,
    inner,
    outer,
    ones,
    squares,
    sums,
    prod,
    hb,
    l32,
    x32,
    hp32,
    h32,
    vs,
    conv_taps,
    down_taps,
    taps,
    wa_w,
    wb_w,
    down_w,
    gain,
    cbias,
    lbias,
    send,
    local_sem,
    send_sem,
    recv_sem,
    a2a_send,
    a2a_recv,
):
    ha, wa = lax.axis_index("ha"), lax.axis_index("wa")
    up, down = lax.rem(ha + n_ha - 1, n_ha), lax.rem(ha + 1, n_ha)
    left, right = lax.rem(wa + n_wa - 1, n_wa), lax.rem(wa + 1, n_wa)

    own = pl.ds(0, OWN * 128)
    loads = [
        pltpu.make_async_copy(frames.at[0, t], ext.at[2 + t, :, own], local_sem.at[t])
        for t in range(T)
    ]
    loads += [
        pltpu.make_async_copy(cache.at[0, t], ext.at[t, :, own], local_sem.at[T + t])
        for t in range(2)
    ]
    small = [
        pltpu.make_async_copy(source, target, local_sem.at[8 + n])
        for n, (source, target) in enumerate(
            (
                (owners_in, owners),
                (norm_gain_in, norm_gain),
                (conv_bias_in, conv_bias),
                (down_bias_in, down_bias),
                (latent_weight_in, latent_weight),
                (latent_bias_in, latent_bias),
            )
        )
    ]
    load_conv = pltpu.make_async_copy(conv_weight, conv_taps, local_sem.at[6])
    load_down = pltpu.make_async_copy(down_weight, down_taps, local_sem.at[7])
    for load in loads + small + [load_conv, load_down]:
        load.start()

    barrier = pltpu.get_barrier_semaphore()
    greeted = [
        {"ha": up, "wa": wa},
        {"ha": down, "wa": wa},
        {"ha": ha, "wa": left},
        {"ha": ha, "wa": right},
        {"ha": up, "wa": left},
        {"ha": up, "wa": right},
        {"ha": down, "wa": left},
        {"ha": down, "wa": right},
        {"ha": lax.rem(ha + 2, n_ha), "wa": wa},
    ]
    for device in greeted:
        pl.semaphore_signal(
            barrier, inc=1, device_id=device, device_id_type=pl.DeviceIdType.MESH
        )

    def remote(src, dst, index, device):
        return pltpu.make_async_remote_copy(
            src_ref=src,
            dst_ref=dst,
            send_sem=send_sem.at[index],
            recv_sem=recv_sem.at[index],
            device_id=device,
            device_id_type=pl.DeviceIdType.MESH,
        )

    first, last = pl.ds(0, 256), pl.ds((OWN - 1) * 128, 128)
    from_right, from_left = pl.ds(OWN * 128, 256), pl.ds((OWN + 2) * 128, 128)
    col_copies = [
        remote(
            frames.at[0, :, :, first],
            ext.at[pl.ds(2, T), :, from_right],
            6,
            {"ha": ha, "wa": left},
        ),
        remote(
            cache.at[0, :, :, first],
            ext.at[pl.ds(0, 2), :, from_right],
            7,
            {"ha": ha, "wa": left},
        ),
        remote(
            frames.at[0, :, :, last],
            ext.at[pl.ds(2, T), :, from_left],
            8,
            {"ha": ha, "wa": right},
        ),
        remote(
            cache.at[0, :, :, last],
            ext.at[pl.ds(0, 2), :, from_left],
            9,
            {"ha": ha, "wa": right},
        ),
    ]
    pl.semaphore_wait(barrier, len(greeted))
    for copy in col_copies:
        copy.start()
    for load in loads:
        load.wait()

    sub = lax.broadcasted_iota(jnp.int32, (8, 128), 0)

    def top_rows(tile):
        tops = [ext[f, pl.ds(0, 16), pl.ds(tile * 128, 128)].astype(F32)[:8] for f in range(6)]
        lo = jnp.zeros((8, 128), F32)
        hi = jnp.zeros((8, 128), F32)
        for t in range(T):
            lo = jnp.where(sub == t, tops[2 + t][0:1], lo)
            lo = jnp.where(sub == 4 + t, tops[2 + t][1:2], lo)
        for t in range(2):
            hi = jnp.where(sub == t, tops[t][0:1], hi)
            hi = jnp.where(sub == 2 + t, tops[t][1:2], hi)
        return lo, hi

    def bottom_rows(tile):
        bots = [ext[f, pl.ds(16, 16), pl.ds(tile * 128, 128)].astype(F32)[8:] for f in range(6)]
        lo = jnp.zeros((8, 128), F32)
        for t in range(T):
            lo = jnp.where(sub == t, bots[2 + t][7:8], lo)
        for t in range(2):
            lo = jnp.where(sub == 4 + t, bots[t][7:8], lo)
        return lo

    def put_pack(target, tile, lo, hi):
        target[:, pl.ds(tile * 128, 128)] = jnp.concatenate([lo, hi], axis=0).astype(BF16)

    above_us, below_us = {"ha": up, "wa": wa}, {"ha": down, "wa": wa}
    half = TOP_TILES // 2 * 128
    row_copies = []

    def send_rows(copy):
        copy.start()
        row_copies.append(copy)

    spread = TOP_TILES // 3
    for tile in range(TOP_TILES):
        lo, hi = top_rows(tile) if tile < TOP_TILES - 1 else (jnp.zeros((8, 128), F32),) * 2
        far_lo, far_hi = top_rows(TOP_TILES - 1 + tile % spread)
        far = (pltpu.roll(far_lo, 4, 0), far_lo, pltpu.roll(far_hi, 4, 0))[tile // spread]
        put_pack(pack_top, tile, lo, jnp.where(sub < 4, hi, far))
        if tile == TOP_TILES // 2 - 1:
            cut = pl.ds(0, half)
            send_rows(remote(pack_top.at[:, cut], below.at[:, cut], 0, above_us))
    cut = pl.ds(half, half)
    send_rows(remote(pack_top.at[:, cut], below.at[:, cut], 10, above_us))
    for tile in range(BOTTOM_TILES):
        far = tile + BOTTOM_TILES
        hi = bottom_rows(far) if far < OWN else jnp.zeros((8, 128), F32)
        put_pack(pack_bot, tile, bottom_rows(tile), hi)
    send_rows(remote(pack_bot, above, 1, below_us))
    for n, tile in enumerate((0, 1, OWN - 1)):
        put_pack(corner_top, n, *top_rows(tile))
        put_pack(corner_bot, n, bottom_rows(tile), jnp.zeros((8, 128), F32))
    one, two = pl.ds(0, 256), pl.ds(256, 128)
    for source, target, index, to in (
        (corner_top, below_side, 2, up),
        (corner_bot, above_side, 4, down),
    ):
        for n, (cut, side) in enumerate(((one, left), (two, right))):
            send_rows(
                remote(source.at[:, cut], target.at[:, cut], index + n, {"ha": to, "wa": side})
            )

    lane = lax.broadcasted_iota(jnp.int32, (1, 128), 1)

    def column_of(axis):
        index = lax.broadcasted_iota(jnp.int32, (384, 384), axis)
        return sum((index >= edge).astype(jnp.int32) for edge in (96, 192, 288))

    ones[...] = jnp.where(column_of(0) == column_of(1), 1.0, 0.0).astype(BF16)

    for load in small:
        load.wait()
    by_column = (((1,), (1,)), ((), ()))
    by_z = jnp.concatenate([latent_weight[...]] * QB, axis=0)
    rest = down_bias[...]
    pieces = []
    for _ in range(3):
        piece = rest.astype(BF16)
        pieces.append(piece.astype(F32))
        rest = rest - pieces[-1]
    pieces = jnp.concatenate(pieces + [jnp.zeros((13, C), F32)], axis=0).astype(BF16)
    lbias_row = jnp.sum(
        lax.dot_general(pieces, by_z, by_column, preferred_element_type=F32),
        axis=0,
        keepdims=True,
    ) + jnp.concatenate([latent_bias[...]] * QB, axis=1)

    lbias[...] = lbias_row
    bias = conv_bias[...]
    bias = jnp.concatenate([bias[:, 64:]] + [bias] * 3 + [bias[:, :64]], axis=1)
    for j in range(3):
        cbias[j] = bias[:, 128 * j : 128 * (j + 1)]

    gain[...] = jnp.concatenate([norm_gain[...]] * 4, axis=1) * (0.5 * C**0.5)
    row = lax.broadcasted_iota(jnp.int32, (64, 64), 0)
    col = lax.broadcasted_iota(jnp.int32, (64, 64), 1)
    by_col = jnp.broadcast_to(owners[...], (64, 64))
    by_row = jnp.sum(jnp.where(row == col, by_col, 0), axis=1, keepdims=True)
    rank = jnp.sum(jnp.where((by_row == by_col) & (row < col), 1, 0), axis=0, keepdims=True)
    slot = owners[...] * 32 + rank
    slots = lax.broadcasted_iota(jnp.int32, (128, 64), 0)
    selector[...] = jnp.where(slots == slot, 1.0, 0.0).astype(BF16)


    load_conv.wait()
    load_down.wait()

    @pl.loop(0, C // 4, unroll=4)
    def _(g):
        win = lanes(3 * g, 3)
        for weight, count, at in ((conv_taps, 27, 0), (down_taps, 9, 27)):
            x = weight[:, win].astype(F32)
            t0, t1, t2 = (x[:, 128 * j : 128 * (j + 1)] for j in range(3))
            parts = [
                t0,
                jnp.where(lane < 32, pltpu.roll(t0, 32, 1), pltpu.roll(t1, 32, 1)),
                jnp.where(lane < 64, pltpu.roll(t1, 64, 1), pltpu.roll(t2, 64, 1)),
                pltpu.roll(t2, 96, 1),
            ]
            for u in range(4):
                taps[pl.ds(at * C + 4 * g + u, count, C)] = jnp.where(lane < C, parts[u], 0.0)

    @pl.loop(0, 3)
    def _(a):
        for c in range(0, C, 16):
            g = [
                [taps[pl.ds((9 * a + 3 * r + s) * C + c, 16)] for s in range(3)] for r in range(3)
            ]
            for m in range(4):
                if m == 0:
                    w = g[0]
                elif m == 3:
                    w = g[2]
                else:
                    sign = 1.0 if m == 1 else -1.0
                    w = [0.5 * (g[0][s] + g[2][s] + sign * g[1][s]) for s in range(3)]
                zero = jnp.zeros((16, 128), F32)
                by96 = [zero] + [pltpu.roll(x, 96, 1) for x in w]
                by64 = [pltpu.roll(x, 64, 1) for x in w] + [zero]
                by32 = [zero] + [pltpu.roll(x, 32, 1) for x in w]
                w = list(w) + [zero]
                at = m * 1152 + a * 384
                for s in range(4):
                    rows = pl.ds(pl.multiple_of(at + s * 96 + c, 16), 16)
                    wa_w[rows, pl.ds(0, 128)] = jnp.where(lane < 96, w[s], by96[s]).astype(BF16)
                    wa_w[rows, pl.ds(128, 128)] = jnp.where(lane < 64, by96[s], 0.0).astype(BF16)
                    rows = pl.ds(pl.multiple_of(at + (s * 96 + c + 64) % 384, 16), 16)
                    wb_w[rows, pl.ds(0, 128)] = jnp.where(lane < 64, 0.0, by64[s]).astype(BF16)
                    wb_w[rows, pl.ds(128, 128)] = jnp.where(lane < 32, by64[s], by32[s]).astype(BF16)

    fused = lax.dot_general(
        taps[pl.ds(27 * C, 9 * C)][:, :C].astype(BF16),
        by_z,
        by_column,
        preferred_element_type=F32,
    )
    down_w[...] = jnp.zeros((1024, 128), BF16)
    for r in range(3):
        first = (0, 0, 2)[r]
        for col in range(5):
            block = jnp.zeros((C, 128), F32)
            for s in range(3):
                q = col - s
                if q in (0, 2):
                    tap = fused[(3 * r + s) * C : (3 * r + s + 1) * C]
                    place = first + q // 2
                    block = jnp.where((lane >= 16 * place) & (lane < 16 * (place + 1)), tap, block)
            rows = pl.ds((512 if r == 1 else 0) + 32 + C * col, C)
            if r == 2:
                block = block + down_w[rows].astype(F32)
            down_w[rows] = block.astype(BF16)

    has_left = jnp.where(wa == 0, 0.0, 1.0).astype(F32)
    has_right = jnp.where(wa == n_wa - 1, 0.0, 1.0).astype(F32)
    has_above = jnp.where(ha == 0, 0.0, 1.0).astype(F32)
    has_below = jnp.where(ha == n_ha - 1, 0.0, 1.0).astype(F32)

    def activate(x):
        squares = jnp.dot((x * x).astype(BF16), ones[...], preferred_element_type=F32)
        u = x * lax.rsqrt(squares + C * EPS) * gain[...]
        return u + u * jnp.tanh(u)

    def piece(g, f, j, edge):
        x = ext[f, :, lanes(3 * g + j)].astype(F32)
        if edge and g == 13:
            x = x * (has_right if j < 2 else has_left)
        return x

    def groups(gs, edge):
        for g in gs:
            for f in range(T):
                for j in range(3):
                    x = piece(g, 2 + f, j, edge)
                    squares[g, pl.ds(f * TH, TH), pl.ds(128 * j, 128)] = (x * x).astype(BF16)
        sums[pl.ds(gs[0], len(gs))] = jnp.dot(
            squares[pl.ds(gs[0], len(gs))].reshape(len(gs) * T * TH, 384),
            ones[...],
            preferred_element_type=F32,
        ).reshape(len(gs), T * TH, 384)
        for g in gs:
            for f in range(6):
                rows = pl.ds((f - 2) * TH, TH)
                if f >= 2:
                    before = pltpu.roll(piece(max(g - 1, 0), f, 2, edge), 32, 1)
                for j in range(3):
                    tile = 3 * g + j
                    x = piece(g, f, j, edge)
                    if f >= 2:
                        if tile < 40:
                            here = pltpu.roll(x, 32, 1)
                            xf[tile + 1, rows] = jnp.where(lane < 32, before, here)
                            before = here
                        total = sums[g, rows, pl.ds(128 * j, 128)]
                        u = x * lax.rsqrt(total + C * EPS) * gain[:, 128 * j : 128 * (j + 1)]
                        x = u + u * jnp.tanh(u)
                    act[tile, pl.ds(f * FS + 8, TH)] = x
                    d1 = act[tile, pl.ds(f * FS + 8, 16, 2)]
                    d2 = act[tile, pl.ds(f * FS + 9, 16, 2)]
                    inner[0, tile + 1, pl.ds(f * 16, 16)] = (d1 + d2).astype(BF16)
                    inner[1, tile + 1, pl.ds(f * 16, 16)] = (d2 - d1).astype(BF16)

    for n in range(4):
        groups([3 * n, 3 * n + 1, 3 * n + 2], False)

    for copy in col_copies:
        copy.wait_recv()
    groups([12, 13], True)
    for copy in row_copies:
        copy.wait_recv()

    def halo_rows(tile):
        if tile >= OWN:
            cut = pl.ds((tile - OWN) * 128, 128)
            hi, lo = below_side[:, cut].astype(F32), above_side[:, cut].astype(F32)[:8]
            mask = has_right if tile < OWN + 2 else has_left
            return hi * (has_below * mask), lo * (has_above * mask)
        if tile < TOP_TILES - 1:
            hi = below[:, pl.ds(tile * 128, 128)].astype(F32)
        else:
            far = [
                below[:, pl.ds((spread * n + tile - TOP_TILES + 1) * 128, 128)].astype(F32)[8:]
                for n in range(3)
            ]
            hi = jnp.concatenate(
                [jnp.where(sub < 4, pltpu.roll(far[0], 4, 0), far[1]), pltpu.roll(far[2], 4, 0)],
                axis=0,
            )
        lo = above[:, pl.ds(tile % BOTTOM_TILES * 128, 128)].astype(F32)
        lo = lo[:8] if tile < BOTTOM_TILES else lo[8:]
        return hi * has_below, lo * has_above

    for part in range(2):
        tiles = range(21 * part, 21 * (part + 1))
        rows = [halo_rows(tile) for tile in tiles]
        stacked = [jnp.concatenate([hi[:8], lo], axis=0) for hi, lo in rows]
        activated = activate(
            jnp.concatenate(
                [jnp.concatenate(stacked[3 * n : 3 * n + 3], axis=1) for n in range(7)], axis=0
            )
        )
        before = halo_rows(max(21 * part - 1, 0))[0][:8]
        before = pltpu.roll(before, 32, 1)
        for n, tile in enumerate(tiles):
            hi, lo = rows[n]
            cut = slice(128 * (n % 3), 128 * (n % 3 + 1))
            new = activated[16 * (n // 3) : 16 * (n // 3 + 1), cut]
            act[tile, pl.ds(2 * FS + 40, T, FS)] = new[0:4]
            act[tile, pl.ds(2 * FS + 41, T, FS)] = new[4:8]
            act[tile, pl.ds(2 * FS + 7, T, FS)] = new[8:12]
            act[tile, pl.ds(40, 2, FS)] = hi[8:10]
            act[tile, pl.ds(41, 2, FS)] = hi[10:12]
            act[tile, pl.ds(7, 2, FS)] = lo[4:6]
            here = pltpu.roll(hi[:8], 32, 1)
            x32[tile + 1] = jnp.where(lane < 32, before, here)
            before = here

    def tile_a(k, j):
        return 3 * k + j + 1

    def tile_b(i, j):
        return EXT + 1 + i if j == 0 else 3 * i + j - 1

    def join(planes):
        @pl.loop(0, 2)
        def _(m):
            planes[m, 0] = planes[m, EXT]
            for i in range(14):
                later = planes[m, 3 * i + 2]
                sooner = planes[m, 41 if i == 0 else 3 * i - 1]
                planes[m, EXT + 1 + i] = jnp.where(lane < 64, later, sooner)

    def product(planes, m, at, base, tile_of, weights):
        rows = []
        for w in range(7):
            pieces = [
                planes[m, tile_of(base + w, j), pl.ds(a * 16, 64)]
                for a in range(3)
                for j in range(3)
            ]
            rows.append(jnp.concatenate(pieces, axis=1))
        return jnp.dot(
            jnp.concatenate(rows, axis=0),
            weights[pl.ds(at * 1152, 1152)],
            preferred_element_type=F32,
        )

    def outer_planes(tile):
        for f in range(6):
            d0, d1, d2, d3 = (act[tile, pl.ds(f * FS + 7 + r, 16, 2)] for r in range(4))
            outer[0, tile + 1, pl.ds(f * 16, 16)] = (d0 - d2).astype(BF16)
            outer[1, tile + 1, pl.ds(f * 16, 16)] = (d1 - d3).astype(BF16)

        for a in range(3):
            d0, d1, d2 = (act[tile, pl.ds(a * FS + 39 + r, T, FS)] for r in range(3))
            l32[tile, a, pl.ds(0, T)] = d0 - d2
            l32[tile, 3 + a, pl.ds(0, T)] = d1 + d2
            l32[tile, 6 + a, pl.ds(0, T)] = d2 - d1

    join(inner)

    for step in range(2):
        for n in range(21):
            outer_planes(21 * step + n)
        rows = pl.ds(448 * step, 448)
        for m in range(2):
            prod[0, 1 + m, rows] = product(inner, m, 1 + m, 6 * step, tile_a, wa_w)
            prod[1, 1 + m, rows] = product(inner, m, 1 + m, 7 * step, tile_b, wb_w)

    join(outer)
    cut_right = jnp.where((lane >= 32) & (wa == n_wa - 1), 0.0, 1.0).astype(F32)

    for step in range(2):
        rows = pl.ds(448 * step, 448)
        for m in range(2):
            prod[0, 3 * m, rows] = product(outer, m, 3 * m, 6 * step, tile_a, wa_w)
            prod[1, 3 * m, rows] = product(outer, m, 3 * m, 7 * step, tile_b, wb_w)

        def both_rows(side, window, half, at):
            row = 64 * window + (64 if side == 0 and window > 6 else 0) + at
            cut = (pl.ds(row, 32), pl.ds(128 * half, 128))
            p0, p1, p2, p3 = (prod[(side, m) + cut] for m in range(4))
            return p0 + (p1 + p2), (p1 - p2) - p3

        def put(tile, at, values, mask=None):
            for parity in range(2):
                x = xf[tile + 1, pl.ds(2 * at + parity, 32, 2)]
                h = x + values[parity] + cbias[tile % 3]
                h = h if mask is None else h * mask
                hb[parity, tile + 1, pl.ds(at, 32)] = h.astype(BF16)

        for at in range(0, 64, 32):
            for k in range(7 * step, 7 + 6 * step):
                put(3 * k + 1, at, both_rows(0, k, 0, at))
            for i in range(7 * step, 7 * step + 7):
                if i:
                    one, two = both_rows(0, i - 1, 1, at), both_rows(1, i, 0, at)
                    put(3 * i - 1, at, (one[0] + two[0], one[1] + two[1]))
                put(3 * i, at, both_rows(1, i, 1, at), cut_right if i == 13 else None)

    for i in range(14):
        sooner = 40 if i == 0 else 3 * i - 2
        for n in range(9):
            l32[EXT + i, n] = jnp.where(lane < 64, l32[3 * i + 1, n], l32[sooner, n])

    def tile32_a(k, j):
        return 3 * k + j

    def tile32_b(i, j):
        return EXT + i if j == 0 else (41 if i == 0 and j == 1 else 3 * i + j - 2)

    def conv32(tile_of, weights):
        rows = []
        for w in range(14):
            pieces = [l32[tile_of(w, j), n] for n in range(9) for j in range(3)]
            rows.append(jnp.concatenate(pieces, axis=1))
        lhs = jnp.concatenate(rows, axis=0).astype(BF16)
        return jnp.dot(lhs, weights[pl.ds(0, KK * 128)], preferred_element_type=F32)

    acc = conv32(tile32_a, wa_w)
    for k in range(13):
        part = acc[8 * k : 8 * (k + 1)]
        h32[3 * k + 2] = (x32[3 * k + 2] + part[:, :128] + cbias[1]) * has_below
        hp32[k + 1] = part[:, 128:]
    acc = conv32(tile32_b, wb_w)
    for i in range(14):
        part = acc[8 * i : 8 * (i + 1)]
        if i:
            h = x32[3 * i] + part[:, :128] + hp32[i] + cbias[2]
            h32[3 * i] = h * has_below
        h = (x32[3 * i + 1] + part[:, 128:] + cbias[0]) * has_below
        h32[3 * i + 1] = h * cut_right if i == 13 else h

    rows = []
    for k in range(13):
        pieces = [hb[parity, 3 * k + j + 1] for parity in range(2) for j in range(4)]
        rows.append(jnp.concatenate(pieces, axis=1))
    main = jnp.dot(jnp.concatenate(rows, axis=0), down_w[...], preferred_element_type=F32)
    rows = [
        jnp.concatenate([h32[3 * min(k, 12) + j + 1] for j in range(4)], axis=1) for k in range(14)
    ]
    extra = jnp.dot(
        jnp.concatenate(rows, axis=0).astype(BF16),
        down_w[pl.ds(0, 512)],
        preferred_element_type=F32,
    )
    blocks = []
    for b in range(4):
        here = jnp.zeros((64, 128), F32)
        over = jnp.zeros((64, 128), F32)
        over32 = jnp.zeros((8, 128), F32)
        for j in range(4 if b < 3 else 1):
            k = 4 * b + j
            fits = (lane >= 32 * j) & (lane < 32 * (j + 1))
            part = main[64 * k : 64 * (k + 1)]
            turned = pltpu.roll(part, 32 * j, 1) if j else part
            here = jnp.where(fits, turned, here)
            turned = pltpu.roll(part, (32 * j + 96) % 128, 1) if j != 1 else part
            over = jnp.where(fits, turned, over)
            part = extra[8 * k : 8 * (k + 1)]
            turned = pltpu.roll(part, (32 * j + 96) % 128, 1) if j != 1 else part
            over32 = jnp.where(fits, turned, over32)
        for t in range(T):
            vs[t, pl.ds(0, 16)] = over[16 * t : 16 * (t + 1)]
            vs[t, pl.ds(16, 1)] = over32[t : t + 1]
        shifted = jnp.concatenate([vs[t, pl.ds(1, 16)] for t in range(T)], axis=0)
        blocks.append(here + shifted + lbias[...])
    latent = jnp.concatenate(blocks[:3] + [blocks[3][:, :32]], axis=1)
    frame_of = lax.broadcasted_iota(jnp.int32, (64, 1), 0)
    latent = jnp.where(frame_of < valid[0] * 16, latent, 0.0).astype(BF16)

    send[...] = jnp.dot(selector[...], latent, preferred_element_type=F32).astype(BF16)

    here = pl.ds(pl.multiple_of(ha * 32, 32), 32)
    keep = pltpu.make_async_copy(send.at[here], out.at[0, 0, 0, here], local_sem.at[0])
    copies = []
    for d in range(1, n_ha):
        target = lax.rem(ha + d, n_ha)
        copies.append(
            pltpu.make_async_remote_copy(
                src_ref=send.at[pl.ds(pl.multiple_of(target * 32, 32), 32)],
                dst_ref=out.at[0, 0, 0, here],
                send_sem=a2a_send.at[d - 1],
                recv_sem=a2a_recv.at[d - 1],
                device_id={"ha": target, "wa": wa},
                device_id_type=pl.DeviceIdType.MESH,
            )
        )
    for copy in copies:
        copy.start()
    keep.start()
    for copy in row_copies + col_copies:
        copy.wait_send()
    for copy in copies:
        copy.wait()
    keep.wait()


def per_device(
    n_ha,
    n_wa,
    frames,
    cache,
    norm_gain,
    conv_weight,
    conv_bias,
    down_weight,
    down_bias,
    latent_weight,
    latent_bias,
    valid_frames,
    owners,
):
    hbm = pl.BlockSpec(memory_space=pltpu.HBM)
    return pl.pallas_call(
        functools.partial(kernel, n_ha, n_wa),
        out_shape=jax.ShapeDtypeStruct((1, 1, 1, 128, 416), BF16),
        in_specs=[hbm, hbm, hbm, pl.BlockSpec(memory_space=pltpu.SMEM)] + [hbm] * 7,
        out_specs=hbm,
        scratch_shapes=[
            pltpu.VMEM((1, 64), jnp.int32),
            pltpu.VMEM((1, C), F32),
            pltpu.VMEM((1, C), F32),
            pltpu.VMEM((1, C), F32),
            pltpu.VMEM((Z, C), BF16),
            pltpu.VMEM((1, Z), F32),
            pltpu.VMEM((128, 64), BF16),
            pltpu.VMEM((6, TH, EXT * 128), BF16),
            pltpu.VMEM((16, TOP_TILES * 128), BF16),
            pltpu.VMEM((16, BOTTOM_TILES * 128), BF16),
            pltpu.VMEM((16, 384), BF16),
            pltpu.VMEM((16, 384), BF16),
            pltpu.VMEM((16, BOTTOM_TILES * 128), BF16),
            pltpu.VMEM((16, 384), BF16),
            pltpu.VMEM((16, TOP_TILES * 128), BF16),
            pltpu.VMEM((16, 384), BF16),
            pltpu.VMEM((EXT, 6 * FS, 128), F32),
            pltpu.VMEM((41, T * TH, 128), F32),
            pltpu.VMEM((2, EXT + 15, 96, 128), BF16),
            pltpu.VMEM((2, EXT + 15, 96, 128), BF16),
            pltpu.VMEM((384, 384), BF16),
            pltpu.VMEM((14, T * TH, 384), BF16),
            pltpu.VMEM((14, T * TH, 384), F32),
            pltpu.VMEM((2, 4, 896, 256), F32),
            pltpu.VMEM((2, 41, 64, 128), BF16),
            pltpu.VMEM((EXT + 14, 9, 8, 128), F32),
            pltpu.VMEM((EXT + 1, 8, 128), F32),
            pltpu.VMEM((14, 8, 128), F32),
            pltpu.VMEM((41, 8, 128), F32),
            pltpu.VMEM((T, 24, 128), F32),
            pltpu.VMEM((27, C * C), BF16),
            pltpu.VMEM((9, C * C), BF16),
            pltpu.VMEM((36 * C, 128), F32),
            pltpu.VMEM((4608, 256), BF16),
            pltpu.VMEM((4608, 256), BF16),
            pltpu.VMEM((1024, 128), BF16),
            pltpu.VMEM((1, 384), F32),
            pltpu.VMEM((3, 1, 128), F32),
            pltpu.VMEM((1, 128), F32),
            pltpu.VMEM((128, 416), BF16),
            pltpu.SemaphoreType.DMA((14,)),
            pltpu.SemaphoreType.DMA((11,)),
            pltpu.SemaphoreType.DMA((11,)),
            pltpu.SemaphoreType.DMA((n_ha - 1,)),
            pltpu.SemaphoreType.DMA((n_ha - 1,)),
        ],
        compiler_params=pltpu.CompilerParams(
            collective_id=0, has_side_effects=True, vmem_limit_bytes=56 * 2**20
        ),
        name="encoder_step",
    )(
        frames,
        cache,
        owners.reshape(1, 64),
        valid_frames,
        norm_gain.reshape(1, C),
        conv_weight,
        conv_bias.reshape(1, C),
        down_weight,
        down_bias.reshape(1, C),
        latent_weight.T,
        latent_bias.reshape(1, Z),
    )


def solution(mesh):
    in_specs = (
        P("ba", None, "ha", "wa"),
        P("ba", None, "ha", "wa"),
        P(),
        P(),
        P(),
        P(),
        P(),
        P(),
        P(),
        P("ba"),
        P("ba", "ha", "wa", None, None),
    )
    out_specs = P("ba", "ha", "wa", None, None)
    return jax.shard_map(
        functools.partial(per_device, mesh.shape["ha"], mesh.shape["wa"]),
        mesh=mesh,
        in_specs=in_specs,
        out_specs=out_specs,
        check_vma=False,
    )
```

```python
import functools

import jax
import jax.numpy as jnp
import numpy as np
from jax import lax
from jax.experimental import pallas as pl
from jax.experimental.pallas import tpu as pltpu
from jax.sharding import PartitionSpec as P

EPS = 1e-06
C = 96
Z = 16
T = 4
TH = 32
TW = 52
TOP_TILES = 30
BOTTOM_TILES = 20
OWN = 39
EXT = 42
FS = 48
KK = 27
QB = 8
F32 = jnp.float32
BF16 = jnp.bfloat16


def lanes(tile, count=1):
    return pl.ds(pl.multiple_of(tile * 128, 128), count * 128)


def kernel(
    n_ha,
    n_wa,
    frames,
    cache,
    owners_in,
    valid,
    norm_gain_in,
    conv_weight,
    conv_bias_in,
    down_weight,
    down_bias_in,
    latent_weight_in,
    latent_bias_in,
    out,
    owners,
    norm_gain,
    conv_bias,
    down_bias,
    latent_weight,
    latent_bias,
    selector,
    ext,
    pack_top,
    pack_bot,
    corner_top,
    corner_bot,
    above,
    above_side,
    below,
    below_side,
    act,
    xf,
    inner,
    outer,
    ones,
    squares,
    sums,
    prod,
    hb,
    l32,
    x32,
    hp32,
    h32,
    vs,
    conv_taps,
    down_taps,
    taps,
    wa_w,
    wb_w,
    down_w,
    gain,
    cbias,
    lbias,
    send,
    local_sem,
    send_sem,
    recv_sem,
    a2a_send,
    a2a_recv,
):
    ha, wa = lax.axis_index("ha"), lax.axis_index("wa")
    up, down = lax.rem(ha + n_ha - 1, n_ha), lax.rem(ha + 1, n_ha)
    left, right = lax.rem(wa + n_wa - 1, n_wa), lax.rem(wa + 1, n_wa)

    own = pl.ds(0, OWN * 128)
    loads = [
        pltpu.make_async_copy(frames.at[0, t], ext.at[2 + t, :, own], local_sem.at[t])
        for t in range(T)
    ]
    loads += [
        pltpu.make_async_copy(cache.at[0, t], ext.at[t, :, own], local_sem.at[T + t])
        for t in range(2)
    ]
    small = [
        pltpu.make_async_copy(source, target, local_sem.at[8 + n])
        for n, (source, target) in enumerate(
            (
                (owners_in, owners),
                (norm_gain_in, norm_gain),
                (conv_bias_in, conv_bias),
                (down_bias_in, down_bias),
                (latent_weight_in, latent_weight),
                (latent_bias_in, latent_bias),
            )
        )
    ]
    load_conv = pltpu.make_async_copy(conv_weight, conv_taps, local_sem.at[6])
    load_down = pltpu.make_async_copy(down_weight, down_taps, local_sem.at[7])
    for load in loads + small + [load_conv, load_down]:
        load.start()

    barrier = pltpu.get_barrier_semaphore()
    greeted = [
        {"ha": up, "wa": wa},
        {"ha": down, "wa": wa},
        {"ha": ha, "wa": left},
        {"ha": ha, "wa": right},
        {"ha": up, "wa": left},
        {"ha": up, "wa": right},
        {"ha": down, "wa": left},
        {"ha": down, "wa": right},
        {"ha": lax.rem(ha + 2, n_ha), "wa": wa},
    ]
    for device in greeted:
        pl.semaphore_signal(
            barrier, inc=1, device_id=device, device_id_type=pl.DeviceIdType.MESH
        )

    def remote(src, dst, index, device):
        return pltpu.make_async_remote_copy(
            src_ref=src,
            dst_ref=dst,
            send_sem=send_sem.at[index],
            recv_sem=recv_sem.at[index],
            device_id=device,
            device_id_type=pl.DeviceIdType.MESH,
        )

    first, last = pl.ds(0, 256), pl.ds((OWN - 1) * 128, 128)
    from_right, from_left = pl.ds(OWN * 128, 256), pl.ds((OWN + 2) * 128, 128)
    col_copies = [
        remote(
            frames.at[0, :, :, first],
            ext.at[pl.ds(2, T), :, from_right],
            6,
            {"ha": ha, "wa": left},
        ),
        remote(
            cache.at[0, :, :, first],
            ext.at[pl.ds(0, 2), :, from_right],
            7,
            {"ha": ha, "wa": left},
        ),
        remote(
            frames.at[0, :, :, last],
            ext.at[pl.ds(2, T), :, from_left],
            8,
            {"ha": ha, "wa": right},
        ),
        remote(
            cache.at[0, :, :, last],
            ext.at[pl.ds(0, 2), :, from_left],
            9,
            {"ha": ha, "wa": right},
        ),
    ]
    pl.semaphore_wait(barrier, len(greeted))
    for copy in col_copies:
        copy.start()
    lane = lax.broadcasted_iota(jnp.int32, (1, 128), 1)

    def column_of(axis):
        index = lax.broadcasted_iota(jnp.int32, (384, 384), axis)
        return sum((index >= edge).astype(jnp.int32) for edge in (96, 192, 288))

    ones[...] = jnp.where(column_of(0) == column_of(1), 1.0, 0.0).astype(BF16)

    for load in small:
        load.wait()
    by_column = (((1,), (1,)), ((), ()))
    by_z = jnp.concatenate([latent_weight[...]] * QB, axis=0)
    rest = down_bias[...]
    pieces = []
    for _ in range(3):
        piece = rest.astype(BF16)
        pieces.append(piece.astype(F32))
        rest = rest - pieces[-1]
    pieces = jnp.concatenate(pieces + [jnp.zeros((13, C), F32)], axis=0).astype(BF16)
    lbias_row = jnp.sum(
        lax.dot_general(pieces, by_z, by_column, preferred_element_type=F32),
        axis=0,
        keepdims=True,
    ) + jnp.concatenate([latent_bias[...]] * QB, axis=1)

    lbias[...] = lbias_row
    bias = conv_bias[...]
    bias = jnp.concatenate([bias[:, 64:]] + [bias] * 3 + [bias[:, :64]], axis=1)
    for j in range(3):
        cbias[j] = bias[:, 128 * j : 128 * (j + 1)]

    gain[...] = jnp.concatenate([norm_gain[...]] * 4, axis=1) * (0.5 * C**0.5)
    row = lax.broadcasted_iota(jnp.int32, (64, 64), 0)
    col = lax.broadcasted_iota(jnp.int32, (64, 64), 1)
    by_col = jnp.broadcast_to(owners[...], (64, 64))
    by_row = jnp.sum(jnp.where(row == col, by_col, 0), axis=1, keepdims=True)
    rank = jnp.sum(jnp.where((by_row == by_col) & (row < col), 1, 0), axis=0, keepdims=True)
    slot = owners[...] * 32 + rank
    slots = lax.broadcasted_iota(jnp.int32, (128, 64), 0)
    selector[...] = jnp.where(slots == slot, 1.0, 0.0).astype(BF16)


    for load in loads:
        load.wait()

    sub = lax.broadcasted_iota(jnp.int32, (8, 128), 0)

    def top_rows(tile):
        tops = [ext[f, pl.ds(0, 16), pl.ds(tile * 128, 128)].astype(F32)[:8] for f in range(6)]
        lo = jnp.zeros((8, 128), F32)
        hi = jnp.zeros((8, 128), F32)
        for t in range(T):
            lo = jnp.where(sub == t, tops[2 + t][0:1], lo)
            lo = jnp.where(sub == 4 + t, tops[2 + t][1:2], lo)
        for t in range(2):
            hi = jnp.where(sub == t, tops[t][0:1], hi)
            hi = jnp.where(sub == 2 + t, tops[t][1:2], hi)
        return lo, hi

    def bottom_rows(tile):
        bots = [ext[f, pl.ds(16, 16), pl.ds(tile * 128, 128)].astype(F32)[8:] for f in range(6)]
        lo = jnp.zeros((8, 128), F32)
        for t in range(T):
            lo = jnp.where(sub == t, bots[2 + t][7:8], lo)
        for t in range(2):
            lo = jnp.where(sub == 4 + t, bots[t][7:8], lo)
        return lo

    def put_pack(target, tile, lo, hi):
        target[:, pl.ds(tile * 128, 128)] = jnp.concatenate([lo, hi], axis=0).astype(BF16)

    above_us, below_us = {"ha": up, "wa": wa}, {"ha": down, "wa": wa}
    half = TOP_TILES // 2 * 128
    row_copies = []

    def send_rows(copy):
        copy.start()
        row_copies.append(copy)

    spread = TOP_TILES // 3
    for tile in range(TOP_TILES):
        lo, hi = top_rows(tile) if tile < TOP_TILES - 1 else (jnp.zeros((8, 128), F32),) * 2
        far_lo, far_hi = top_rows(TOP_TILES - 1 + tile % spread)
        far = (pltpu.roll(far_lo, 4, 0), far_lo, pltpu.roll(far_hi, 4, 0))[tile // spread]
        put_pack(pack_top, tile, lo, jnp.where(sub < 4, hi, far))
        if tile == TOP_TILES // 2 - 1:
            cut = pl.ds(0, half)
            send_rows(remote(pack_top.at[:, cut], below.at[:, cut], 0, above_us))
    cut = pl.ds(half, half)
    send_rows(remote(pack_top.at[:, cut], below.at[:, cut], 10, above_us))
    for tile in range(BOTTOM_TILES):
        far = tile + BOTTOM_TILES
        hi = bottom_rows(far) if far < OWN else jnp.zeros((8, 128), F32)
        put_pack(pack_bot, tile, bottom_rows(tile), hi)
    send_rows(remote(pack_bot, above, 1, below_us))
    for n, tile in enumerate((0, 1, OWN - 1)):
        put_pack(corner_top, n, *top_rows(tile))
        put_pack(corner_bot, n, bottom_rows(tile), jnp.zeros((8, 128), F32))
    one, two = pl.ds(0, 256), pl.ds(256, 128)
    for source, target, index, to in (
        (corner_top, below_side, 2, up),
        (corner_bot, above_side, 4, down),
    ):
        for n, (cut, side) in enumerate(((one, left), (two, right))):
            send_rows(
                remote(source.at[:, cut], target.at[:, cut], index + n, {"ha": to, "wa": side})
            )


    load_conv.wait()
    load_down.wait()

    @pl.loop(0, C // 4, unroll=4)
    def _(g):
        win = lanes(3 * g, 3)
        for weight, count, at in ((conv_taps, 27, 0), (down_taps, 9, 27)):
            x = weight[:, win].astype(F32)
            t0, t1, t2 = (x[:, 128 * j : 128 * (j + 1)] for j in range(3))
            parts = [
                t0,
                jnp.where(lane < 32, pltpu.roll(t0, 32, 1), pltpu.roll(t1, 32, 1)),
                jnp.where(lane < 64, pltpu.roll(t1, 64, 1), pltpu.roll(t2, 64, 1)),
                pltpu.roll(t2, 96, 1),
            ]
            for u in range(4):
                taps[pl.ds(at * C + 4 * g + u, count, C)] = jnp.where(lane < C, parts[u], 0.0)

    @pl.loop(0, 3)
    def _(a):
        for c in range(0, C, 16):
            g = [
                [taps[pl.ds((9 * a + 3 * r + s) * C + c, 16)] for s in range(3)] for r in range(3)
            ]
            for m in range(4):
                if m == 0:
                    w = g[0]
                elif m == 3:
                    w = g[2]
                else:
                    sign = 1.0 if m == 1 else -1.0
                    w = [0.5 * (g[0][s] + g[2][s] + sign * g[1][s]) for s in range(3)]
                zero = jnp.zeros((16, 128), F32)
                by96 = [zero] + [pltpu.roll(x, 96, 1) for x in w]
                by64 = [pltpu.roll(x, 64, 1) for x in w] + [zero]
                by32 = [zero] + [pltpu.roll(x, 32, 1) for x in w]
                w = list(w) + [zero]
                at = m * 1152 + a * 384
                for s in range(4):
                    rows = pl.ds(pl.multiple_of(at + s * 96 + c, 16), 16)
                    wa_w[rows, pl.ds(0, 128)] = jnp.where(lane < 96, w[s], by96[s]).astype(BF16)
                    wa_w[rows, pl.ds(128, 128)] = jnp.where(lane < 64, by96[s], 0.0).astype(BF16)
                    rows = pl.ds(pl.multiple_of(at + (s * 96 + c + 64) % 384, 16), 16)
                    wb_w[rows, pl.ds(0, 128)] = jnp.where(lane < 64, 0.0, by64[s]).astype(BF16)
                    wb_w[rows, pl.ds(128, 128)] = jnp.where(lane < 32, by64[s], by32[s]).astype(BF16)

    fused = lax.dot_general(
        taps[pl.ds(27 * C, 9 * C)][:, :C].astype(BF16),
        by_z,
        by_column,
        preferred_element_type=F32,
    )
    down_w[...] = jnp.zeros((1024, 128), BF16)
    for r in range(3):
        first = (0, 0, 2)[r]
        for col in range(5):
            block = jnp.zeros((C, 128), F32)
            for s in range(3):
                q = col - s
                if q in (0, 2):
                    tap = fused[(3 * r + s) * C : (3 * r + s + 1) * C]
                    place = first + q // 2
                    block = jnp.where((lane >= 16 * place) & (lane < 16 * (place + 1)), tap, block)
            rows = pl.ds((512 if r == 1 else 0) + 32 + C * col, C)
            if r == 2:
                block = block + down_w[rows].astype(F32)
            down_w[rows] = block.astype(BF16)

    has_left = jnp.where(wa == 0, 0.0, 1.0).astype(F32)
    has_right = jnp.where(wa == n_wa - 1, 0.0, 1.0).astype(F32)
    has_above = jnp.where(ha == 0, 0.0, 1.0).astype(F32)
    has_below = jnp.where(ha == n_ha - 1, 0.0, 1.0).astype(F32)

    def activate(x):
        squares = jnp.dot((x * x).astype(BF16), ones[...], preferred_element_type=F32)
        u = x * lax.rsqrt(squares + C * EPS) * gain[...]
        return u + u * jnp.tanh(u)

    def piece(g, f, j, edge):
        x = ext[f, :, lanes(3 * g + j)].astype(F32)
        if edge and g == 13:
            x = x * (has_right if j < 2 else has_left)
        return x

    def groups(gs, edge):
        for g in gs:
            for f in range(T):
                for j in range(3):
                    x = piece(g, 2 + f, j, edge)
                    squares[g, pl.ds(f * TH, TH), pl.ds(128 * j, 128)] = (x * x).astype(BF16)
        sums[pl.ds(gs[0], len(gs))] = jnp.dot(
            squares[pl.ds(gs[0], len(gs))].reshape(len(gs) * T * TH, 384),
            ones[...],
            preferred_element_type=F32,
        ).reshape(len(gs), T * TH, 384)
        for g in gs:
            for f in range(6):
                rows = pl.ds((f - 2) * TH, TH)
                if f >= 2:
                    before = pltpu.roll(piece(max(g - 1, 0), f, 2, edge), 32, 1)
                for j in range(3):
                    tile = 3 * g + j
                    x = piece(g, f, j, edge)
                    if f >= 2:
                        if tile < 40:
                            here = pltpu.roll(x, 32, 1)
                            xf[tile + 1, rows] = jnp.where(lane < 32, before, here)
                            before = here
                        total = sums[g, rows, pl.ds(128 * j, 128)]
                        u = x * lax.rsqrt(total + C * EPS) * gain[:, 128 * j : 128 * (j + 1)]
                        x = u + u * jnp.tanh(u)
                    act[tile, pl.ds(f * FS + 8, TH)] = x
                    d1 = act[tile, pl.ds(f * FS + 8, 16, 2)]
                    d2 = act[tile, pl.ds(f * FS + 9, 16, 2)]
                    inner[0, tile + 1, pl.ds(f * 16, 16)] = (d1 + d2).astype(BF16)
                    inner[1, tile + 1, pl.ds(f * 16, 16)] = (d2 - d1).astype(BF16)

    def tile_a(k, j):
        return 3 * k + j + 1

    def tile_b(i, j):
        return EXT + 1 + i if j == 0 else 3 * i + j - 1

    def join(planes):
        for m in range(2):
            planes[m, 0] = planes[m, EXT]
            for i in range(14):
                later = planes[m, 3 * i + 2]
                sooner = planes[m, 41 if i == 0 else 3 * i - 1]
                planes[m, EXT + 1 + i] = jnp.where(lane < 64, later, sooner)

    def product(planes, m, at, base, tile_of, weights):
        rows = []
        for w in range(7):
            pieces = [
                planes[m, tile_of(base + w, j), pl.ds(a * 16, 64)]
                for a in range(3)
                for j in range(3)
            ]
            rows.append(jnp.concatenate(pieces, axis=1))
        return jnp.dot(
            jnp.concatenate(rows, axis=0),
            weights[pl.ds(at * 1152, 1152)],
            preferred_element_type=F32,
        )

    def inner_products(side, step):
        tile_of, weights = ((tile_a, wa_w), (tile_b, wb_w))[side]
        for m in range(2):
            prod[side, 1 + m, pl.ds(448 * step, 448)] = product(
                inner, m, 1 + m, (6 + side) * step, tile_of, weights
            )

    for n in range(3):
        groups([3 * n, 3 * n + 1, 3 * n + 2], False)
    inner_products(0, 0)
    groups([9, 10, 11], False)

    for copy in col_copies:
        copy.wait_recv()
    groups([12, 13], True)
    join(inner)
    for copy in row_copies:
        copy.wait_recv()
    inner_products(0, 1)

    def halo_rows(tile):
        if tile >= OWN:
            cut = pl.ds((tile - OWN) * 128, 128)
            hi, lo = below_side[:, cut].astype(F32), above_side[:, cut].astype(F32)[:8]
            mask = has_right if tile < OWN + 2 else has_left
            return hi * (has_below * mask), lo * (has_above * mask)
        if tile < TOP_TILES - 1:
            hi = below[:, pl.ds(tile * 128, 128)].astype(F32)
        else:
            far = [
                below[:, pl.ds((spread * n + tile - TOP_TILES + 1) * 128, 128)].astype(F32)[8:]
                for n in range(3)
            ]
            hi = jnp.concatenate(
                [jnp.where(sub < 4, pltpu.roll(far[0], 4, 0), far[1]), pltpu.roll(far[2], 4, 0)],
                axis=0,
            )
        lo = above[:, pl.ds(tile % BOTTOM_TILES * 128, 128)].astype(F32)
        lo = lo[:8] if tile < BOTTOM_TILES else lo[8:]
        return hi * has_below, lo * has_above

    for part in range(2):
        tiles = range(21 * part, 21 * (part + 1))
        rows = [halo_rows(tile) for tile in tiles]
        stacked = [jnp.concatenate([hi[:8], lo], axis=0) for hi, lo in rows]
        activated = activate(
            jnp.concatenate(
                [jnp.concatenate(stacked[3 * n : 3 * n + 3], axis=1) for n in range(7)], axis=0
            )
        )
        before = halo_rows(max(21 * part - 1, 0))[0][:8]
        before = pltpu.roll(before, 32, 1)
        for n, tile in enumerate(tiles):
            hi, lo = rows[n]
            cut = slice(128 * (n % 3), 128 * (n % 3 + 1))
            new = activated[16 * (n // 3) : 16 * (n // 3 + 1), cut]
            act[tile, pl.ds(2 * FS + 40, T, FS)] = new[0:4]
            act[tile, pl.ds(2 * FS + 41, T, FS)] = new[4:8]
            act[tile, pl.ds(2 * FS + 7, T, FS)] = new[8:12]
            act[tile, pl.ds(40, 2, FS)] = hi[8:10]
            act[tile, pl.ds(41, 2, FS)] = hi[10:12]
            act[tile, pl.ds(7, 2, FS)] = lo[4:6]
            here = pltpu.roll(hi[:8], 32, 1)
            x32[tile + 1] = jnp.where(lane < 32, before, here)
            before = here

    def outer_planes(tile):
        for f in range(6):
            d0, d1, d2, d3 = (act[tile, pl.ds(f * FS + 7 + r, 16, 2)] for r in range(4))
            outer[0, tile + 1, pl.ds(f * 16, 16)] = (d0 - d2).astype(BF16)
            outer[1, tile + 1, pl.ds(f * 16, 16)] = (d1 - d3).astype(BF16)

        for a in range(3):
            d0, d1, d2 = (act[tile, pl.ds(a * FS + 39 + r, T, FS)] for r in range(3))
            l32[tile, a, pl.ds(0, T)] = d0 - d2
            l32[tile, 3 + a, pl.ds(0, T)] = d1 + d2
            l32[tile, 6 + a, pl.ds(0, T)] = d2 - d1

    for step in range(2):
        for n in range(21):
            outer_planes(21 * step + n)
        inner_products(1, step)

    join(outer)
    cut_right = jnp.where((lane >= 32) & (wa == n_wa - 1), 0.0, 1.0).astype(F32)

    for step in range(2):
        rows = pl.ds(448 * step, 448)
        for m in range(2):
            prod[0, 3 * m, rows] = product(outer, m, 3 * m, 6 * step, tile_a, wa_w)
            prod[1, 3 * m, rows] = product(outer, m, 3 * m, 7 * step, tile_b, wb_w)

    def epilogue(step):
        def both_rows(side, window, half, at):
            row = 64 * window + (64 if side == 0 and window > 6 else 0) + at
            cut = (pl.ds(row, 32), pl.ds(128 * half, 128))
            p0, p1, p2, p3 = (prod[(side, m) + cut] for m in range(4))
            return p0 + (p1 + p2), (p1 - p2) - p3

        def put(tile, at, values, mask=None):
            for parity in range(2):
                x = xf[tile + 1, pl.ds(2 * at + parity, 32, 2)]
                h = x + values[parity] + cbias[tile % 3]
                h = h if mask is None else h * mask
                hb[parity, tile + 1, pl.ds(at, 32)] = h.astype(BF16)

        for at in range(0, 64, 32):
            for k in range(7 * step, 7 + 6 * step):
                put(3 * k + 1, at, both_rows(0, k, 0, at))
            for i in range(7 * step, 7 * step + 7):
                if i:
                    one, two = both_rows(0, i - 1, 1, at), both_rows(1, i, 0, at)
                    put(3 * i - 1, at, (one[0] + two[0], one[1] + two[1]))
                put(3 * i, at, both_rows(1, i, 1, at), cut_right if i == 13 else None)

    for i in range(14):
        sooner = 40 if i == 0 else 3 * i - 2
        for n in range(9):
            l32[EXT + i, n] = jnp.where(lane < 64, l32[3 * i + 1, n], l32[sooner, n])

    def tile32_a(k, j):
        return 3 * k + j

    def tile32_b(i, j):
        return EXT + i if j == 0 else (41 if i == 0 and j == 1 else 3 * i + j - 2)

    def conv32(tile_of, weights):
        rows = []
        for w in range(14):
            pieces = [l32[tile_of(w, j), n] for n in range(9) for j in range(3)]
            rows.append(jnp.concatenate(pieces, axis=1))
        lhs = jnp.concatenate(rows, axis=0).astype(BF16)
        return jnp.dot(lhs, weights[pl.ds(0, KK * 128)], preferred_element_type=F32)

    acc = conv32(tile32_a, wa_w)
    for k in range(13):
        part = acc[8 * k : 8 * (k + 1)]
        h32[3 * k + 2] = (x32[3 * k + 2] + part[:, :128] + cbias[1]) * has_below
        hp32[k + 1] = part[:, 128:]
    acc = conv32(tile32_b, wb_w)
    for i in range(14):
        part = acc[8 * i : 8 * (i + 1)]
        if i:
            h = x32[3 * i] + part[:, :128] + hp32[i] + cbias[2]
            h32[3 * i] = h * has_below
        h = (x32[3 * i + 1] + part[:, 128:] + cbias[0]) * has_below
        h32[3 * i + 1] = h * cut_right if i == 13 else h

    def downsample(ks):
        rows = []
        for k in ks:
            pieces = [hb[parity, 3 * k + j + 1] for parity in range(2) for j in range(4)]
            rows.append(jnp.concatenate(pieces, axis=1))
        return jnp.dot(jnp.concatenate(rows, axis=0), down_w[...], preferred_element_type=F32)

    epilogue(0)
    main_0 = downsample(range(6))
    epilogue(1)
    main_1 = downsample(range(6, 13))
    rows = [
        jnp.concatenate([h32[3 * min(k, 12) + j + 1] for j in range(4)], axis=1) for k in range(14)
    ]
    extra = jnp.dot(
        jnp.concatenate(rows, axis=0).astype(BF16),
        down_w[pl.ds(0, 512)],
        preferred_element_type=F32,
    )
    blocks = []
    for b in range(4):
        here = jnp.zeros((64, 128), F32)
        over = jnp.zeros((64, 128), F32)
        over32 = jnp.zeros((8, 128), F32)
        for j in range(4 if b < 3 else 1):
            k = 4 * b + j
            fits = (lane >= 32 * j) & (lane < 32 * (j + 1))
            part = main_0[64 * k : 64 * (k + 1)] if k < 6 else main_1[64 * (k - 6) : 64 * (k - 5)]
            turned = pltpu.roll(part, 32 * j, 1) if j else part
            here = jnp.where(fits, turned, here)
            turned = pltpu.roll(part, (32 * j + 96) % 128, 1) if j != 1 else part
            over = jnp.where(fits, turned, over)
            part = extra[8 * k : 8 * (k + 1)]
            turned = pltpu.roll(part, (32 * j + 96) % 128, 1) if j != 1 else part
            over32 = jnp.where(fits, turned, over32)
        for t in range(T):
            vs[t, pl.ds(0, 16)] = over[16 * t : 16 * (t + 1)]
            vs[t, pl.ds(16, 1)] = over32[t : t + 1]
        shifted = jnp.concatenate([vs[t, pl.ds(1, 16)] for t in range(T)], axis=0)
        blocks.append(here + shifted + lbias[...])
    latent = jnp.concatenate(blocks[:3] + [blocks[3][:, :32]], axis=1)
    frame_of = lax.broadcasted_iota(jnp.int32, (64, 1), 0)
    latent = jnp.where(frame_of < valid[0] * 16, latent, 0.0).astype(BF16)

    send[...] = jnp.dot(selector[...], latent, preferred_element_type=F32).astype(BF16)

    here = pl.ds(pl.multiple_of(ha * 32, 32), 32)
    keep = pltpu.make_async_copy(send.at[here], out.at[0, 0, 0, here], local_sem.at[0])
    copies = []
    for d in range(1, n_ha):
        target = lax.rem(ha + d, n_ha)
        copies.append(
            pltpu.make_async_remote_copy(
                src_ref=send.at[pl.ds(pl.multiple_of(target * 32, 32), 32)],
                dst_ref=out.at[0, 0, 0, here],
                send_sem=a2a_send.at[d - 1],
                recv_sem=a2a_recv.at[d - 1],
                device_id={"ha": target, "wa": wa},
                device_id_type=pl.DeviceIdType.MESH,
            )
        )
    for copy in copies:
        copy.start()
    keep.start()
    for copy in row_copies + col_copies:
        copy.wait_send()
    for copy in copies:
        copy.wait()
    keep.wait()


def per_device(
    n_ha,
    n_wa,
    frames,
    cache,
    norm_gain,
    conv_weight,
    conv_bias,
    down_weight,
    down_bias,
    latent_weight,
    latent_bias,
    valid_frames,
    owners,
):
    hbm = pl.BlockSpec(memory_space=pltpu.HBM)
    return pl.pallas_call(
        functools.partial(kernel, n_ha, n_wa),
        out_shape=jax.ShapeDtypeStruct((1, 1, 1, 128, 416), BF16),
        in_specs=[hbm, hbm, hbm, pl.BlockSpec(memory_space=pltpu.SMEM)] + [hbm] * 7,
        out_specs=hbm,
        scratch_shapes=[
            pltpu.VMEM((1, 64), jnp.int32),
            pltpu.VMEM((1, C), F32),
            pltpu.VMEM((1, C), F32),
            pltpu.VMEM((1, C), F32),
            pltpu.VMEM((Z, C), BF16),
            pltpu.VMEM((1, Z), F32),
            pltpu.VMEM((128, 64), BF16),
            pltpu.VMEM((6, TH, EXT * 128), BF16),
            pltpu.VMEM((16, TOP_TILES * 128), BF16),
            pltpu.VMEM((16, BOTTOM_TILES * 128), BF16),
            pltpu.VMEM((16, 384), BF16),
            pltpu.VMEM((16, 384), BF16),
            pltpu.VMEM((16, BOTTOM_TILES * 128), BF16),
            pltpu.VMEM((16, 384), BF16),
            pltpu.VMEM((16, TOP_TILES * 128), BF16),
            pltpu.VMEM((16, 384), BF16),
            pltpu.VMEM((EXT, 6 * FS, 128), F32),
            pltpu.VMEM((41, T * TH, 128), F32),
            pltpu.VMEM((2, EXT + 15, 96, 128), BF16),
            pltpu.VMEM((2, EXT + 15, 96, 128), BF16),
            pltpu.VMEM((384, 384), BF16),
            pltpu.VMEM((14, T * TH, 384), BF16),
            pltpu.VMEM((14, T * TH, 384), F32),
            pltpu.VMEM((2, 4, 896, 256), F32),
            pltpu.VMEM((2, 41, 64, 128), BF16),
            pltpu.VMEM((EXT + 14, 9, 8, 128), F32),
            pltpu.VMEM((EXT + 1, 8, 128), F32),
            pltpu.VMEM((14, 8, 128), F32),
            pltpu.VMEM((41, 8, 128), F32),
            pltpu.VMEM((T, 24, 128), F32),
            pltpu.VMEM((27, C * C), BF16),
            pltpu.VMEM((9, C * C), BF16),
            pltpu.VMEM((36 * C, 128), F32),
            pltpu.VMEM((4608, 256), BF16),
            pltpu.VMEM((4608, 256), BF16),
            pltpu.VMEM((1024, 128), BF16),
            pltpu.VMEM((1, 384), F32),
            pltpu.VMEM((3, 1, 128), F32),
            pltpu.VMEM((1, 128), F32),
            pltpu.VMEM((128, 416), BF16),
            pltpu.SemaphoreType.DMA((14,)),
            pltpu.SemaphoreType.DMA((11,)),
            pltpu.SemaphoreType.DMA((11,)),
            pltpu.SemaphoreType.DMA((n_ha - 1,)),
            pltpu.SemaphoreType.DMA((n_ha - 1,)),
        ],
        compiler_params=pltpu.CompilerParams(
            collective_id=0, has_side_effects=True, vmem_limit_bytes=56 * 2**20
        ),
        name="encoder_step",
    )(
        frames,
        cache,
        owners.reshape(1, 64),
        valid_frames,
        norm_gain.reshape(1, C),
        conv_weight,
        conv_bias.reshape(1, C),
        down_weight,
        down_bias.reshape(1, C),
        latent_weight.T,
        latent_bias.reshape(1, Z),
    )


def solution(mesh):
    in_specs = (
        P("ba", None, "ha", "wa"),
        P("ba", None, "ha", "wa"),
        P(),
        P(),
        P(),
        P(),
        P(),
        P(),
        P(),
        P("ba"),
        P("ba", "ha", "wa", None, None),
    )
    out_specs = P("ba", "ha", "wa", None, None)
    return jax.shard_map(
        functools.partial(per_device, mesh.shape["ha"], mesh.shape["wa"]),
        mesh=mesh,
        in_specs=in_specs,
        out_specs=out_specs,
        check_vma=False,
    )
```

```python
import functools

import jax
import jax.numpy as jnp
import numpy as np
from jax import lax
from jax.experimental import pallas as pl
from jax.experimental.pallas import tpu as pltpu
from jax.sharding import PartitionSpec as P

EPS = 1e-06
C = 96
Z = 16
T = 4
TH = 32
TW = 52
TOP_TILES = 30
BOTTOM_TILES = 20
OWN = 39
EXT = 42
FS = 48
KK = 27
QB = 8
F32 = jnp.float32
BF16 = jnp.bfloat16


def lanes(tile, count=1):
    return pl.ds(pl.multiple_of(tile * 128, 128), count * 128)


def kernel(
    n_ha,
    n_wa,
    frames,
    cache,
    owners_in,
    valid,
    norm_gain_in,
    conv_weight,
    conv_bias_in,
    down_weight,
    down_bias_in,
    latent_weight_in,
    latent_bias_in,
    out,
    owners,
    norm_gain,
    conv_bias,
    down_bias,
    latent_weight,
    latent_bias,
    selector,
    ext,
    pack_top,
    pack_bot,
    corner_top,
    corner_bot,
    above,
    above_side,
    below,
    below_side,
    act,
    xf,
    inner,
    outer,
    ones,
    squares,
    sums,
    prod,
    hb,
    l32,
    x32,
    hp32,
    h32,
    vs,
    conv_taps,
    down_taps,
    taps,
    wa_w,
    wb_w,
    down_w,
    gain,
    cbias,
    lbias,
    send,
    local_sem,
    send_sem,
    recv_sem,
    a2a_send,
    a2a_recv,
):
    ha, wa = lax.axis_index("ha"), lax.axis_index("wa")
    up, down = lax.rem(ha + n_ha - 1, n_ha), lax.rem(ha + 1, n_ha)
    left, right = lax.rem(wa + n_wa - 1, n_wa), lax.rem(wa + 1, n_wa)

    own = pl.ds(0, OWN * 128)
    loads = [
        pltpu.make_async_copy(frames.at[0, t], ext.at[2 + t, :, own], local_sem.at[t])
        for t in range(T)
    ]
    loads += [
        pltpu.make_async_copy(cache.at[0, t], ext.at[t, :, own], local_sem.at[T + t])
        for t in range(2)
    ]
    small = [
        pltpu.make_async_copy(source, target, local_sem.at[8 + n])
        for n, (source, target) in enumerate(
            (
                (owners_in, owners),
                (norm_gain_in, norm_gain),
                (conv_bias_in, conv_bias),
                (down_bias_in, down_bias),
                (latent_weight_in, latent_weight),
                (latent_bias_in, latent_bias),
            )
        )
    ]
    load_conv = pltpu.make_async_copy(conv_weight, conv_taps, local_sem.at[6])
    load_down = pltpu.make_async_copy(down_weight, down_taps, local_sem.at[7])
    for load in loads + small + [load_conv, load_down]:
        load.start()

    barrier = pltpu.get_barrier_semaphore()
    greeted = [
        {"ha": up, "wa": wa},
        {"ha": down, "wa": wa},
        {"ha": ha, "wa": left},
        {"ha": ha, "wa": right},
        {"ha": up, "wa": left},
        {"ha": up, "wa": right},
        {"ha": down, "wa": left},
        {"ha": down, "wa": right},
        {"ha": lax.rem(ha + 2, n_ha), "wa": wa},
    ]
    for device in greeted:
        pl.semaphore_signal(
            barrier, inc=1, device_id=device, device_id_type=pl.DeviceIdType.MESH
        )

    def remote(src, dst, index, device):
        return pltpu.make_async_remote_copy(
            src_ref=src,
            dst_ref=dst,
            send_sem=send_sem.at[index],
            recv_sem=recv_sem.at[index],
            device_id=device,
            device_id_type=pl.DeviceIdType.MESH,
        )

    first, last = pl.ds(0, 256), pl.ds((OWN - 1) * 128, 128)
    from_right, from_left = pl.ds(OWN * 128, 256), pl.ds((OWN + 2) * 128, 128)
    col_copies = [
        remote(
            frames.at[0, :, :, first],
            ext.at[pl.ds(2, T), :, from_right],
            6,
            {"ha": ha, "wa": left},
        ),
        remote(
            cache.at[0, :, :, first],
            ext.at[pl.ds(0, 2), :, from_right],
            7,
            {"ha": ha, "wa": left},
        ),
        remote(
            frames.at[0, :, :, last],
            ext.at[pl.ds(2, T), :, from_left],
            8,
            {"ha": ha, "wa": right},
        ),
        remote(
            cache.at[0, :, :, last],
            ext.at[pl.ds(0, 2), :, from_left],
            9,
            {"ha": ha, "wa": right},
        ),
    ]
    pl.semaphore_wait(barrier, len(greeted))
    for copy in col_copies:
        copy.start()
    lane = lax.broadcasted_iota(jnp.int32, (1, 128), 1)

    def column_of(axis):
        index = lax.broadcasted_iota(jnp.int32, (384, 384), axis)
        return sum((index >= edge).astype(jnp.int32) for edge in (96, 192, 288))

    ones[...] = jnp.where(column_of(0) == column_of(1), 1.0, 0.0).astype(BF16)

    for load in small:
        load.wait()
    by_column = (((1,), (1,)), ((), ()))
    by_z = jnp.concatenate([latent_weight[...]] * QB, axis=0)
    rest = down_bias[...]
    pieces = []
    for _ in range(3):
        piece = rest.astype(BF16)
        pieces.append(piece.astype(F32))
        rest = rest - pieces[-1]
    pieces = jnp.concatenate(pieces + [jnp.zeros((13, C), F32)], axis=0).astype(BF16)
    lbias_row = jnp.sum(
        lax.dot_general(pieces, by_z, by_column, preferred_element_type=F32),
        axis=0,
        keepdims=True,
    ) + jnp.concatenate([latent_bias[...]] * QB, axis=1)

    lbias[...] = lbias_row
    bias = conv_bias[...]
    bias = jnp.concatenate([bias[:, 64:]] + [bias] * 3 + [bias[:, :64]], axis=1)
    for j in range(3):
        cbias[j] = bias[:, 128 * j : 128 * (j + 1)]

    gain[...] = jnp.concatenate([norm_gain[...]] * 4, axis=1) * (0.5 * C**0.5)
    row = lax.broadcasted_iota(jnp.int32, (64, 64), 0)
    col = lax.broadcasted_iota(jnp.int32, (64, 64), 1)
    by_col = jnp.broadcast_to(owners[...], (64, 64))
    by_row = jnp.sum(jnp.where(row == col, by_col, 0), axis=1, keepdims=True)
    rank = jnp.sum(jnp.where((by_row == by_col) & (row < col), 1, 0), axis=0, keepdims=True)
    slot = owners[...] * 32 + rank
    slots = lax.broadcasted_iota(jnp.int32, (128, 64), 0)
    selector[...] = jnp.where(slots == slot, 1.0, 0.0).astype(BF16)


    for load in loads:
        load.wait()

    sub = lax.broadcasted_iota(jnp.int32, (8, 128), 0)

    def top_rows(tile):
        tops = [ext[f, pl.ds(0, 16), pl.ds(tile * 128, 128)].astype(F32)[:8] for f in range(6)]
        lo = jnp.zeros((8, 128), F32)
        hi = jnp.zeros((8, 128), F32)
        for t in range(T):
            lo = jnp.where(sub == t, tops[2 + t][0:1], lo)
            lo = jnp.where(sub == 4 + t, tops[2 + t][1:2], lo)
        for t in range(2):
            hi = jnp.where(sub == t, tops[t][0:1], hi)
            hi = jnp.where(sub == 2 + t, tops[t][1:2], hi)
        return lo, hi

    def bottom_rows(tile):
        bots = [ext[f, pl.ds(16, 16), pl.ds(tile * 128, 128)].astype(F32)[8:] for f in range(6)]
        lo = jnp.zeros((8, 128), F32)
        for t in range(T):
            lo = jnp.where(sub == t, bots[2 + t][7:8], lo)
        for t in range(2):
            lo = jnp.where(sub == 4 + t, bots[t][7:8], lo)
        return lo

    def put_pack(target, tile, lo, hi):
        target[:, pl.ds(tile * 128, 128)] = jnp.concatenate([lo, hi], axis=0).astype(BF16)

    above_us, below_us = {"ha": up, "wa": wa}, {"ha": down, "wa": wa}
    half = TOP_TILES // 2 * 128
    row_copies = []

    def send_rows(copy):
        copy.start()
        row_copies.append(copy)

    spread = TOP_TILES // 3
    for tile in range(TOP_TILES):
        lo, hi = top_rows(tile) if tile < TOP_TILES - 1 else (jnp.zeros((8, 128), F32),) * 2
        far_lo, far_hi = top_rows(TOP_TILES - 1 + tile % spread)
        far = (pltpu.roll(far_lo, 4, 0), far_lo, pltpu.roll(far_hi, 4, 0))[tile // spread]
        put_pack(pack_top, tile, lo, jnp.where(sub < 4, hi, far))
        if tile == TOP_TILES // 2 - 1:
            cut = pl.ds(0, half)
            send_rows(remote(pack_top.at[:, cut], below.at[:, cut], 0, above_us))
    cut = pl.ds(half, half)
    send_rows(remote(pack_top.at[:, cut], below.at[:, cut], 10, above_us))
    for tile in range(BOTTOM_TILES):
        far = tile + BOTTOM_TILES
        hi = bottom_rows(far) if far < OWN else jnp.zeros((8, 128), F32)
        put_pack(pack_bot, tile, bottom_rows(tile), hi)
    send_rows(remote(pack_bot, above, 1, below_us))
    for n, tile in enumerate((0, 1, OWN - 1)):
        put_pack(corner_top, n, *top_rows(tile))
        put_pack(corner_bot, n, bottom_rows(tile), jnp.zeros((8, 128), F32))
    one, two = pl.ds(0, 256), pl.ds(256, 128)
    for source, target, index, to in (
        (corner_top, below_side, 2, up),
        (corner_bot, above_side, 4, down),
    ):
        for n, (cut, side) in enumerate(((one, left), (two, right))):
            send_rows(
                remote(source.at[:, cut], target.at[:, cut], index + n, {"ha": to, "wa": side})
            )


    load_conv.wait()
    load_down.wait()

    for g in range(C // 4):
        win = lanes(3 * g, 3)
        for weight, count, at in ((conv_taps, 27, 0), (down_taps, 9, 27)):
            x = weight[:, win].astype(F32)
            t0, t1, t2 = (x[:, 128 * j : 128 * (j + 1)] for j in range(3))
            parts = [
                t0,
                jnp.where(lane < 32, pltpu.roll(t0, 32, 1), pltpu.roll(t1, 32, 1)),
                jnp.where(lane < 64, pltpu.roll(t1, 64, 1), pltpu.roll(t2, 64, 1)),
                pltpu.roll(t2, 96, 1),
            ]
            for u in range(4):
                taps[pl.ds(at * C + 4 * g + u, count, C)] = jnp.where(lane < C, parts[u], 0.0)

    for a in range(3):
        for c in range(0, C, 16):
            g = [
                [taps[pl.ds((9 * a + 3 * r + s) * C + c, 16)] for s in range(3)] for r in range(3)
            ]
            for m in range(4):
                if m == 0:
                    w = g[0]
                elif m == 3:
                    w = g[2]
                else:
                    sign = 1.0 if m == 1 else -1.0
                    w = [0.5 * (g[0][s] + g[2][s] + sign * g[1][s]) for s in range(3)]
                zero = jnp.zeros((16, 128), F32)
                by96 = [zero] + [pltpu.roll(x, 96, 1) for x in w]
                by64 = [pltpu.roll(x, 64, 1) for x in w] + [zero]
                by32 = [zero] + [pltpu.roll(x, 32, 1) for x in w]
                w = list(w) + [zero]
                at = m * 1152 + a * 384
                for s in range(4):
                    rows = pl.ds(pl.multiple_of(at + s * 96 + c, 16), 16)
                    wa_w[rows, pl.ds(0, 128)] = jnp.where(lane < 96, w[s], by96[s]).astype(BF16)
                    wa_w[rows, pl.ds(128, 128)] = jnp.where(lane < 64, by96[s], 0.0).astype(BF16)
                    rows = pl.ds(pl.multiple_of(at + (s * 96 + c + 64) % 384, 16), 16)
                    wb_w[rows, pl.ds(0, 128)] = jnp.where(lane < 64, 0.0, by64[s]).astype(BF16)
                    wb_w[rows, pl.ds(128, 128)] = jnp.where(lane < 32, by64[s], by32[s]).astype(BF16)

    fused = lax.dot_general(
        taps[pl.ds(27 * C, 9 * C)][:, :C].astype(BF16),
        by_z,
        by_column,
        preferred_element_type=F32,
    )
    down_w[...] = jnp.zeros((1024, 128), BF16)
    for r in range(3):
        first = (0, 0, 2)[r]
        for col in range(5):
            block = jnp.zeros((C, 128), F32)
            for s in range(3):
                q = col - s
                if q in (0, 2):
                    tap = fused[(3 * r + s) * C : (3 * r + s + 1) * C]
                    place = first + q // 2
                    block = jnp.where((lane >= 16 * place) & (lane < 16 * (place + 1)), tap, block)
            rows = pl.ds((512 if r == 1 else 0) + 32 + C * col, C)
            if r == 2:
                block = block + down_w[rows].astype(F32)
            down_w[rows] = block.astype(BF16)

    has_left = jnp.where(wa == 0, 0.0, 1.0).astype(F32)
    has_right = jnp.where(wa == n_wa - 1, 0.0, 1.0).astype(F32)
    has_above = jnp.where(ha == 0, 0.0, 1.0).astype(F32)
    has_below = jnp.where(ha == n_ha - 1, 0.0, 1.0).astype(F32)

    def activate(x):
        squares = jnp.dot((x * x).astype(BF16), ones[...], preferred_element_type=F32)
        u = x * lax.rsqrt(squares + C * EPS) * gain[...]
        return u + u * jnp.tanh(u)

    def piece(g, f, j, edge):
        x = ext[f, :, lanes(3 * g + j)].astype(F32)
        if edge and g == 13:
            x = x * (has_right if j < 2 else has_left)
        return x

    def groups(gs, edge):
        for g in gs:
            for f in range(T):
                for j in range(3):
                    x = piece(g, 2 + f, j, edge)
                    squares[g, pl.ds(f * TH, TH), pl.ds(128 * j, 128)] = (x * x).astype(BF16)
        sums[pl.ds(gs[0], len(gs))] = jnp.dot(
            squares[pl.ds(gs[0], len(gs))].reshape(len(gs) * T * TH, 384),
            ones[...],
            preferred_element_type=F32,
        ).reshape(len(gs), T * TH, 384)
        for g in gs:
            for f in range(6):
                rows = pl.ds((f - 2) * TH, TH)
                if f >= 2:
                    before = pltpu.roll(piece(max(g - 1, 0), f, 2, edge), 32, 1)
                for j in range(3):
                    tile = 3 * g + j
                    x = piece(g, f, j, edge)
                    if f >= 2:
                        if tile < 40:
                            here = pltpu.roll(x, 32, 1)
                            xf[tile + 1, rows] = jnp.where(lane < 32, before, here)
                            before = here
                        total = sums[g, rows, pl.ds(128 * j, 128)]
                        u = x * lax.rsqrt(total + C * EPS) * gain[:, 128 * j : 128 * (j + 1)]
                        x = u + u * jnp.tanh(u)
                    act[tile, pl.ds(f * FS + 8, TH)] = x
                    d1 = act[tile, pl.ds(f * FS + 8, 16, 2)]
                    d2 = act[tile, pl.ds(f * FS + 9, 16, 2)]
                    inner[0, tile + 1, pl.ds(f * 16, 16)] = (d1 + d2).astype(BF16)
                    inner[1, tile + 1, pl.ds(f * 16, 16)] = (d2 - d1).astype(BF16)

    def tile_a(k, j):
        return 3 * k + j + 1

    def tile_b(i, j):
        return EXT + 1 + i if j == 0 else 3 * i + j - 1

    def join(planes):
        for m in range(2):
            planes[m, 0] = planes[m, EXT]
            for i in range(14):
                later = planes[m, 3 * i + 2]
                sooner = planes[m, 41 if i == 0 else 3 * i - 1]
                planes[m, EXT + 1 + i] = jnp.where(lane < 64, later, sooner)

    def product(planes, m, at, base, tile_of, weights):
        rows = []
        for w in range(7):
            pieces = [
                planes[m, tile_of(base + w, j), pl.ds(a * 16, 64)]
                for a in range(3)
                for j in range(3)
            ]
            rows.append(jnp.concatenate(pieces, axis=1))
        return jnp.dot(
            jnp.concatenate(rows, axis=0),
            weights[pl.ds(at * 1152, 1152)],
            preferred_element_type=F32,
        )

    def inner_products(side, step):
        tile_of, weights = ((tile_a, wa_w), (tile_b, wb_w))[side]
        for m in range(2):
            prod[side, 1 + m, pl.ds(448 * step, 448)] = product(
                inner, m, 1 + m, (6 + side) * step, tile_of, weights
            )

    for n in range(3):
        groups([3 * n, 3 * n + 1, 3 * n + 2], False)
    inner_products(0, 0)
    groups([9, 10, 11], False)

    for copy in col_copies:
        copy.wait_recv()
    groups([12, 13], True)
    join(inner)
    for copy in row_copies:
        copy.wait_recv()
    inner_products(0, 1)

    def halo_rows(tile):
        if tile >= OWN:
            cut = pl.ds((tile - OWN) * 128, 128)
            hi, lo = below_side[:, cut].astype(F32), above_side[:, cut].astype(F32)[:8]
            mask = has_right if tile < OWN + 2 else has_left
            return hi * (has_below * mask), lo * (has_above * mask)
        if tile < TOP_TILES - 1:
            hi = below[:, pl.ds(tile * 128, 128)].astype(F32)
        else:
            far = [
                below[:, pl.ds((spread * n + tile - TOP_TILES + 1) * 128, 128)].astype(F32)[8:]
                for n in range(3)
            ]
            hi = jnp.concatenate(
                [jnp.where(sub < 4, pltpu.roll(far[0], 4, 0), far[1]), pltpu.roll(far[2], 4, 0)],
                axis=0,
            )
        lo = above[:, pl.ds(tile % BOTTOM_TILES * 128, 128)].astype(F32)
        lo = lo[:8] if tile < BOTTOM_TILES else lo[8:]
        return hi * has_below, lo * has_above

    for part in range(2):
        tiles = range(21 * part, 21 * (part + 1))
        rows = [halo_rows(tile) for tile in tiles]
        stacked = [jnp.concatenate([hi[:8], lo], axis=0) for hi, lo in rows]
        activated = activate(
            jnp.concatenate(
                [jnp.concatenate(stacked[3 * n : 3 * n + 3], axis=1) for n in range(7)], axis=0
            )
        )
        before = halo_rows(max(21 * part - 1, 0))[0][:8]
        before = pltpu.roll(before, 32, 1)
        for n, tile in enumerate(tiles):
            hi, lo = rows[n]
            cut = slice(128 * (n % 3), 128 * (n % 3 + 1))
            new = activated[16 * (n // 3) : 16 * (n // 3 + 1), cut]
            act[tile, pl.ds(2 * FS + 40, T, FS)] = new[0:4]
            act[tile, pl.ds(2 * FS + 41, T, FS)] = new[4:8]
            act[tile, pl.ds(2 * FS + 7, T, FS)] = new[8:12]
            act[tile, pl.ds(40, 2, FS)] = hi[8:10]
            act[tile, pl.ds(41, 2, FS)] = hi[10:12]
            act[tile, pl.ds(7, 2, FS)] = lo[4:6]
            here = pltpu.roll(hi[:8], 32, 1)
            x32[tile + 1] = jnp.where(lane < 32, before, here)
            before = here

    def outer_planes(tile):
        for f in range(6):
            d0, d1, d2, d3 = (act[tile, pl.ds(f * FS + 7 + r, 16, 2)] for r in range(4))
            outer[0, tile + 1, pl.ds(f * 16, 16)] = (d0 - d2).astype(BF16)
            outer[1, tile + 1, pl.ds(f * 16, 16)] = (d1 - d3).astype(BF16)

        for a in range(3):
            d0, d1, d2 = (act[tile, pl.ds(a * FS + 39 + r, T, FS)] for r in range(3))
            l32[tile, a, pl.ds(0, T)] = d0 - d2
            l32[tile, 3 + a, pl.ds(0, T)] = d1 + d2
            l32[tile, 6 + a, pl.ds(0, T)] = d2 - d1

    for step in range(2):
        for n in range(21):
            outer_planes(21 * step + n)
        inner_products(1, step)

    join(outer)
    cut_right = jnp.where((lane >= 32) & (wa == n_wa - 1), 0.0, 1.0).astype(F32)

    for step in range(2):
        rows = pl.ds(448 * step, 448)
        for m in range(2):
            prod[0, 3 * m, rows] = product(outer, m, 3 * m, 6 * step, tile_a, wa_w)
            prod[1, 3 * m, rows] = product(outer, m, 3 * m, 7 * step, tile_b, wb_w)

    def epilogue(step):
        def both_rows(side, window, half, at):
            row = 64 * window + (64 if side == 0 and window > 6 else 0) + at
            cut = (pl.ds(row, 32), pl.ds(128 * half, 128))
            p0, p1, p2, p3 = (prod[(side, m) + cut] for m in range(4))
            return p0 + (p1 + p2), (p1 - p2) - p3

        def put(tile, at, values, mask=None):
            for parity in range(2):
                x = xf[tile + 1, pl.ds(2 * at + parity, 32, 2)]
                h = x + values[parity] + cbias[tile % 3]
                h = h if mask is None else h * mask
                hb[parity, tile + 1, pl.ds(at, 32)] = h.astype(BF16)

        for at in range(0, 64, 32):
            for k in range(7 * step, 7 + 6 * step):
                put(3 * k + 1, at, both_rows(0, k, 0, at))
            for i in range(7 * step, 7 * step + 7):
                if i:
                    one, two = both_rows(0, i - 1, 1, at), both_rows(1, i, 0, at)
                    put(3 * i - 1, at, (one[0] + two[0], one[1] + two[1]))
                put(3 * i, at, both_rows(1, i, 1, at), cut_right if i == 13 else None)

    for i in range(14):
        sooner = 40 if i == 0 else 3 * i - 2
        for n in range(9):
            l32[EXT + i, n] = jnp.where(lane < 64, l32[3 * i + 1, n], l32[sooner, n])

    def tile32_a(k, j):
        return 3 * k + j

    def tile32_b(i, j):
        return EXT + i if j == 0 else (41 if i == 0 and j == 1 else 3 * i + j - 2)

    def conv32(tile_of, weights):
        rows = []
        for w in range(14):
            pieces = [l32[tile_of(w, j), n] for n in range(9) for j in range(3)]
            rows.append(jnp.concatenate(pieces, axis=1))
        lhs = jnp.concatenate(rows, axis=0).astype(BF16)
        return jnp.dot(lhs, weights[pl.ds(0, KK * 128)], preferred_element_type=F32)

    acc = conv32(tile32_a, wa_w)
    for k in range(13):
        part = acc[8 * k : 8 * (k + 1)]
        h32[3 * k + 2] = (x32[3 * k + 2] + part[:, :128] + cbias[1]) * has_below
        hp32[k + 1] = part[:, 128:]
    acc = conv32(tile32_b, wb_w)
    for i in range(14):
        part = acc[8 * i : 8 * (i + 1)]
        if i:
            h = x32[3 * i] + part[:, :128] + hp32[i] + cbias[2]
            h32[3 * i] = h * has_below
        h = (x32[3 * i + 1] + part[:, 128:] + cbias[0]) * has_below
        h32[3 * i + 1] = h * cut_right if i == 13 else h

    def downsample(ks):
        rows = []
        for k in ks:
            pieces = [hb[parity, 3 * k + j + 1] for parity in range(2) for j in range(4)]
            rows.append(jnp.concatenate(pieces, axis=1))
        return jnp.dot(jnp.concatenate(rows, axis=0), down_w[...], preferred_element_type=F32)

    epilogue(0)
    main_0 = downsample(range(6))
    epilogue(1)
    main_1 = downsample(range(6, 13))
    rows = [
        jnp.concatenate([h32[3 * min(k, 12) + j + 1] for j in range(4)], axis=1) for k in range(14)
    ]
    extra = jnp.dot(
        jnp.concatenate(rows, axis=0).astype(BF16),
        down_w[pl.ds(0, 512)],
        preferred_element_type=F32,
    )
    blocks = []
    for b in range(4):
        here = jnp.zeros((64, 128), F32)
        over = jnp.zeros((64, 128), F32)
        over32 = jnp.zeros((8, 128), F32)
        for j in range(4 if b < 3 else 1):
            k = 4 * b + j
            fits = (lane >= 32 * j) & (lane < 32 * (j + 1))
            part = main_0[64 * k : 64 * (k + 1)] if k < 6 else main_1[64 * (k - 6) : 64 * (k - 5)]
            turned = pltpu.roll(part, 32 * j, 1) if j else part
            here = jnp.where(fits, turned, here)
            turned = pltpu.roll(part, (32 * j + 96) % 128, 1) if j != 1 else part
            over = jnp.where(fits, turned, over)
            part = extra[8 * k : 8 * (k + 1)]
            turned = pltpu.roll(part, (32 * j + 96) % 128, 1) if j != 1 else part
            over32 = jnp.where(fits, turned, over32)
        for t in range(T):
            vs[t, pl.ds(0, 16)] = over[16 * t : 16 * (t + 1)]
            vs[t, pl.ds(16, 1)] = over32[t : t + 1]
        shifted = jnp.concatenate([vs[t, pl.ds(1, 16)] for t in range(T)], axis=0)
        blocks.append(here + shifted + lbias[...])
    latent = jnp.concatenate(blocks[:3] + [blocks[3][:, :32]], axis=1)
    frame_of = lax.broadcasted_iota(jnp.int32, (64, 1), 0)
    latent = jnp.where(frame_of < valid[0] * 16, latent, 0.0).astype(BF16)

    send[...] = jnp.dot(selector[...], latent, preferred_element_type=F32).astype(BF16)

    here = pl.ds(pl.multiple_of(ha * 32, 32), 32)
    keep = pltpu.make_async_copy(send.at[here], out.at[0, 0, 0, here], local_sem.at[0])
    copies = []
    for d in range(1, n_ha):
        target = lax.rem(ha + d, n_ha)
        copies.append(
            pltpu.make_async_remote_copy(
                src_ref=send.at[pl.ds(pl.multiple_of(target * 32, 32), 32)],
                dst_ref=out.at[0, 0, 0, here],
                send_sem=a2a_send.at[d - 1],
                recv_sem=a2a_recv.at[d - 1],
                device_id={"ha": target, "wa": wa},
                device_id_type=pl.DeviceIdType.MESH,
            )
        )
    for copy in copies:
        copy.start()
    keep.start()
    for copy in row_copies + col_copies:
        copy.wait_send()
    for copy in copies:
        copy.wait()
    keep.wait()


def per_device(
    n_ha,
    n_wa,
    frames,
    cache,
    norm_gain,
    conv_weight,
    conv_bias,
    down_weight,
    down_bias,
    latent_weight,
    latent_bias,
    valid_frames,
    owners,
):
    hbm = pl.BlockSpec(memory_space=pltpu.HBM)
    return pl.pallas_call(
        functools.partial(kernel, n_ha, n_wa),
        out_shape=jax.ShapeDtypeStruct((1, 1, 1, 128, 416), BF16),
        in_specs=[hbm, hbm, hbm, pl.BlockSpec(memory_space=pltpu.SMEM)] + [hbm] * 7,
        out_specs=hbm,
        scratch_shapes=[
            pltpu.VMEM((1, 64), jnp.int32),
            pltpu.VMEM((1, C), F32),
            pltpu.VMEM((1, C), F32),
            pltpu.VMEM((1, C), F32),
            pltpu.VMEM((Z, C), BF16),
            pltpu.VMEM((1, Z), F32),
            pltpu.VMEM((128, 64), BF16),
            pltpu.VMEM((6, TH, EXT * 128), BF16),
            pltpu.VMEM((16, TOP_TILES * 128), BF16),
            pltpu.VMEM((16, BOTTOM_TILES * 128), BF16),
            pltpu.VMEM((16, 384), BF16),
            pltpu.VMEM((16, 384), BF16),
            pltpu.VMEM((16, BOTTOM_TILES * 128), BF16),
            pltpu.VMEM((16, 384), BF16),
            pltpu.VMEM((16, TOP_TILES * 128), BF16),
            pltpu.VMEM((16, 384), BF16),
            pltpu.VMEM((EXT, 6 * FS, 128), F32),
            pltpu.VMEM((41, T * TH, 128), F32),
            pltpu.VMEM((2, EXT + 15, 96, 128), BF16),
            pltpu.VMEM((2, EXT + 15, 96, 128), BF16),
            pltpu.VMEM((384, 384), BF16),
            pltpu.VMEM((14, T * TH, 384), BF16),
            pltpu.VMEM((14, T * TH, 384), F32),
            pltpu.VMEM((2, 4, 896, 256), F32),
            pltpu.VMEM((2, 41, 64, 128), BF16),
            pltpu.VMEM((EXT + 14, 9, 8, 128), F32),
            pltpu.VMEM((EXT + 1, 8, 128), F32),
            pltpu.VMEM((14, 8, 128), F32),
            pltpu.VMEM((41, 8, 128), F32),
            pltpu.VMEM((T, 24, 128), F32),
            pltpu.VMEM((27, C * C), BF16),
            pltpu.VMEM((9, C * C), BF16),
            pltpu.VMEM((36 * C, 128), F32),
            pltpu.VMEM((4608, 256), BF16),
            pltpu.VMEM((4608, 256), BF16),
            pltpu.VMEM((1024, 128), BF16),
            pltpu.VMEM((1, 384), F32),
            pltpu.VMEM((3, 1, 128), F32),
            pltpu.VMEM((1, 128), F32),
            pltpu.VMEM((128, 416), BF16),
            pltpu.SemaphoreType.DMA((14,)),
            pltpu.SemaphoreType.DMA((11,)),
            pltpu.SemaphoreType.DMA((11,)),
            pltpu.SemaphoreType.DMA((n_ha - 1,)),
            pltpu.SemaphoreType.DMA((n_ha - 1,)),
        ],
        compiler_params=pltpu.CompilerParams(
            collective_id=0, has_side_effects=True, vmem_limit_bytes=56 * 2**20
        ),
        name="encoder_step",
    )(
        frames,
        cache,
        owners.reshape(1, 64),
        valid_frames,
        norm_gain.reshape(1, C),
        conv_weight,
        conv_bias.reshape(1, C),
        down_weight,
        down_bias.reshape(1, C),
        latent_weight.T,
        latent_bias.reshape(1, Z),
    )


def solution(mesh):
    in_specs = (
        P("ba", None, "ha", "wa"),
        P("ba", None, "ha", "wa"),
        P(),
        P(),
        P(),
        P(),
        P(),
        P(),
        P(),
        P("ba"),
        P("ba", "ha", "wa", None, None),
    )
    out_specs = P("ba", "ha", "wa", None, None)
    return jax.shard_map(
        functools.partial(per_device, mesh.shape["ha"], mesh.shape["wa"]),
        mesh=mesh,
        in_specs=in_specs,
        out_specs=out_specs,
        check_vma=False,
    )
```

```python
import functools

import jax
import jax.numpy as jnp
import numpy as np
from jax import lax
from jax.experimental import pallas as pl
from jax.experimental.pallas import tpu as pltpu
from jax.sharding import PartitionSpec as P

EPS = 1e-06
C = 96
Z = 16
T = 4
TH = 32
TW = 52
TOP_TILES = 30
BOTTOM_TILES = 20
OWN = 39
EXT = 42
FS = 48
KK = 27
QB = 8
F32 = jnp.float32
BF16 = jnp.bfloat16


def lanes(tile, count=1):
    return pl.ds(pl.multiple_of(tile * 128, 128), count * 128)


def kernel(
    n_ha,
    n_wa,
    frames,
    cache,
    owners_in,
    valid,
    norm_gain_in,
    conv_weight,
    conv_bias_in,
    down_weight,
    down_bias_in,
    latent_weight_in,
    latent_bias_in,
    out,
    owners,
    norm_gain,
    conv_bias,
    down_bias,
    latent_weight,
    latent_bias,
    selector,
    ext,
    pack_top,
    pack_bot,
    corner_top,
    corner_bot,
    above,
    above_side,
    below,
    below_side,
    act,
    xf,
    inner,
    outer,
    ones,
    squares,
    sums,
    prod,
    hb,
    l32,
    x32,
    hp32,
    h32,
    vs,
    conv_taps,
    down_taps,
    taps,
    wa_w,
    wb_w,
    down_w,
    gain,
    cbias,
    lbias,
    send,
    local_sem,
    send_sem,
    recv_sem,
    a2a_send,
    a2a_recv,
):
    ha, wa = lax.axis_index("ha"), lax.axis_index("wa")
    up, down = lax.rem(ha + n_ha - 1, n_ha), lax.rem(ha + 1, n_ha)
    left, right = lax.rem(wa + n_wa - 1, n_wa), lax.rem(wa + 1, n_wa)

    own = pl.ds(0, OWN * 128)
    loads = [
        pltpu.make_async_copy(frames.at[0, t], ext.at[2 + t, :, own], local_sem.at[t])
        for t in range(T)
    ]
    loads += [
        pltpu.make_async_copy(cache.at[0, t], ext.at[t, :, own], local_sem.at[T + t])
        for t in range(2)
    ]
    small = [
        pltpu.make_async_copy(source, target, local_sem.at[8 + n])
        for n, (source, target) in enumerate(
            (
                (owners_in, owners),
                (norm_gain_in, norm_gain),
                (conv_bias_in, conv_bias),
                (down_bias_in, down_bias),
                (latent_weight_in, latent_weight),
                (latent_bias_in, latent_bias),
            )
        )
    ]
    load_conv = pltpu.make_async_copy(conv_weight, conv_taps, local_sem.at[6])
    load_down = pltpu.make_async_copy(down_weight, down_taps, local_sem.at[7])
    for load in loads + small + [load_conv, load_down]:
        load.start()

    barrier = pltpu.get_barrier_semaphore()
    greeted = [
        {"ha": up, "wa": wa},
        {"ha": down, "wa": wa},
        {"ha": ha, "wa": left},
        {"ha": ha, "wa": right},
        {"ha": up, "wa": left},
        {"ha": up, "wa": right},
        {"ha": down, "wa": left},
        {"ha": down, "wa": right},
        {"ha": lax.rem(ha + 2, n_ha), "wa": wa},
    ]
    for device in greeted:
        pl.semaphore_signal(
            barrier, inc=1, device_id=device, device_id_type=pl.DeviceIdType.MESH
        )

    def remote(src, dst, index, device):
        return pltpu.make_async_remote_copy(
            src_ref=src,
            dst_ref=dst,
            send_sem=send_sem.at[index],
            recv_sem=recv_sem.at[index],
            device_id=device,
            device_id_type=pl.DeviceIdType.MESH,
        )

    first, last = pl.ds(0, 256), pl.ds((OWN - 1) * 128, 128)
    from_right, from_left = pl.ds(OWN * 128, 256), pl.ds((OWN + 2) * 128, 128)
    col_copies = [
        remote(
            frames.at[0, :, :, first],
            ext.at[pl.ds(2, T), :, from_right],
            6,
            {"ha": ha, "wa": left},
        ),
        remote(
            cache.at[0, :, :, first],
            ext.at[pl.ds(0, 2), :, from_right],
            7,
            {"ha": ha, "wa": left},
        ),
        remote(
            frames.at[0, :, :, last],
            ext.at[pl.ds(2, T), :, from_left],
            8,
            {"ha": ha, "wa": right},
        ),
        remote(
            cache.at[0, :, :, last],
            ext.at[pl.ds(0, 2), :, from_left],
            9,
            {"ha": ha, "wa": right},
        ),
    ]
    pl.semaphore_wait(barrier, len(greeted))
    for copy in col_copies:
        copy.start()
    lane = lax.broadcasted_iota(jnp.int32, (1, 128), 1)

    def column_of(axis):
        index = lax.broadcasted_iota(jnp.int32, (384, 384), axis)
        return sum((index >= edge).astype(jnp.int32) for edge in (96, 192, 288))

    ones[...] = jnp.where(column_of(0) == column_of(1), 1.0, 0.0).astype(BF16)

    for load in small:
        load.wait()
    by_column = (((1,), (1,)), ((), ()))
    by_z = jnp.concatenate([latent_weight[...]] * QB, axis=0)
    rest = down_bias[...]
    pieces = []
    for _ in range(3):
        piece = rest.astype(BF16)
        pieces.append(piece.astype(F32))
        rest = rest - pieces[-1]
    pieces = jnp.concatenate(pieces + [jnp.zeros((13, C), F32)], axis=0).astype(BF16)
    lbias_row = jnp.sum(
        lax.dot_general(pieces, by_z, by_column, preferred_element_type=F32),
        axis=0,
        keepdims=True,
    ) + jnp.concatenate([latent_bias[...]] * QB, axis=1)

    lbias[...] = lbias_row
    bias = conv_bias[...]
    bias = jnp.concatenate([bias[:, 64:]] + [bias] * 3 + [bias[:, :64]], axis=1)
    for j in range(3):
        cbias[j] = bias[:, 128 * j : 128 * (j + 1)]

    gain[...] = jnp.concatenate([norm_gain[...]] * 4, axis=1) * (0.5 * C**0.5)
    row = lax.broadcasted_iota(jnp.int32, (64, 64), 0)
    col = lax.broadcasted_iota(jnp.int32, (64, 64), 1)
    by_col = jnp.broadcast_to(owners[...], (64, 64))
    by_row = jnp.sum(jnp.where(row == col, by_col, 0), axis=1, keepdims=True)
    rank = jnp.sum(jnp.where((by_row == by_col) & (row < col), 1, 0), axis=0, keepdims=True)
    slot = owners[...] * 32 + rank
    slots = lax.broadcasted_iota(jnp.int32, (128, 64), 0)
    selector[...] = jnp.where(slots == slot, 1.0, 0.0).astype(BF16)


    for load in loads:
        load.wait()

    sub = lax.broadcasted_iota(jnp.int32, (8, 128), 0)

    def top_rows(tile):
        tops = [ext[f, pl.ds(0, 16), pl.ds(tile * 128, 128)].astype(F32)[:8] for f in range(6)]
        lo = jnp.zeros((8, 128), F32)
        hi = jnp.zeros((8, 128), F32)
        for t in range(T):
            lo = jnp.where(sub == t, tops[2 + t][0:1], lo)
            lo = jnp.where(sub == 4 + t, tops[2 + t][1:2], lo)
        for t in range(2):
            hi = jnp.where(sub == t, tops[t][0:1], hi)
            hi = jnp.where(sub == 2 + t, tops[t][1:2], hi)
        return lo, hi

    def bottom_rows(tile):
        bots = [ext[f, pl.ds(16, 16), pl.ds(tile * 128, 128)].astype(F32)[8:] for f in range(6)]
        lo = jnp.zeros((8, 128), F32)
        for t in range(T):
            lo = jnp.where(sub == t, bots[2 + t][7:8], lo)
        for t in range(2):
            lo = jnp.where(sub == 4 + t, bots[t][7:8], lo)
        return lo

    def put_pack(target, tile, lo, hi):
        target[:, pl.ds(tile * 128, 128)] = jnp.concatenate([lo, hi], axis=0).astype(BF16)

    above_us, below_us = {"ha": up, "wa": wa}, {"ha": down, "wa": wa}
    half = TOP_TILES // 2 * 128
    row_copies = []

    def send_rows(copy):
        copy.start()
        row_copies.append(copy)

    spread = TOP_TILES // 3
    for tile in range(TOP_TILES):
        lo, hi = top_rows(tile) if tile < TOP_TILES - 1 else (jnp.zeros((8, 128), F32),) * 2
        far_lo, far_hi = top_rows(TOP_TILES - 1 + tile % spread)
        far = (pltpu.roll(far_lo, 4, 0), far_lo, pltpu.roll(far_hi, 4, 0))[tile // spread]
        put_pack(pack_top, tile, lo, jnp.where(sub < 4, hi, far))
        if tile == TOP_TILES // 2 - 1:
            cut = pl.ds(0, half)
            send_rows(remote(pack_top.at[:, cut], below.at[:, cut], 0, above_us))
    cut = pl.ds(half, half)
    send_rows(remote(pack_top.at[:, cut], below.at[:, cut], 10, above_us))
    for tile in range(BOTTOM_TILES):
        far = tile + BOTTOM_TILES
        hi = bottom_rows(far) if far < OWN else jnp.zeros((8, 128), F32)
        put_pack(pack_bot, tile, bottom_rows(tile), hi)
    send_rows(remote(pack_bot, above, 1, below_us))
    for n, tile in enumerate((0, 1, OWN - 1)):
        put_pack(corner_top, n, *top_rows(tile))
        put_pack(corner_bot, n, bottom_rows(tile), jnp.zeros((8, 128), F32))
    one, two = pl.ds(0, 256), pl.ds(256, 128)
    for source, target, index, to in (
        (corner_top, below_side, 2, up),
        (corner_bot, above_side, 4, down),
    ):
        for n, (cut, side) in enumerate(((one, left), (two, right))):
            send_rows(
                remote(source.at[:, cut], target.at[:, cut], index + n, {"ha": to, "wa": side})
            )


    load_conv.wait()
    load_down.wait()

    for g in range(C // 4):
        win = lanes(3 * g, 3)
        for weight, count, at in ((conv_taps, 27, 0), (down_taps, 9, 27)):
            x = weight[:, win].astype(F32)
            t0, t1, t2 = (x[:, 128 * j : 128 * (j + 1)] for j in range(3))
            parts = [
                t0,
                jnp.where(lane < 32, pltpu.roll(t0, 32, 1), pltpu.roll(t1, 32, 1)),
                jnp.where(lane < 64, pltpu.roll(t1, 64, 1), pltpu.roll(t2, 64, 1)),
                pltpu.roll(t2, 96, 1),
            ]
            for u in range(4):
                taps[pl.ds(at * C + 4 * g + u, count, C)] = jnp.where(lane < C, parts[u], 0.0)

    for a in range(3):
        for c in range(0, C, 16):
            g = [
                [taps[pl.ds((9 * a + 3 * r + s) * C + c, 16)] for s in range(3)] for r in range(3)
            ]
            for m in range(4):
                if m == 0:
                    w = g[0]
                elif m == 3:
                    w = g[2]
                else:
                    sign = 1.0 if m == 1 else -1.0
                    w = [0.5 * (g[0][s] + g[2][s] + sign * g[1][s]) for s in range(3)]
                zero = jnp.zeros((16, 128), F32)
                by96 = [zero] + [pltpu.roll(x, 96, 1) for x in w]
                by64 = [pltpu.roll(x, 64, 1) for x in w] + [zero]
                by32 = [zero] + [pltpu.roll(x, 32, 1) for x in w]
                w = list(w) + [zero]
                at = m * 1152 + a * 384
                for s in range(4):
                    rows = pl.ds(pl.multiple_of(at + s * 96 + c, 16), 16)
                    wa_w[rows, pl.ds(0, 128)] = jnp.where(lane < 96, w[s], by96[s]).astype(BF16)
                    wa_w[rows, pl.ds(128, 128)] = jnp.where(lane < 64, by96[s], 0.0).astype(BF16)
                    rows = pl.ds(pl.multiple_of(at + (s * 96 + c + 64) % 384, 16), 16)
                    wb_w[rows, pl.ds(0, 128)] = jnp.where(lane < 64, 0.0, by64[s]).astype(BF16)
                    wb_w[rows, pl.ds(128, 128)] = jnp.where(lane < 32, by64[s], by32[s]).astype(BF16)

    fused = lax.dot_general(
        taps[pl.ds(27 * C, 9 * C)][:, :C].astype(BF16),
        by_z,
        by_column,
        preferred_element_type=F32,
    )
    down_w[...] = jnp.zeros((1024, 128), BF16)
    for r in range(3):
        first = (0, 0, 2)[r]
        for col in range(5):
            block = jnp.zeros((C, 128), F32)
            for s in range(3):
                q = col - s
                if q in (0, 2):
                    tap = fused[(3 * r + s) * C : (3 * r + s + 1) * C]
                    place = first + q // 2
                    block = jnp.where((lane >= 16 * place) & (lane < 16 * (place + 1)), tap, block)
            rows = pl.ds((512 if r == 1 else 0) + 32 + C * col, C)
            if r == 2:
                block = block + down_w[rows].astype(F32)
            down_w[rows] = block.astype(BF16)

    has_left = jnp.where(wa == 0, 0.0, 1.0).astype(F32)
    has_right = jnp.where(wa == n_wa - 1, 0.0, 1.0).astype(F32)
    has_above = jnp.where(ha == 0, 0.0, 1.0).astype(F32)
    has_below = jnp.where(ha == n_ha - 1, 0.0, 1.0).astype(F32)

    def activate(x):
        squares = jnp.dot((x * x).astype(BF16), ones[...], preferred_element_type=F32)
        u = x * lax.rsqrt(squares + C * EPS) * gain[...]
        return u + u * jnp.tanh(u)

    def piece(g, f, j, edge):
        x = ext[f, :, lanes(3 * g + j)].astype(F32)
        if edge and g == 13:
            x = x * (has_right if j < 2 else has_left)
        return x

    def groups(gs, edge):
        for g in gs:
            for f in range(T):
                for j in range(3):
                    x = piece(g, 2 + f, j, edge)
                    squares[g, pl.ds(f * TH, TH), pl.ds(128 * j, 128)] = (x * x).astype(BF16)
        sums[pl.ds(gs[0], len(gs))] = jnp.dot(
            squares[pl.ds(gs[0], len(gs))].reshape(len(gs) * T * TH, 384),
            ones[...],
            preferred_element_type=F32,
        ).reshape(len(gs), T * TH, 384)
        for g in gs:
            for f in range(6):
                rows = pl.ds((f - 2) * TH, TH)
                if f >= 2:
                    before = pltpu.roll(piece(max(g - 1, 0), f, 2, edge), 32, 1)
                for j in range(3):
                    tile = 3 * g + j
                    x = piece(g, f, j, edge)
                    if f >= 2:
                        if tile < 40:
                            here = pltpu.roll(x, 32, 1)
                            xf[tile + 1, rows] = jnp.where(lane < 32, before, here)
                            before = here
                        total = sums[g, rows, pl.ds(128 * j, 128)]
                        u = x * lax.rsqrt(total + C * EPS) * gain[:, 128 * j : 128 * (j + 1)]
                        x = u + u * jnp.tanh(u)
                    act[tile, pl.ds(f * FS + 8, TH)] = x
                    d1 = act[tile, pl.ds(f * FS + 8, 16, 2)]
                    d2 = act[tile, pl.ds(f * FS + 9, 16, 2)]
                    inner[0, tile + 1, pl.ds(f * 16, 16)] = (d1 + d2).astype(BF16)
                    inner[1, tile + 1, pl.ds(f * 16, 16)] = (d2 - d1).astype(BF16)

    def tile_a(k, j):
        return 3 * k + j + 1

    def tile_b(i, j):
        return EXT + 1 + i if j == 0 else 3 * i + j - 1

    def join(planes):
        for m in range(2):
            planes[m, 0] = planes[m, EXT]
            for i in range(14):
                later = planes[m, 3 * i + 2]
                sooner = planes[m, 41 if i == 0 else 3 * i - 1]
                planes[m, EXT + 1 + i] = jnp.where(lane < 64, later, sooner)

    def product(planes, m, at, base, tile_of, weights):
        rows = []
        for w in range(7):
            pieces = [
                planes[m, tile_of(base + w, j), pl.ds(a * 16, 64)]
                for a in range(3)
                for j in range(3)
            ]
            rows.append(jnp.concatenate(pieces, axis=1))
        return jnp.dot(
            jnp.concatenate(rows, axis=0),
            weights[pl.ds(at * 1152, 1152)],
            preferred_element_type=F32,
        )

    def inner_products(side, step):
        tile_of, weights = ((tile_a, wa_w), (tile_b, wb_w))[side]
        for m in range(2):
            prod[side, 1 + m, pl.ds(448 * step, 448)] = product(
                inner, m, 1 + m, (6 + side) * step, tile_of, weights
            )

    for n in range(3):
        groups([3 * n, 3 * n + 1, 3 * n + 2], False)
    inner_products(0, 0)
    groups([9, 10, 11, 12], False)
    inner_products(0, 1)

    for copy in col_copies:
        copy.wait_recv()
    groups([13], True)
    join(inner)
    for copy in row_copies:
        copy.wait_recv()

    def halo_rows(tile):
        if tile >= OWN:
            cut = pl.ds((tile - OWN) * 128, 128)
            hi, lo = below_side[:, cut].astype(F32), above_side[:, cut].astype(F32)[:8]
            mask = has_right if tile < OWN + 2 else has_left
            return hi * (has_below * mask), lo * (has_above * mask)
        if tile < TOP_TILES - 1:
            hi = below[:, pl.ds(tile * 128, 128)].astype(F32)
        else:
            far = [
                below[:, pl.ds((spread * n + tile - TOP_TILES + 1) * 128, 128)].astype(F32)[8:]
                for n in range(3)
            ]
            hi = jnp.concatenate(
                [jnp.where(sub < 4, pltpu.roll(far[0], 4, 0), far[1]), pltpu.roll(far[2], 4, 0)],
                axis=0,
            )
        lo = above[:, pl.ds(tile % BOTTOM_TILES * 128, 128)].astype(F32)
        lo = lo[:8] if tile < BOTTOM_TILES else lo[8:]
        return hi * has_below, lo * has_above

    for part in range(2):
        tiles = range(21 * part, 21 * (part + 1))
        rows = [halo_rows(tile) for tile in tiles]
        stacked = [jnp.concatenate([hi[:8], lo], axis=0) for hi, lo in rows]
        activated = activate(
            jnp.concatenate(
                [jnp.concatenate(stacked[3 * n : 3 * n + 3], axis=1) for n in range(7)], axis=0
            )
        )
        before = halo_rows(max(21 * part - 1, 0))[0][:8]
        before = pltpu.roll(before, 32, 1)
        for n, tile in enumerate(tiles):
            hi, lo = rows[n]
            cut = slice(128 * (n % 3), 128 * (n % 3 + 1))
            new = activated[16 * (n // 3) : 16 * (n // 3 + 1), cut]
            act[tile, pl.ds(2 * FS + 40, T, FS)] = new[0:4]
            act[tile, pl.ds(2 * FS + 41, T, FS)] = new[4:8]
            act[tile, pl.ds(2 * FS + 7, T, FS)] = new[8:12]
            act[tile, pl.ds(40, 2, FS)] = hi[8:10]
            act[tile, pl.ds(41, 2, FS)] = hi[10:12]
            act[tile, pl.ds(7, 2, FS)] = lo[4:6]
            here = pltpu.roll(hi[:8], 32, 1)
            x32[tile + 1] = jnp.where(lane < 32, before, here)
            before = here

    def outer_planes(tile):
        for f in range(6):
            d0, d1, d2, d3 = (act[tile, pl.ds(f * FS + 7 + r, 16, 2)] for r in range(4))
            outer[0, tile + 1, pl.ds(f * 16, 16)] = (d0 - d2).astype(BF16)
            outer[1, tile + 1, pl.ds(f * 16, 16)] = (d1 - d3).astype(BF16)

        for a in range(3):
            d0, d1, d2 = (act[tile, pl.ds(a * FS + 39 + r, T, FS)] for r in range(3))
            l32[tile, a, pl.ds(0, T)] = d0 - d2
            l32[tile, 3 + a, pl.ds(0, T)] = d1 + d2
            l32[tile, 6 + a, pl.ds(0, T)] = d2 - d1

    for step in range(2):
        for n in range(21):
            outer_planes(21 * step + n)
        inner_products(1, step)

    join(outer)
    cut_right = jnp.where((lane >= 32) & (wa == n_wa - 1), 0.0, 1.0).astype(F32)

    for step in range(2):
        rows = pl.ds(448 * step, 448)
        for m in range(2):
            prod[0, 3 * m, rows] = product(outer, m, 3 * m, 6 * step, tile_a, wa_w)
            prod[1, 3 * m, rows] = product(outer, m, 3 * m, 7 * step, tile_b, wb_w)

    def epilogue(step):
        def both_rows(side, window, half, at):
            row = 64 * window + (64 if side == 0 and window > 6 else 0) + at
            cut = (pl.ds(row, 32), pl.ds(128 * half, 128))
            p0, p1, p2, p3 = (prod[(side, m) + cut] for m in range(4))
            return p0 + (p1 + p2), (p1 - p2) - p3

        def put(tile, at, values, mask=None):
            for parity in range(2):
                x = xf[tile + 1, pl.ds(2 * at + parity, 32, 2)]
                h = x + values[parity] + cbias[tile % 3]
                h = h if mask is None else h * mask
                hb[parity, tile + 1, pl.ds(at, 32)] = h.astype(BF16)

        for at in range(0, 64, 32):
            for k in range(7 * step, 7 + 6 * step):
                put(3 * k + 1, at, both_rows(0, k, 0, at))
            for i in range(7 * step, 7 * step + 7):
                if i:
                    one, two = both_rows(0, i - 1, 1, at), both_rows(1, i, 0, at)
                    put(3 * i - 1, at, (one[0] + two[0], one[1] + two[1]))
                put(3 * i, at, both_rows(1, i, 1, at), cut_right if i == 13 else None)

    for i in range(14):
        sooner = 40 if i == 0 else 3 * i - 2
        for n in range(9):
            l32[EXT + i, n] = jnp.where(lane < 64, l32[3 * i + 1, n], l32[sooner, n])

    def tile32_a(k, j):
        return 3 * k + j

    def tile32_b(i, j):
        return EXT + i if j == 0 else (41 if i == 0 and j == 1 else 3 * i + j - 2)

    def conv32(tile_of, weights):
        rows = []
        for w in range(14):
            pieces = [l32[tile_of(w, j), n] for n in range(9) for j in range(3)]
            rows.append(jnp.concatenate(pieces, axis=1))
        lhs = jnp.concatenate(rows, axis=0).astype(BF16)
        return jnp.dot(lhs, weights[pl.ds(0, KK * 128)], preferred_element_type=F32)

    acc = conv32(tile32_a, wa_w)
    for k in range(13):
        part = acc[8 * k : 8 * (k + 1)]
        h32[3 * k + 2] = (x32[3 * k + 2] + part[:, :128] + cbias[1]) * has_below
        hp32[k + 1] = part[:, 128:]
    acc = conv32(tile32_b, wb_w)
    for i in range(14):
        part = acc[8 * i : 8 * (i + 1)]
        if i:
            h = x32[3 * i] + part[:, :128] + hp32[i] + cbias[2]
            h32[3 * i] = h * has_below
        h = (x32[3 * i + 1] + part[:, 128:] + cbias[0]) * has_below
        h32[3 * i + 1] = h * cut_right if i == 13 else h

    def downsample(ks):
        rows = []
        for k in ks:
            pieces = [hb[parity, 3 * k + j + 1] for parity in range(2) for j in range(4)]
            rows.append(jnp.concatenate(pieces, axis=1))
        return jnp.dot(jnp.concatenate(rows, axis=0), down_w[...], preferred_element_type=F32)

    epilogue(0)
    main_0 = downsample(range(6))
    epilogue(1)
    main_1 = downsample(range(6, 13))
    rows = [
        jnp.concatenate([h32[3 * min(k, 12) + j + 1] for j in range(4)], axis=1) for k in range(14)
    ]
    extra = jnp.dot(
        jnp.concatenate(rows, axis=0).astype(BF16),
        down_w[pl.ds(0, 512)],
        preferred_element_type=F32,
    )
    blocks = []
    for b in range(4):
        here = jnp.zeros((64, 128), F32)
        over = jnp.zeros((64, 128), F32)
        over32 = jnp.zeros((8, 128), F32)
        for j in range(4 if b < 3 else 1):
            k = 4 * b + j
            fits = (lane >= 32 * j) & (lane < 32 * (j + 1))
            part = main_0[64 * k : 64 * (k + 1)] if k < 6 else main_1[64 * (k - 6) : 64 * (k - 5)]
            turned = pltpu.roll(part, 32 * j, 1) if j else part
            here = jnp.where(fits, turned, here)
            turned = pltpu.roll(part, (32 * j + 96) % 128, 1) if j != 1 else part
            over = jnp.where(fits, turned, over)
            part = extra[8 * k : 8 * (k + 1)]
            turned = pltpu.roll(part, (32 * j + 96) % 128, 1) if j != 1 else part
            over32 = jnp.where(fits, turned, over32)
        for t in range(T):
            vs[t, pl.ds(0, 16)] = over[16 * t : 16 * (t + 1)]
            vs[t, pl.ds(16, 1)] = over32[t : t + 1]
        shifted = jnp.concatenate([vs[t, pl.ds(1, 16)] for t in range(T)], axis=0)
        blocks.append(here + shifted + lbias[...])
    latent = jnp.concatenate(blocks[:3] + [blocks[3][:, :32]], axis=1)
    frame_of = lax.broadcasted_iota(jnp.int32, (64, 1), 0)
    latent = jnp.where(frame_of < valid[0] * 16, latent, 0.0).astype(BF16)

    send[...] = jnp.dot(selector[...], latent, preferred_element_type=F32).astype(BF16)

    here = pl.ds(pl.multiple_of(ha * 32, 32), 32)
    keep = pltpu.make_async_copy(send.at[here], out.at[0, 0, 0, here], local_sem.at[0])
    copies = []
    for d in range(1, n_ha):
        target = lax.rem(ha + d, n_ha)
        copies.append(
            pltpu.make_async_remote_copy(
                src_ref=send.at[pl.ds(pl.multiple_of(target * 32, 32), 32)],
                dst_ref=out.at[0, 0, 0, here],
                send_sem=a2a_send.at[d - 1],
                recv_sem=a2a_recv.at[d - 1],
                device_id={"ha": target, "wa": wa},
                device_id_type=pl.DeviceIdType.MESH,
            )
        )
    for copy in copies:
        copy.start()
    keep.start()
    for copy in row_copies + col_copies:
        copy.wait_send()
    for copy in copies:
        copy.wait()
    keep.wait()


def per_device(
    n_ha,
    n_wa,
    frames,
    cache,
    norm_gain,
    conv_weight,
    conv_bias,
    down_weight,
    down_bias,
    latent_weight,
    latent_bias,
    valid_frames,
    owners,
):
    hbm = pl.BlockSpec(memory_space=pltpu.HBM)
    return pl.pallas_call(
        functools.partial(kernel, n_ha, n_wa),
        out_shape=jax.ShapeDtypeStruct((1, 1, 1, 128, 416), BF16),
        in_specs=[hbm, hbm, hbm, pl.BlockSpec(memory_space=pltpu.SMEM)] + [hbm] * 7,
        out_specs=hbm,
        scratch_shapes=[
            pltpu.VMEM((1, 64), jnp.int32),
            pltpu.VMEM((1, C), F32),
            pltpu.VMEM((1, C), F32),
            pltpu.VMEM((1, C), F32),
            pltpu.VMEM((Z, C), BF16),
            pltpu.VMEM((1, Z), F32),
            pltpu.VMEM((128, 64), BF16),
            pltpu.VMEM((6, TH, EXT * 128), BF16),
            pltpu.VMEM((16, TOP_TILES * 128), BF16),
            pltpu.VMEM((16, BOTTOM_TILES * 128), BF16),
            pltpu.VMEM((16, 384), BF16),
            pltpu.VMEM((16, 384), BF16),
            pltpu.VMEM((16, BOTTOM_TILES * 128), BF16),
            pltpu.VMEM((16, 384), BF16),
            pltpu.VMEM((16, TOP_TILES * 128), BF16),
            pltpu.VMEM((16, 384), BF16),
            pltpu.VMEM((EXT, 6 * FS, 128), F32),
            pltpu.VMEM((41, T * TH, 128), F32),
            pltpu.VMEM((2, EXT + 15, 96, 128), BF16),
            pltpu.VMEM((2, EXT + 15, 96, 128), BF16),
            pltpu.VMEM((384, 384), BF16),
            pltpu.VMEM((14, T * TH, 384), BF16),
            pltpu.VMEM((14, T * TH, 384), F32),
            pltpu.VMEM((2, 4, 896, 256), F32),
            pltpu.VMEM((2, 41, 64, 128), BF16),
            pltpu.VMEM((EXT + 14, 9, 8, 128), F32),
            pltpu.VMEM((EXT + 1, 8, 128), F32),
            pltpu.VMEM((14, 8, 128), F32),
            pltpu.VMEM((41, 8, 128), F32),
            pltpu.VMEM((T, 24, 128), F32),
            pltpu.VMEM((27, C * C), BF16),
            pltpu.VMEM((9, C * C), BF16),
            pltpu.VMEM((36 * C, 128), F32),
            pltpu.VMEM((4608, 256), BF16),
            pltpu.VMEM((4608, 256), BF16),
            pltpu.VMEM((1024, 128), BF16),
            pltpu.VMEM((1, 384), F32),
            pltpu.VMEM((3, 1, 128), F32),
            pltpu.VMEM((1, 128), F32),
            pltpu.VMEM((128, 416), BF16),
            pltpu.SemaphoreType.DMA((14,)),
            pltpu.SemaphoreType.DMA((11,)),
            pltpu.SemaphoreType.DMA((11,)),
            pltpu.SemaphoreType.DMA((n_ha - 1,)),
            pltpu.SemaphoreType.DMA((n_ha - 1,)),
        ],
        compiler_params=pltpu.CompilerParams(
            collective_id=0, has_side_effects=True, vmem_limit_bytes=56 * 2**20
        ),
        name="encoder_step",
    )(
        frames,
        cache,
        owners.reshape(1, 64),
        valid_frames,
        norm_gain.reshape(1, C),
        conv_weight,
        conv_bias.reshape(1, C),
        down_weight,
        down_bias.reshape(1, C),
        latent_weight.T,
        latent_bias.reshape(1, Z),
    )


def solution(mesh):
    in_specs = (
        P("ba", None, "ha", "wa"),
        P("ba", None, "ha", "wa"),
        P(),
        P(),
        P(),
        P(),
        P(),
        P(),
        P(),
        P("ba"),
        P("ba", "ha", "wa", None, None),
    )
    out_specs = P("ba", "ha", "wa", None, None)
    return jax.shard_map(
        functools.partial(per_device, mesh.shape["ha"], mesh.shape["wa"]),
        mesh=mesh,
        in_specs=in_specs,
        out_specs=out_specs,
        check_vma=False,
    )
```
